32 devices in a mesh: grp: 2 (over core), fsdp: 16 (over z, y, x).
Axes of the slice: x: 2, y: 2, z: 4, core: 2. Of those that a mesh axis runs over, the one named last changes fastest.
Arguments:
- tokens: bfloat16 [32768, 1024], P(('grp', 'fsdp')), may hold values from -6 to 6
- cotangent: bfloat16 [32768, 1024], P(('grp', 'fsdp')), may hold values from -6 to 6
- segment_ids: int32 [32768], P(('grp', 'fsdp')), may hold values from 0 to 127, as said below
- group_counts: int32 [2], replicated, may hold values from 1000 to 4999
- qkv_weight: float32 [1024, 3072], P('fsdp'), may hold values from -0.1875 to 0.1875
- out_weight: float32 [1024, 1024], P('fsdp'), may hold values from -0.75 to 0.75
- up_weight: float32 [1024, 4096], P('fsdp'), may hold values from -0.1875 to 0.1875
- down_weight: float32 [4096, 1024], P('fsdp'), may hold values from -0.09375 to 0.09375
- small_params: float32 [12288], P('fsdp')
- qkv_first: float32 [1024, 3072], P('fsdp'), may hold values from -0.00048828125 to 0.00048828125
- out_first: float32 [1024, 1024], P('fsdp'), may hold values from -0.00048828125 to 0.00048828125
- up_first: float32 [1024, 4096], P('fsdp'), may hold values from -0.00048828125 to 0.00048828125
- down_first: float32 [4096, 1024], P('fsdp'), may hold values from -0.00048828125 to 0.00048828125
- small_first: float32 [12288], P('fsdp'), may hold values from -0.00048828125 to 0.00048828125
- qkv_second: float32 [1024, 3072], P('fsdp'), may hold values from 7.947286e-11 to 3.1789144e-10
- out_second: float32 [1024, 1024], P('fsdp'), may hold values from 7.947286e-11 to 3.1789144e-10
- up_second: float32 [1024, 4096], P('fsdp'), may hold values from 7.947286e-11 to 3.1789144e-10
- down_second: float32 [4096, 1024], P('fsdp'), may hold values from 7.947286e-11 to 3.1789144e-10
- small_second: float32 [12288], P('fsdp'), may hold values from 7.947286e-11 to 3.1789144e-10
Outputs:
- block_output: bfloat16 [32768, 1024], P(('grp', 'fsdp'))
- tokens_grad: bfloat16 [32768, 1024], P(('grp', 'fsdp'))
- new_qkv_weight: float32 [1024, 3072], P('fsdp')
- new_out_weight: float32 [1024, 1024], P('fsdp')
- new_up_weight: float32 [1024, 4096], P('fsdp')
- new_down_weight: float32 [4096, 1024], P('fsdp')
- new_small_params: float32 [12288], P('fsdp')
- new_qkv_first: float32 [1024, 3072], P('fsdp')
- new_out_first: float32 [1024, 1024], P('fsdp')
- new_up_first: float32 [1024, 4096], P('fsdp')
- new_down_first: float32 [4096, 1024], P('fsdp')
- new_small_first: float32 [12288], P('fsdp')
- new_qkv_second: float32 [1024, 3072], P('fsdp')
- new_out_second: float32 [1024, 1024], P('fsdp')
- new_up_second: float32 [1024, 4096], P('fsdp')
- new_down_second: float32 [4096, 1024], P('fsdp')
- new_small_second: float32 [12288], P('fsdp')
- grad_norm_sq: float32 [], replicated
The draws below stay inside these ranges and needn't reach their ends.
Inputs may be any that keep to these rules, and one draw needn't show every extreme that they name: `segment_ids`: within each device's 1024 tokens the numbers start at 0, never fall, and equal numbers form one crop. On devices of the global group crops hold 40 to 50 tokens and the first holds 50; on the local group 8 to 10 and the first 10; a device's last crop may be cut short. The first device of the local group has crops of 8 tokens after its first.
All inputs are finite; a program needn't handle non-finite values.
Results may differ from the reference program's by a relative error of at most 0.017.
Values may be sent and summed in bfloat16 or wider, within the bound.
No kernel may reach another device: no remote copies, remote signals or barrier semaphores. Data moves between devices by JAX's collectives and lax.ppermute only.
A program may use at most 256 MiB of HBM per device.

```python
import math
import jax
import jax.numpy as jnp
from jax import lax

D = 1024
FF = 4096
HD = 64
TOK_DEV = 1024
STEP = 10
HEADS = 16
TOKENS = 32768
SMALL = 12288
PARAMS = 12582912
N_GRP = 2
N_FSDP = 16


def draw_segment_ids(key, part):
    key = jax.random.fold_in(key, 7)
    devices = N_GRP * N_FSDP
    count = TOK_DEV // 8 + 1
    device = jnp.arange(devices)
    most = jnp.where(device // N_FSDP >= N_GRP // 2, 10, 50)[:, None]
    least = most - most // 5
    raw = jax.random.randint(key, (devices, count), 0, 1 << 20)
    lengths = raw % (most - least + 1) + least
    first_local = N_GRP // 2 * N_FSDP
    lengths = jnp.where((device == first_local)[:, None], least, lengths)
    lengths = jnp.concatenate([most, lengths[:, 1:]], axis=1)
    ends = jnp.cumsum(lengths, axis=1)
    place = jnp.arange(TOK_DEV)
    ids = jnp.sum((ends[:, None, :] <= place[None, :, None]).astype(jnp.int32), axis=-1)
    return ids.reshape(-1).astype(jnp.int32)


def draw_small_params(key, part):
    key = jax.random.fold_in(key, 11)
    first_key, second_key = jax.random.split(key)
    place = jnp.arange(SMALL)
    within = (place % D).astype(jnp.float32) / D
    rising = 0.6 + 1.2 * within
    noise = 0.1 * jax.random.normal(first_key, (SMALL,), jnp.float32)
    spread = 0.1 * jax.random.normal(second_key, (SMALL,), jnp.float32)
    is_gain = (place < D) | (place >= 5 * D) & (place < 6 * D)
    return jnp.where(is_gain, rising * (1.0 + noise), spread).astype(jnp.float32)


def levels(key, shape, cuts, low, largest):
    level, own = 1.0, jax.random.fold_in(key, 6)
    for dim, blocks in cuts:
        heights = jnp.exp(jax.random.uniform(jax.random.fold_in(own, dim), (blocks,), jnp.float32, low / len(cuts), largest / len(cuts)))
        level = level * jnp.repeat(heights, shape[dim] // blocks).reshape([-1 if axis == dim else 1 for axis in range(len(shape))])
    return level


def gaussian(rng, dims, scale, most, cuts=(), kind=jnp.bfloat16):
    values = scale * jax.random.normal(rng, dims, jnp.float32)
    if cuts:
        values = values * levels(rng, dims, cuts, -0.22, 0.18)
    return jnp.clip(values, -most, most).astype(kind)


def setup_inputs(seed: int = 0) -> dict:
    key_of = jax.random.split(jax.random.key(seed), 20)
    return {
        "tokens": gaussian(key_of[0], (TOKENS, D), 1.0, 6.0, ((0, 32),)),
        "cotangent": gaussian(key_of[1], (TOKENS, D), 1.0, 6.0, ((0, 32),)),
        "segment_ids": draw_segment_ids(jax.random.fold_in(key_of[19], 71), 0),
        "group_counts": jax.random.randint(key_of[3], (2,), 1000, 5000).astype(jnp.int32),
        "qkv_weight": gaussian(key_of[4], (D, 3 * D), D ** -0.5, 0.1875, ((0, 16),), jnp.float32),
        "out_weight": gaussian(key_of[5], (D, D), (D // 16) ** -0.5, 0.75, ((0, 16),), jnp.float32),
        "up_weight": gaussian(key_of[6], (D, FF), D ** -0.5, 0.1875, ((0, 16),), jnp.float32),
        "down_weight": gaussian(key_of[7], (FF, D), FF ** -0.5, 0.09375, ((0, 16),), jnp.float32),
        "small_params": draw_small_params(jax.random.fold_in(key_of[19], 71), 0),
        "qkv_first": gaussian(key_of[9], (D, 3 * D), (0.11 * PARAMS ** -0.5), 0.00048828125, ((0, 16),), jnp.float32),
        "out_first": gaussian(key_of[10], (D, D), (0.11 * PARAMS ** -0.5), 0.00048828125, ((0, 16),), jnp.float32),
        "up_first": gaussian(key_of[11], (D, FF), (0.11 * PARAMS ** -0.5), 0.00048828125, ((0, 16),), jnp.float32),
        "down_first": gaussian(key_of[12], (FF, D), (0.11 * PARAMS ** -0.5), 0.00048828125, ((0, 16),), jnp.float32),
        "small_first": gaussian(key_of[13], (SMALL,), (0.11 * PARAMS ** -0.5), 0.00048828125, ((0, 16),), jnp.float32),
        "qkv_second": jnp.clip(jnp.exp(math.log(3.178914353973994e-10) - 1.3862944 * jax.random.uniform(key_of[14], (D, 3 * D), jnp.float32) ** levels(key_of[14], (D, 3 * D), ((0, 16),), -0.2, 0.2)), 7.947285884934985e-11, 3.178914353973994e-10),
        "out_second": jnp.clip(jnp.exp(math.log(3.178914353973994e-10) - 1.3862944 * jax.random.uniform(key_of[15], (D, D), jnp.float32) ** levels(key_of[15], (D, D), ((0, 16),), -0.2, 0.2)), 7.947285884934985e-11, 3.178914353973994e-10),
        "up_second": jnp.clip(jnp.exp(math.log(3.178914353973994e-10) - 1.3862944 * jax.random.uniform(key_of[16], (D, FF), jnp.float32) ** levels(key_of[16], (D, FF), ((0, 16),), -0.2, 0.2)), 7.947285884934985e-11, 3.178914353973994e-10),
        "down_second": jnp.clip(jnp.exp(math.log(3.178914353973994e-10) - 1.3862944 * jax.random.uniform(key_of[17], (FF, D), jnp.float32) ** levels(key_of[17], (FF, D), ((0, 16),), -0.2, 0.2)), 7.947285884934985e-11, 3.178914353973994e-10),
        "small_second": jnp.clip(jnp.exp(math.log(3.178914353973994e-10) - 1.3862944 * jax.random.uniform(key_of[18], (SMALL,), jnp.float32) ** levels(key_of[18], (SMALL,), ((0, 16),), -0.2, 0.2)), 7.947285884934985e-11, 3.178914353973994e-10),
    }


@jax.custom_vjp
def low(v):
    return lax.optimization_barrier(v.astype(jnp.bfloat16)).astype(jnp.float32)

@jax.custom_vjp
def low_back(v):
    return v

def low_keep(v):
    return (low(v), None)

def low_pass(kept, grad):
    return (grad,)

def back_keep(v):
    return (v, None)

def back_low(kept, grad):
    return (low(grad),)
low.defvjp(low_keep, low_pass)
low_back.defvjp(back_keep, back_low)
HIGH = lax.Precision.HIGHEST
EPS_NORM = 1e-06
CLIP = 1.0
RATE = 0.04
RATE_SMALL = 0.25
DECAY = 0.05
BETA_ONE = 0.9
BETA_TWO = 0.999
EPS_ADAM = 1e-08

def layer_norm(x, gain, bias):
    mean = lax.optimization_barrier(jnp.mean(x, -1, keepdims=True))
    centred = x - mean
    var = lax.optimization_barrier(jnp.mean(centred * centred, -1, keepdims=True))
    return centred * lax.rsqrt(var + EPS_NORM) * gain + bias

def unpack(small):
    pieces = [small[i * D:(i + 1) * D] for i in range(7)]
    return pieces + [small[7 * D:7 * D + FF], small[7 * D + FF:]]

def attend(query, keys, values, seg):
    count = query.shape[0]
    qh = query.reshape(count, HEADS, HD)
    kh = keys.reshape(count, HEADS, HD)
    vh = values.reshape(count, HEADS, HD)
    scores = low_back(jnp.einsum('qhd,khd->hqk', qh, kh, precision=HIGH) * HD ** (-0.5))
    same = seg[:, None] == seg[None, :]
    scores = jnp.where(same[None], scores, -1e+30)
    top = lax.optimization_barrier(jnp.max(scores, -1, keepdims=True))
    expo = jnp.exp(scores - top)
    probs = expo / lax.optimization_barrier(jnp.sum(expo, -1, keepdims=True))
    return jnp.einsum('hqk,khd->qhd', low(probs), vh, precision=HIGH).reshape(count, D)

def layer(params, x, seg):
    qkv_w, out_w, up_w, down_w, small = params
    gain_one, bias_one, bias_query, bias_value, bias_out, gain_two, bias_two, bias_up, bias_down = unpack(low(small))
    normed_one = low(layer_norm(x, gain_one, bias_one))
    qkv_bias = jnp.concatenate([bias_query, jnp.zeros_like(bias_query), bias_value])
    project = low(low_back(jnp.dot(normed_one, low(qkv_w), precision=HIGH) + qkv_bias))
    att = low(low_back(attend(project[:, :D], project[:, D:2 * D], project[:, 2 * D:], seg)))
    middle = x + low_back(jnp.dot(att, low(out_w), precision=HIGH) + bias_out)
    normed_two = low(layer_norm(middle, gain_two, bias_two))
    pre_act = low_back(jnp.dot(normed_two, low(up_w), precision=HIGH) + bias_up)
    act = low(jax.nn.gelu(pre_act))
    return middle + low_back(jnp.dot(act, low(down_w), precision=HIGH) + bias_down)

def adam(weight, first, second, grad, decay, rate):
    first = BETA_ONE * first + (1.0 - BETA_ONE) * grad
    second = BETA_TWO * second + (1.0 - BETA_TWO) * grad * grad
    step_size = first / (1.0 - BETA_ONE ** STEP) / (jnp.sqrt(second / (1.0 - BETA_TWO ** STEP)) + EPS_ADAM)
    return (weight - rate * (step_size + decay * weight), first, second)

def reference(tokens, cotangent, segment_ids, group_counts, qkv_weight, out_weight, up_weight, down_weight, small_params, qkv_first, out_first, up_first, down_first, small_first, qkv_second, out_second, up_second, down_second, small_second):
    count = N_GRP * N_FSDP
    params = (qkv_weight, out_weight, up_weight, down_weight, small_params)
    counts = group_counts.astype(jnp.float32)
    share = counts / jnp.sum(counts)
    group_of = (jnp.arange(count) // N_FSDP >= N_GRP // 2).astype(jnp.int32)
    weight_of = share[group_of]
    block_x = tokens.reshape(count, TOK_DEV, D)
    block_c = cotangent.reshape(count, TOK_DEV, D)
    block_s = segment_ids.reshape(count, TOK_DEV)

    def visit(acc, item):
        x_blk, c_blk, s_blk, w_blk = item
        out, pull = jax.vjp(lambda p, xx: layer(p, xx, s_blk), params, x_blk.astype(jnp.float32))
        grads, grad_x = pull(c_blk.astype(jnp.float32))
        acc = tuple((a + w_blk * g for a, g in zip(acc, grads)))
        return (acc, (out.astype(jnp.bfloat16), grad_x.astype(jnp.bfloat16)))
    start = tuple((jnp.zeros_like(p) for p in params))
    merged, (outs, grads_x) = lax.scan(visit, start, (block_x, block_c, block_s, weight_of))
    total_sq = sum((jnp.sum(g * g) for g in merged))
    scale = jnp.minimum(1.0, CLIP * lax.rsqrt(total_sq))
    firsts = (qkv_first, out_first, up_first, down_first, small_first)
    seconds = (qkv_second, out_second, up_second, down_second, small_second)
    decays = (DECAY, DECAY, DECAY, DECAY, 0.0)
    rates = (RATE, RATE, RATE, RATE, RATE_SMALL)
    results = [adam(p, m, v, g * scale, dc, rt) for p, m, v, g, dc, rt in zip(params, firsts, seconds, merged, decays, rates)]
    return (outs.reshape(TOKENS, D), grads_x.reshape(TOKENS, D), results[0][0], results[1][0], results[2][0], results[3][0], results[4][0], results[0][1], results[1][1], results[2][1], results[3][1], results[4][1], results[0][2], results[1][2], results[2][2], results[3][2], results[4][2], total_sq)
```

```python
import math

import jax
import jax.numpy as jnp
from jax import lax
from jax.experimental import pallas as pl
from jax.experimental.pallas import tpu as pltpu
from jax.sharding import PartitionSpec as P

HD = 64
STEP = 10
EPS_NORM = 1e-06
CLIP = 1.0
RATE = 0.04
RATE_SMALL = 0.25
DECAY = 0.05
BETA_ONE = 0.9
BETA_TWO = 0.999
EPS_ADAM = 1e-08
F32 = jnp.float32
BF = jnp.bfloat16
BOTH = ("grp", "fsdp")
SWAP = [(0, 1), (1, 0)]
ANY = pl.BlockSpec(memory_space=pl.ANY)
SMEM = pl.BlockSpec(memory_space=pltpu.SMEM)
TILE = 128
SPAN = 256


def dims(n):
    m = max(1, math.isqrt(n // 4))
    return n // (m * m), m


def build_perms(n):
    nz, m = dims(n)

    def chip(z, y, x):
        return (z % nz) * m * m + (y % m) * m + x % m

    def build(move):
        return [
            (c * n + chip(z, y, x), c * n + chip(*move(c, z, y, x)))
            for c in range(2)
            for z in range(nz)
            for y in range(m)
            for x in range(m)
        ]

    return {
        "z": [build(lambda c, z, y, x: (z + k, y, x)) for k in range(nz)],
        "a": [build(lambda c, z, y, x: (z, y, x + k) if c == 0 else (z, y + k, x)) for k in range(m)],
        "b": [build(lambda c, z, y, x: (z, y + k, x) if c == 0 else (z, y, x + k)) for k in range(m)],
        "x": [build(lambda c, z, y, x: (z, y, x + k)) for k in range(m)],
        "y": [build(lambda c, z, y, x: (z, y + k, x)) for k in range(m)],
    }


def send(value, table):
    return lax.ppermute(value, BOTH, table)


def layer_norm(x, gain, bias):
    mean = jnp.mean(x, -1, keepdims=True)
    centred = x - mean
    var = jnp.mean(centred * centred, -1, keepdims=True)
    return centred * lax.rsqrt(var + EPS_NORM) * gain + bias


def unpack(small, width, hidden):
    pieces = [small[i * width : (i + 1) * width] for i in range(7)]
    return pieces + [small[7 * width : 7 * width + hidden], small[7 * width + hidden :]]


def adam(weight, first, second, grad, decay, rate):
    first = BETA_ONE * first + (1.0 - BETA_ONE) * grad
    second = BETA_TWO * second + (1.0 - BETA_TWO) * grad * grad
    step_size = (
        first / (1.0 - BETA_ONE**STEP) / (jnp.sqrt(second / (1.0 - BETA_TWO**STEP)) + EPS_ADAM)
    )
    return (weight - rate * (step_size + decay * weight), first, second)


def after(value, *deps):
    return lax.optimization_barrier((value, *deps))[0]


def gather_pieces(own, perms, nz, m):
    first = jnp.stack([own] + [send(own, perms["z"][k]) for k in range(1, nz)])
    second = [first] + [send(first, perms["a"][k]) for k in range(1, m)]
    mine = []
    for piece in second:
        mine += [piece] + [send(piece, perms["b"][k]) for k in range(1, m)]
    return mine, [lax.ppermute(p, "grp", SWAP) for p in mine]


def assemble(coords, mine, other, nz, m, shapes, plan, name):
    def kernel(*refs):
        coord = refs[0]
        sources = refs[1 : 1 + 2 * m * m]
        outs = refs[1 + 2 * m * m : 1 + 2 * m * m + len(shapes)]
        sem = refs[-1]
        z, y, x, c = coord[0], coord[1], coord[2], coord[3]
        for side in range(2):
            core = c if side == 0 else 1 - c
            for ia in range(m):
                for ib in range(m):
                    src = sources[side * m * m + ia * m + ib]
                    dx = jnp.where(core == 0, ia, ib)
                    dy = jnp.where(core == 0, ib, ia)
                    px = lax.rem(x - dx + m, m)
                    py = lax.rem(y - dy + m, m)
                    for dz in range(nz):
                        pz = lax.rem(z - dz + nz, nz)
                        chip = (pz * m + py) * m + px
                        for out, row, rows, col, cols, scol in plan(chip, core):
                            pltpu.make_async_copy(
                                src.at[dz, :, pl.ds(scol, cols)],
                                outs[out].at[
                                    pl.ds(pl.multiple_of(row, 16), rows),
                                    pl.ds(pl.multiple_of(col, 128), cols),
                                ],
                                sem.at[out],
                            ).start()
        for i, ref in enumerate(outs):
            pltpu.make_async_copy(ref, ref, sem.at[i]).wait()

    total = sum(2 * math.prod(s) for s in shapes)
    return pl.pallas_call(
        kernel,
        out_shape=[jax.ShapeDtypeStruct(s, BF) for s in shapes],
        in_specs=[SMEM] + [ANY] * (2 * m * m),
        out_specs=[pl.BlockSpec(memory_space=pltpu.VMEM)] * len(shapes),
        scratch_shapes=[pltpu.SemaphoreType.DMA((len(shapes),))],
        compiler_params=pltpu.CompilerParams(vmem_limit_bytes=24 << 20),
        cost_estimate=pl.CostEstimate(flops=0, bytes_accessed=2 * total, transcendentals=0),
        name=name,
    )(coords, *mine, *other)


def weight_grad(coords, scale, left, right, side, nz, m, name):
    tokens, total = left.shape
    half = right.shape[1] // 2
    n = nz * m * m
    r = total // n
    zrows = total // nz
    mt = min(256, zrows)
    nt = min(512, half)
    mc, nc = zrows // mt, half // nt

    def kernel(coord, scale_ref, x_hbm, y_hbm, *refs):
        outs = refs[:m]
        xv, yv, acc, xsem, ysem, osem = refs[m:]
        z, y, x, c = coord[0], coord[1], coord[2], coord[3]
        owner = c if side == 0 else 1 - c
        weight = scale_ref[0]

        def xcopy(dz, i):
            pz = lax.rem(z + dz, nz)
            return pltpu.make_async_copy(
                x_hbm.at[:, pl.ds(pl.multiple_of(pz * zrows + i * mt, 128), mt)],
                xv.at[dz * mc + i],
                xsem.at[dz * mc + i],
            )

        def ycopy(j):
            return pltpu.make_async_copy(
                y_hbm.at[:, pl.ds(pl.multiple_of(owner * half + j * nt, 128), nt)],
                yv.at[j],
                ysem.at[j],
            )

        xcopy(0, 0).start()
        for j in range(nc):
            ycopy(j).start()
        for dz in range(nz):
            for i in range(mc):
                if dz or i:
                    xcopy(dz, i).start()
        copies = []
        for dz in range(nz):
            for i in range(mc):
                xcopy(dz, i).wait()
                if dz == 0 and i == 0:
                    for j in range(nc):
                        ycopy(j).wait()

                def step(j, carry):
                    out = lax.dot_general(
                        xv[dz * mc + i],
                        yv[j],
                        (((0,), (0,)), ((), ())),
                        preferred_element_type=F32,
                    )
                    acc[dz, i * mt : (i + 1) * mt, pl.ds(pl.multiple_of(j * nt, 128), nt)] = (
                        out * weight
                    ).astype(BF)
                    return carry

                lax.fori_loop(0, nc, step, 0)
            for ib in range(m):
                for ia in range(m):
                    dx = jnp.where(owner == 0, ia, ib)
                    dy = jnp.where(owner == 0, ib, ia)
                    px = lax.rem(x + dx, m)
                    py = lax.rem(y + dy, m)
                    copy = pltpu.make_async_copy(
                        acc.at[dz, pl.ds(pl.multiple_of((py * m + px) * r, 16), r), :],
                        outs[ib].at[ia, dz],
                        osem.at[dz, ib * m + ia],
                    )
                    copy.start()
                    copies.append(copy)
        for copy in copies:
            copy.wait()

    return pl.pallas_call(
        kernel,
        out_shape=[jax.ShapeDtypeStruct((m, nz, r, half), BF)] * m,
        in_specs=[SMEM, SMEM, ANY, ANY],
        out_specs=[ANY] * m,
        scratch_shapes=[
            pltpu.VMEM((nz * mc, tokens, mt), BF),
            pltpu.VMEM((nc, tokens, nt), BF),
            pltpu.VMEM((nz, zrows, half), BF),
            pltpu.SemaphoreType.DMA((nz * mc,)),
            pltpu.SemaphoreType.DMA((nc,)),
            pltpu.SemaphoreType.DMA((nz, m * m)),
        ],
        compiler_params=pltpu.CompilerParams(vmem_limit_bytes=40 << 20),
        cost_estimate=pl.CostEstimate(
            flops=2 * tokens * total * half,
            bytes_accessed=2 * (tokens * total + tokens * half + total * half),
            transcendentals=0,
        ),
        name=name,
    )(coords, scale, left, right)


def reduce_pieces(mine, other, perms, nz, m):
    got = [lax.ppermute(p, "grp", SWAP) for p in other]
    sums = [None] * m
    for k in list(range(1, m)) + [0]:
        sums[k] = (mine[k].astype(F32) + got[k].astype(F32)).astype(BF)
    for axis, size, nxt in (("b", m, m), ("a", m, nz), ("z", nz, 0)):
        recv = [send(sums[k], perms[axis][k]) for k in range(1, size)]

        def total(pick):
            t = pick(sums[0]).astype(F32)
            for other_part in recv:
                t = t + pick(other_part).astype(F32)
            return t

        if not nxt:
            return total(lambda v: v)
        sums = [total(lambda v, k=k: v[k]).astype(BF) for k in range(nxt)]


def head_stack(block, low_lanes):
    zero = jnp.zeros_like(block)
    return jnp.concatenate(
        [jnp.where(low_lanes, block, zero), jnp.where(low_lanes, zero, block)], 0
    )


def tile_start(t, rows):
    return pl.multiple_of(jnp.clip(t * TILE - (SPAN - TILE) // 2, 0, rows - SPAN), 64)


def tile_mask(seg_col, seg_row, t, start):
    same = seg_col[pl.ds(start, SPAN), :] == seg_row[:, pl.ds(pl.multiple_of(t * TILE, 128), TILE)]
    return jnp.concatenate([same, same], 1)


def probabilities(keys, stack, same):
    scores = lax.dot_general(keys, stack, (((1,), (1,)), ((), ())), preferred_element_type=F32)
    scores = jnp.where(same, scores * HD**-0.5, -1e30)
    expo = jnp.exp(scores - jnp.max(scores, 0, keepdims=True))
    return expo * (1.0 / jnp.sum(expo, 0, keepdims=True))


def attention(project, seg_col, seg_row):
    rows, width = project.shape[0], project.shape[1] // 3
    pairs = width // (2 * HD)

    def kernel(col_ref, row_ref, q_ref, k_ref, v_ref, out_ref):
        t = pl.program_id(0)
        start = tile_start(t, rows)
        same = tile_mask(col_ref, row_ref, t, start)
        low = lax.broadcasted_iota(jnp.int32, (TILE, 2 * HD), 1) < HD
        for h in range(pairs):
            lanes = slice(h * 2 * HD, (h + 1) * 2 * HD)
            probs = probabilities(k_ref[pl.ds(start, SPAN), lanes], head_stack(q_ref[:, lanes], low), same)
            mixed = lax.dot_general(
                probs.astype(BF),
                v_ref[pl.ds(start, SPAN), lanes],
                (((0,), (0,)), ((), ())),
                preferred_element_type=F32,
            )
            out_ref[:, lanes] = jnp.where(low, mixed[:TILE], mixed[TILE:]).astype(BF)

    return pl.pallas_call(
        kernel,
        grid=(rows // TILE,),
        out_shape=jax.ShapeDtypeStruct((rows, width), BF),
        in_specs=[
            pl.BlockSpec((rows, 1), lambda t: (0, 0)),
            pl.BlockSpec((1, rows), lambda t: (0, 0)),
            pl.BlockSpec((TILE, width), lambda t: (t, 0)),
            pl.BlockSpec((rows, width), lambda t: (0, 1)),
            pl.BlockSpec((rows, width), lambda t: (0, 2)),
        ],
        out_specs=pl.BlockSpec((TILE, width), lambda t: (t, 0)),
        compiler_params=pltpu.CompilerParams(vmem_limit_bytes=32 << 20),
        cost_estimate=pl.CostEstimate(
            flops=8 * 10**9, bytes_accessed=8 * rows * width, transcendentals=rows * SPAN * 2 * pairs
        ),
        name="attention",
    )(seg_col, seg_row, project, project, project)


def attention_back(project, grad, seg_col, seg_row):
    rows, width = project.shape[0], project.shape[1] // 3
    pairs = width // (2 * HD)
    tiles = rows // TILE

    def kernel(col_ref, row_ref, q_ref, k_ref, v_ref, g_ref, out_ref, dk, dv):
        t = pl.program_id(0)

        @pl.when(t == 0)
        def _():
            dk[...] = jnp.zeros_like(dk)
            dv[...] = jnp.zeros_like(dv)

        start = tile_start(t, rows)
        window = pl.ds(start, SPAN)
        same = tile_mask(col_ref, row_ref, t, start)
        low = lax.broadcasted_iota(jnp.int32, (TILE, 2 * HD), 1) < HD
        scale = HD**-0.5
        for h in range(pairs):
            lanes = slice(h * 2 * HD, (h + 1) * 2 * HD)
            keys, values = k_ref[window, lanes], v_ref[window, lanes]
            queries = head_stack(q_ref[:, lanes], low)
            grads = head_stack(g_ref[:, lanes], low)
            probs = probabilities(keys, queries, same)
            grad_probs = lax.dot_general(
                values, grads, (((1,), (1,)), ((), ())), preferred_element_type=F32
            )
            inner = jnp.sum(probs * grad_probs, 0, keepdims=True)
            grad_scores = (probs * (grad_probs - inner)).astype(BF)
            dv[window, lanes] += jnp.dot(probs.astype(BF), grads, preferred_element_type=F32)
            dk[window, lanes] += jnp.dot(grad_scores, queries, preferred_element_type=F32)
            dq = lax.dot_general(
                grad_scores, keys, (((0,), (0,)), ((), ())), preferred_element_type=F32
            )
            out_ref[pl.ds(pl.multiple_of(t * TILE, TILE), TILE), lanes] = (
                jnp.where(low, dq[:TILE], dq[TILE:]) * scale
            ).astype(BF)

        @pl.when(t == tiles - 1)
        def _():
            out_ref[:, width : 2 * width] = (dk[...] * scale).astype(BF)
            out_ref[:, 2 * width :] = dv[...].astype(BF)

    return pl.pallas_call(
        kernel,
        grid=(tiles,),
        out_shape=jax.ShapeDtypeStruct((rows, 3 * width), BF),
        in_specs=[
            pl.BlockSpec((rows, 1), lambda t: (0, 0)),
            pl.BlockSpec((1, rows), lambda t: (0, 0)),
            pl.BlockSpec((TILE, width), lambda t: (t, 0)),
            pl.BlockSpec((rows, width), lambda t: (0, 1)),
            pl.BlockSpec((rows, width), lambda t: (0, 2)),
            pl.BlockSpec((TILE, width), lambda t: (t, 0)),
        ],
        out_specs=pl.BlockSpec((rows, 3 * width), lambda t: (0, 0)),
        scratch_shapes=[pltpu.VMEM((rows, width), F32), pltpu.VMEM((rows, width), F32)],
        compiler_params=pltpu.CompilerParams(vmem_limit_bytes=48 << 20),
        cost_estimate=pl.CostEstimate(
            flops=16 * 10**9, bytes_accessed=14 * rows * width, transcendentals=rows * SPAN * 2 * pairs
        ),
        name="attention_back",
    )(seg_col, seg_row, project, project, project, grad)


def shards(
    tokens, cotangent, segment_ids, group_counts,
    qkv_weight, out_weight, up_weight, down_weight, small_params,
    qkv_first, out_first, up_first, down_first, small_first,
    qkv_second, out_second, up_second, down_second, small_second,
):
    width = tokens.shape[1]
    hidden = up_weight.shape[1]
    rows = tokens.shape[0]
    n = lax.axis_size("fsdp")
    nz, m = dims(n)
    perms = build_perms(n)
    chip = lax.axis_index("fsdp")
    core = lax.axis_index("grp")
    z, y, x = chip // (m * m), chip // m % m, chip % m
    coords = jnp.stack([z, y, x, core]).astype(jnp.int32)
    r = qkv_weight.shape[0]
    ratio = down_weight.shape[0] // r

    counts = group_counts.astype(F32)
    share = counts / jnp.sum(counts)
    is_local = core >= lax.axis_size("grp") // 2
    mine = jnp.where(is_local, share[1], share[0])
    scale = mine.reshape(1)

    def half(w):
        cols = w.shape[1] // 2
        return lax.dynamic_slice_in_dim(w, core * cols, cols, 1).astype(BF)

    piece = small_params.astype(BF)
    stack = jnp.stack([piece] + [send(piece, perms["z"][k]) for k in range(1, nz)])
    stack = jnp.stack([stack] + [send(stack, perms["y"][k]) for k in range(1, m)])
    stack = jnp.stack([stack] + [send(stack, perms["x"][k]) for k in range(1, m)])
    index = jnp.arange(n)
    place = (((x - index % m) % m) * m + (y - index // m % m) % m) * nz + (z - index // (m * m)) % nz
    small_full = jnp.take(stack.reshape(n, -1), place, axis=0).reshape(-1).astype(F32)
    gain_one, bias_one, bias_query, bias_value, bias_out, gain_two, bias_two, bias_up, bias_down = (
        unpack(small_full, width, hidden)
    )

    own_one = jnp.concatenate([half(qkv_weight), half(out_weight)], 1)
    own_two = half(up_weight)
    low_down = half(down_weight)
    own_three = jnp.concatenate([low_down[s * r : (s + 1) * r] for s in range(ratio)], 1)
    hq, ho, hu = 3 * width // 2, width // 2, hidden // 2

    mine_one, other_one = gather_pieces(own_one, perms, nz, m)
    qkv_full, out_full = assemble(
        coords, mine_one, other_one, nz, m, [(width, 3 * width), (width, width)],
        lambda chip, c: [(0, chip * r, r, c * hq, hq, 0), (1, chip * r, r, c * ho, ho, hq)],
        "assemble_qkv_out",
    )
    mine_two, other_two = gather_pieces(own_two, perms, nz, m)
    (up_full,) = assemble(
        coords, mine_two, other_two, nz, m, [(width, hidden)],
        lambda chip, c: [(0, chip * r, r, c * hu, hu, 0)],
        "assemble_up",
    )
    mine_three, other_three = gather_pieces(own_three, perms, nz, m)
    (down_full,) = assemble(
        coords, mine_three, other_three, nz, m, [(hidden, width)],
        lambda chip, c: [
            (0, (chip * ratio + s) * r, r, c * ho, ho, s * ho) for s in range(ratio)
        ],
        "assemble_down",
    )

    inputs = tokens.astype(F32)
    normed_one = layer_norm(inputs, gain_one, bias_one).astype(BF)
    qkv_bias = jnp.concatenate([bias_query, jnp.zeros_like(bias_query), bias_value])
    project = (jnp.dot(normed_one, qkv_full, preferred_element_type=F32) + qkv_bias).astype(BF)
    seg_col, seg_row = segment_ids.reshape(rows, 1), segment_ids.reshape(1, rows)
    att = attention(project, seg_col, seg_row)
    middle = inputs + jnp.dot(att, out_full, preferred_element_type=F32) + bias_out
    normed_two = layer_norm(middle, gain_two, bias_two).astype(BF)
    pre_act = jnp.dot(normed_two, up_full, preferred_element_type=F32) + bias_up
    act = jax.nn.gelu(pre_act).astype(BF)
    output = middle + jnp.dot(act, down_full, preferred_element_type=F32) + bias_down
    block_output = output.astype(BF)

    def reduced(left, right, name):
        other = weight_grad(coords, scale, left, right, 1, nz, m, name + "_other")
        own = weight_grad(coords, scale, left, right, 0, nz, m, name + "_own")
        return reduce_pieces(own, other, perms, nz, m), own[0]

    grad_out = cotangent.astype(F32)
    grad_bias_down = jnp.sum(grad_out, 0)
    half_down, done = reduced(act, cotangent, "grad_down")
    grad_act = jnp.einsum("td,fd->tf", after(cotangent, done), down_full, preferred_element_type=F32)
    grad_pre = jax.vjp(jax.nn.gelu, pre_act)[1](grad_act)[0].astype(BF)
    grad_bias_up = jnp.sum(grad_pre.astype(F32), 0)
    half_up, done = reduced(normed_two, grad_pre, "grad_up")
    grad_normed_two = jnp.einsum("tf,df->td", after(grad_pre, done), up_full, preferred_element_type=F32)
    grad_mid, grad_gain_two, grad_bias_two = jax.vjp(layer_norm, middle, gain_two, bias_two)[1](
        grad_normed_two
    )
    grad_mid = grad_out + grad_mid
    grad_mid_low = grad_mid.astype(BF)
    grad_bias_out = jnp.sum(grad_mid_low.astype(F32), 0)
    half_out, done = reduced(att, grad_mid_low, "grad_out")
    grad_att = jnp.einsum("te,de->td", after(grad_mid_low, done), out_full, preferred_element_type=F32).astype(BF)
    grad_project = attention_back(project, grad_att, seg_col, seg_row)
    half_qkv, done = reduced(normed_one, grad_project, "grad_qkv")
    grad_project = after(grad_project, done)
    grad_project_wide = grad_project.astype(F32)
    grad_bias_query = jnp.sum(grad_project_wide[:, :width], 0)
    grad_bias_value = jnp.sum(grad_project_wide[:, 2 * width :], 0)
    grad_normed_one = jnp.einsum("te,de->td", grad_project, qkv_full, preferred_element_type=F32)
    grad_in, grad_gain_one, grad_bias_one = jax.vjp(layer_norm, inputs, gain_one, bias_one)[1](
        grad_normed_one
    )
    tokens_grad = (grad_mid + grad_in).astype(BF)

    grad_small = mine * jnp.concatenate(
        [
            grad_gain_one, grad_bias_one, grad_bias_query, grad_bias_value, grad_bias_out,
            grad_gain_two, grad_bias_two, grad_bias_up, grad_bias_down,
        ]
    )
    part = (grad_small + lax.ppermute(grad_small, "grp", SWAP)).reshape(nz, m, m, -1)
    for axis, at, size, dim in (("y", y, m, 1), ("x", x, m, 1), ("z", z, nz, 0)):
        recv = [
            send(lax.dynamic_index_in_dim(part, (at + k) % size, dim, False), perms[axis][k])
            for k in range(1, size)
        ]
        part = lax.dynamic_index_in_dim(part, at, dim, False)
        for piece in recv:
            part = part + piece
    merged_small = part

    def joined(piece):
        low = piece.astype(BF)
        got = lax.ppermute(low, "grp", SWAP)
        left = jnp.where(core == 0, low, got)
        right = jnp.where(core == 0, got, low)
        return jnp.concatenate([left, right], 1).astype(F32)

    merged = tuple(joined(p) for p in (half_qkv, half_out, half_up, half_down)) + (merged_small,)
    total_sq = sum((jnp.sum(piece * piece) for piece in merged)).reshape(1, 1)
    for axis, size in (("x", m), ("y", m), ("z", nz)):
        got = [total_sq] + [send(total_sq, perms[axis][k]) for k in range(1, size)]
        while len(got) > 1:
            step = len(got) // 2
            got = [got[k] + got[k + step] for k in range(step)]
        total_sq = got[0]
    total_sq = total_sq[0, 0]
    clip = jnp.minimum(1.0, CLIP * lax.rsqrt(total_sq))
    olds = (qkv_weight, out_weight, up_weight, down_weight, small_params)
    firsts = (qkv_first, out_first, up_first, down_first, small_first)
    seconds = (qkv_second, out_second, up_second, down_second, small_second)
    decays = (DECAY, DECAY, DECAY, DECAY, 0.0)
    rates = (RATE, RATE, RATE, RATE, RATE_SMALL)
    results = [
        adam(w, f, s, g * clip, dc, rt)
        for w, f, s, g, dc, rt in zip(olds, firsts, seconds, merged, decays, rates)
    ]
    return (
        block_output,
        tokens_grad,
        *[res[0] for res in results],
        *[res[1] for res in results],
        *[res[2] for res in results],
        total_sq,
    )


def solution(mesh):
    token, flat, row, vec = P(BOTH, None), P(BOTH), P("fsdp", None), P("fsdp")
    params = (row, row, row, row, vec)
    return jax.shard_map(
        shards,
        mesh=mesh,
        in_specs=(token, token, flat, P()) + params * 3,
        out_specs=(token, token) + params * 3 + (P(),),
        check_vma=False,
    )
```

```python
import math

import jax
import jax.numpy as jnp
from jax import lax
from jax.experimental import pallas as pl
from jax.experimental.pallas import tpu as pltpu
from jax.sharding import PartitionSpec as P

HD = 64
STEP = 10
EPS_NORM = 1e-06
CLIP = 1.0
RATE = 0.04
RATE_SMALL = 0.25
DECAY = 0.05
BETA_ONE = 0.9
BETA_TWO = 0.999
EPS_ADAM = 1e-08
F32 = jnp.float32
BF = jnp.bfloat16
BOTH = ("grp", "fsdp")
SWAP = [(0, 1), (1, 0)]
ANY = pl.BlockSpec(memory_space=pl.ANY)
SMEM = pl.BlockSpec(memory_space=pltpu.SMEM)
TILE = 128

RATIO = 0.1


def cost(us):
    return pl.CostEstimate(flops=int(us * RATIO * 1e9), bytes_accessed=0, transcendentals=0)


VMEM = pl.BlockSpec(memory_space=pltpu.VMEM)
SPAN = 256


def dims(n):
    m = max(1, math.isqrt(n // 4))
    return n // (m * m), m


def build_perms(n):
    nz, m = dims(n)

    def chip(z, y, x):
        return (z % nz) * m * m + (y % m) * m + x % m

    def build(move):
        return [
            (c * n + chip(z, y, x), c * n + chip(*move(c, z, y, x)))
            for c in range(2)
            for z in range(nz)
            for y in range(m)
            for x in range(m)
        ]

    return {
        "z": [build(lambda c, z, y, x: (z + k, y, x)) for k in range(nz)],
        "zx": [build(lambda c, z, y, x: (z ^ k, y, x)) for k in range(nz)],
        "a": [build(lambda c, z, y, x: (z, y, x + k) if c == 0 else (z, y + k, x)) for k in range(m)],
        "b": [build(lambda c, z, y, x: (z, y + k, x) if c == 0 else (z, y, x + k)) for k in range(m)],
        "x": [build(lambda c, z, y, x: (z, y, x + k)) for k in range(m)],
        "y": [build(lambda c, z, y, x: (z, y + k, x)) for k in range(m)],
    }


def send(value, table):
    return lax.ppermute(value, BOTH, table)


def layer_norm(x, gain, bias):
    mean = jnp.mean(x, -1, keepdims=True)
    centred = x - mean
    var = jnp.mean(centred * centred, -1, keepdims=True)
    return centred * lax.rsqrt(var + EPS_NORM) * gain + bias


def unpack(small, width, hidden):
    pieces = [small[i * width : (i + 1) * width] for i in range(7)]
    return pieces + [small[7 * width : 7 * width + hidden], small[7 * width + hidden :]]


def adam(weight, first, second, grad, decay, rate):
    first = BETA_ONE * first + (1.0 - BETA_ONE) * grad
    second = BETA_TWO * second + (1.0 - BETA_TWO) * grad * grad
    step_size = (
        first / (1.0 - BETA_ONE**STEP) / (jnp.sqrt(second / (1.0 - BETA_TWO**STEP)) + EPS_ADAM)
    )
    return (weight - rate * (step_size + decay * weight), first, second)


def after(value, *deps):
    return lax.optimization_barrier((value, *deps))[0]


def after_all(values, *deps):
    return lax.optimization_barrier((*values, *deps))[: len(values)]


class Gather:
    def __init__(self, perms, nz, m):
        self.perms, self.nz, self.m = perms, nz, m

    def first(self, start, *hold):
        got = [send(start, self.perms["a"][k]) for k in range(1, self.m)]
        return jnp.stack([after(start, *hold) if hold else start] + got)

    def second(self, part, *deps):
        held = after(part, *deps) if deps else part
        return [part] + [send(held, self.perms["b"][k]) for k in range(1, self.m)]

    def swapped(self, parts, *deps):
        deps = deps or [None] * len(parts)
        first, last = deps[0], deps[-1]
        return [
            lax.ppermute(p if dep is None else after(p, dep), "grp", SWAP)
            for p, dep in zip(parts, [first] + [last] * (len(parts) - 1))
        ]

    def far_start(self, own):
        return jnp.concatenate([own, send(own, self.perms["zx"][1])])

    def far(self, got, deps, hold=()):
        step = 2
        while step < self.nz:
            came = send(after(got, *deps), self.perms["zx"][step])
            got = jnp.concatenate([after(got, *hold) if hold else got, came])
            step *= 2
        return got[1:]

    def sources(self, column, near, near_got, wide, wide_got):
        found = []
        for side, (close, parts) in enumerate(((near, wide), (near_got, wide_got))):
            for ib in range(self.m):
                found.append((close[ib], column, side, [((ia,), 0, ia, ib) for ia in range(self.m)]))
                pieces = [((ia, k - 1), k, ia, ib) for ia in range(self.m) for k in range(1, self.nz)]
                found.append((parts[ib], 0, side, pieces))
        return found


def start_pieces(refs, coord, sources, r, m, put, sems):
    z, y, x, c = coord[0], coord[1], coord[2], coord[3]
    for side in range(2):
        core = c if side == 0 else 1 - c
        for ref, (_, base, at, pieces) in zip(refs, sources):
            if at != side:
                continue
            for index, dz, ia, ib in pieces:
                px = lax.rem(x - jnp.where(core == 0, ia, ib) + m, m)
                py = lax.rem(y - jnp.where(core == 0, ib, ia) + m, m)
                chip = (jnp.bitwise_xor(z, dz) * m + py) * m + px
                src = ref.at[index]
                for dst, scol, cols in put(chip, core):
                    pltpu.make_async_copy(src.at[:, pl.ds(base + scol, cols)], dst, sems.at[side]).start()


def wait_bytes(ref, sem):
    pltpu.make_async_copy(ref, ref, sem).wait()


def aligned_rows(row, r):
    return pl.ds(pl.multiple_of(row, 16), r)


def aligned_cols(col, cols):
    return pl.ds(pl.multiple_of(col, 128), cols)


def pack(coords, qkv, out, up, down, width):
    r = qkv.shape[0]
    quarter, half, wide = width // 4, width // 2, up.shape[1] // 2
    ratio = down.shape[0] // r
    groups = [6 * quarter + half, wide, ratio * half]

    def kernel(coord, q_ref, o_ref, u_ref, d_ref, *outs):
        c = coord[3]

        def store(group, col, value):
            low = value.astype(BF)
            cols = low.shape[1]
            outs[1 + group][0, :, col : col + cols] = low
            at = sum(groups[:group]) + col
            outs[0][0, :, at : at + cols] = low

        for hh in range(2):
            for t in range(3):
                cols = aligned_cols(t * width + hh * half + c * quarter, quarter)
                store(0, (hh * 3 + t) * quarter, q_ref[:, cols])
        store(0, 6 * quarter, o_ref[:, aligned_cols(c * half, half)])
        store(1, 0, u_ref[:, aligned_cols(c * wide, wide)])
        for i in range(ratio):
            store(2, i * half, d_ref[i * r : (i + 1) * r, aligned_cols(c * half, half)])

    return pl.pallas_call(
        kernel,
        out_shape=[jax.ShapeDtypeStruct((1, r, cols), BF) for cols in [sum(groups)] + groups],
        in_specs=[SMEM] + [VMEM] * 4,
        out_specs=[VMEM] * 4,
        compiler_params=pltpu.CompilerParams(vmem_limit_bytes=60 << 20),
        cost_estimate=cost(4),
        name="pack",
    )(coords, qkv, out, up, down)


def assemble(coords, sources, r, m, shape, plan, name):
    def kernel(coord, *refs):
        out, sems = refs[-2:]

        def put(chip, core):
            return [
                (out.at[aligned_rows(row, r), aligned_cols(col, cols)], scol, cols)
                for row, col, cols, scol in plan(chip, core)
            ]

        start_pieces(refs, coord, sources, r, m, put, sems)
        for side in range(2):
            wait_bytes(out.at[:, pl.ds(0, shape[1] // 2)], sems.at[side])

    return pl.pallas_call(
        kernel,
        out_shape=jax.ShapeDtypeStruct(shape, BF),
        in_specs=[SMEM] + [ANY] * len(sources),
        out_specs=pl.BlockSpec(memory_space=pltpu.VMEM),
        scratch_shapes=[pltpu.SemaphoreType.DMA((2,))],
        compiler_params=pltpu.CompilerParams(vmem_limit_bytes=60 << 20),
        cost_estimate=cost(4),
        name=name,
    )(coords, *[source[0] for source in sources])


def project_qkv(coords, sources, normed, bias, r, m):
    rows, width = normed.shape
    part = 3 * width // 4

    def kernel(coord, a_ref, b_ref, *refs):
        out_ref, w_ref, sems = refs[-3:]

        def put(chip, core):
            return [
                (w_ref.at[core, hh, aligned_rows(chip * r, r), :], hh * part, part) for hh in range(2)
            ]

        start_pieces(refs, coord, sources, r, m, put, sems)
        for side in range(2):
            core = coord[3] if side == 0 else 1 - coord[3]
            wait_bytes(w_ref.at[0], sems.at[side])
            for hh in range(2):
                cols = aligned_cols(hh * 2 * part + core * part, part)
                for i in range(0, rows, 256):
                    out = jnp.dot(a_ref[i : i + 256, :], w_ref[core, hh], preferred_element_type=F32)
                    out_ref[i : i + 256, cols] = (out + b_ref[:, cols]).astype(BF)

    vmem = pl.BlockSpec(memory_space=pltpu.VMEM)
    return pl.pallas_call(
        kernel,
        out_shape=jax.ShapeDtypeStruct((rows, 3 * width), BF),
        in_specs=[SMEM, vmem, vmem] + [ANY] * len(sources),
        out_specs=vmem,
        scratch_shapes=[pltpu.VMEM((2, 2, width, part), BF), pltpu.SemaphoreType.DMA((2,))],
        compiler_params=pltpu.CompilerParams(vmem_limit_bytes=60 << 20),
        cost_estimate=cost(10),
        name="project_qkv",
    )(coords, normed, bias.reshape(1, -1), *[source[0] for source in sources])


def project_out(coords, sources, att, tokens, bias, gain_two, bias_two, r, m, first):
    rows, width = att.shape
    half = width // 2

    def kernel(coord, a_ref, t_ref, b_ref, g_ref, c_ref, *refs):
        mid_ref, norm_ref, w_ref, sems = refs[-4:]

        def put(chip, core):
            return [(w_ref.at[aligned_rows(chip * r, r), aligned_cols(core * half, half)], first, half)]

        start_pieces(refs, coord, sources, r, m, put, sems)
        for side in range(2):
            wait_bytes(w_ref.at[:, pl.ds(0, half)], sems.at[side])
        for i in range(0, rows, 128):
            part = slice(i, i + 128)
            mid = (
                t_ref[part, :].astype(F32)
                + jnp.dot(a_ref[part, :], w_ref[...], preferred_element_type=F32)
                + b_ref[...]
            )
            mid_ref[part, :] = mid
            norm_ref[part, :] = layer_norm(mid, g_ref[...], c_ref[...]).astype(BF)

    vmem = pl.BlockSpec(memory_space=pltpu.VMEM)
    return pl.pallas_call(
        kernel,
        out_shape=[
            jax.ShapeDtypeStruct((rows, width), F32),
            jax.ShapeDtypeStruct((rows, width), BF),
            jax.ShapeDtypeStruct((width, width), BF),
        ],
        in_specs=[SMEM] + [vmem] * 5 + [ANY] * len(sources),
        out_specs=[vmem] * 3,
        scratch_shapes=[pltpu.SemaphoreType.DMA((2,))],
        compiler_params=pltpu.CompilerParams(vmem_limit_bytes=60 << 20),
        cost_estimate=cost(8),
        name="project_out",
    )(
        coords, att, tokens, bias.reshape(1, -1), gain_two.reshape(1, -1), bias_two.reshape(1, -1),
        *[source[0] for source in sources],
    )


def weight_grad(coords, scale, pairs, nz, m, name, us):
    tokens, total = pairs[0][0].shape
    halves = [right.shape[1] // 2 for _, right in pairs]
    cols = sum(halves)
    r = total // (nz * m * m)
    zrows = total // nz
    mt = min(256, zrows)
    mc = zrows // mt
    count = len(pairs)

    def kernel(coord, scale_ref, *refs):
        x_hbm = refs[0 : 2 * count : 2]
        y_hbm = refs[1 : 2 * count : 2]
        outs = refs[2 * count : 2 * count + 2]
        scratch = refs[2 * count + 2 :]
        xv = scratch[0:count]
        yv = scratch[count : 2 * count]
        acc, xsem, ysem, osem = scratch[2 * count :]
        z, y, x, c = coord[0], coord[1], coord[2], coord[3]
        weight = scale_ref[0]

        def xcopy(p, dz, i):
            pz = lax.rem(z + dz, nz)
            return pltpu.make_async_copy(
                x_hbm[p].at[:, pl.ds(pl.multiple_of(pz * zrows + i * mt, 128), mt)],
                xv[p].at[dz * mc + i],
                xsem.at[p, dz * mc + i],
            )

        def ycopy(p, side):
            owner = c if side == 0 else 1 - c
            return pltpu.make_async_copy(
                y_hbm[p].at[:, pl.ds(pl.multiple_of(owner * halves[p], 128), halves[p])],
                yv[p].at[side],
                ysem.at[p, side],
            )

        for p in range(count):
            xcopy(p, 0, 0).start()
            ycopy(p, 1).start()
            ycopy(p, 0).start()
        for p in range(count):
            for dz in range(nz):
                for i in range(mc):
                    if dz or i:
                        xcopy(p, dz, i).start()
        copies = []
        for dz in range(nz):
            for i in range(mc):
                for p in range(count):
                    low = sum(halves[:p])
                    xcopy(p, dz, i).wait()
                    left = xv[p][dz * mc + i].T
                    for side in (1, 0):
                        if dz == 0 and i == 0:
                            ycopy(p, side).wait()
                        out = jnp.dot(left, yv[p][side], preferred_element_type=F32)
                        acc[side, dz, i * mt : (i + 1) * mt, low : low + halves[p]] = (
                            out * weight
                        ).astype(BF)
            for side in (1, 0):
                owner = c if side == 0 else 1 - c
                for ib in range(m):
                    for ia in range(m):
                        dx = jnp.where(owner == 0, ia, ib)
                        dy = jnp.where(owner == 0, ib, ia)
                        px = lax.rem(x + dx, m)
                        py = lax.rem(y + dy, m)
                        copy = pltpu.make_async_copy(
                            acc.at[side, dz, pl.ds(pl.multiple_of((py * m + px) * r, 16), r), :],
                            outs[side].at[ib, ia, dz],
                            osem.at[side, dz, ib * m + ia],
                        )
                        copy.start()
                        copies.append(copy)
        for copy in copies:
            copy.wait()

    return pl.pallas_call(
        kernel,
        out_shape=[jax.ShapeDtypeStruct((m, m, nz, r, cols), BF)] * 2,
        in_specs=[SMEM, SMEM] + [ANY] * (2 * count),
        out_specs=[ANY] * 2,
        scratch_shapes=[pltpu.VMEM((nz * mc, tokens, mt), BF) for _ in pairs]
        + [pltpu.VMEM((2, tokens, h), BF) for h in halves]
        + [
            pltpu.VMEM((2, nz, zrows, cols), BF),
            pltpu.SemaphoreType.DMA((count, nz * mc)),
            pltpu.SemaphoreType.DMA((count, 2)),
            pltpu.SemaphoreType.DMA((2, nz, m * m)),
        ],
        compiler_params=pltpu.CompilerParams(vmem_limit_bytes=60 << 20),
        cost_estimate=cost(us),
        name=name,
    )(coords, scale, *[v for pair in pairs for v in pair])


def weight_grad_both(coords, scales, pairs, nz, m, name, us):
    tokens, total = pairs[0][0].shape
    widths = [[own.shape[1] for own, _ in pair[2]] for pair in pairs]
    halves = [sum(w) for w in widths]
    cols = sum(halves)
    r = total // (nz * m * m)
    zrows = total // nz
    count = len(pairs)
    operands, places = [], []
    for pair in pairs:
        places.append(len(operands))
        operands += [*pair[:2], *[v for both in pair[2] for v in both]]

    def kernel(coord, scale_ref, *refs):
        ins = refs[: len(operands)]
        outs = refs[len(operands) : len(operands) + m]
        scratch = refs[len(operands) + m :]
        held = scratch[: 4 * count]
        acc, xsem, ysem, osem = scratch[4 * count :]
        z, y, x, c = coord[0], coord[1], coord[2], coord[3]

        def xcopy(p, who, dz):
            pz = lax.rem(z + dz, nz)
            return pltpu.make_async_copy(
                ins[places[p] + who].at[:, pl.ds(pl.multiple_of(pz * zrows, 128), zrows)],
                held[4 * p + who].at[dz],
                xsem.at[p, who, dz],
            )

        def ycopies(p, who):
            dst = held[4 * p + 2 + who]
            found = []
            for k, h in enumerate(widths[p]):
                at = pl.ds(sum(widths[p][:k]), h)
                src = ins[places[p] + 2 + 2 * k + who]
                found.append(pltpu.make_async_copy(src, dst.at[:, at], ysem.at[p, who, k]))
            return found

        for p in range(count):
            for who in range(2):
                xcopy(p, who, 0).start()
                for copy in ycopies(p, who):
                    copy.start()
        for p in range(count):
            for dz in range(1, nz):
                for who in range(2):
                    xcopy(p, who, dz).start()
        copies = []
        for dz in range(nz):
            for p in range(count):
                low = sum(halves[:p])
                out = None
                for who in range(2):
                    xcopy(p, who, dz).wait()
                    if dz == 0:
                        for copy in ycopies(p, who):
                            copy.wait()
                    part = jnp.dot(
                        held[4 * p + who][dz].T, held[4 * p + 2 + who][...], preferred_element_type=F32
                    )
                    out = part * scale_ref[who] if out is None else out + part * scale_ref[who]
                acc[dz, :, low : low + halves[p]] = out.astype(BF)
            for ib in range(m):
                for ia in range(m):
                    px = lax.rem(x + jnp.where(c == 0, ia, ib), m)
                    py = lax.rem(y + jnp.where(c == 0, ib, ia), m)
                    copy = pltpu.make_async_copy(
                        acc.at[dz, aligned_rows((py * m + px) * r, r), :],
                        outs[ib].at[ia, dz],
                        osem.at[dz, ib * m + ia],
                    )
                    copy.start()
                    copies.append(copy)
        for copy in copies:
            copy.wait()

    shapes = []
    for h in halves:
        shapes += [pltpu.VMEM((nz, tokens, zrows), BF)] * 2 + [pltpu.VMEM((tokens, h), BF)] * 2
    return pl.pallas_call(
        kernel,
        out_shape=[jax.ShapeDtypeStruct((m, nz, r, cols), BF)] * m,
        in_specs=[SMEM, SMEM] + [ANY] * len(operands),
        out_specs=[ANY] * m,
        scratch_shapes=shapes
        + [
            pltpu.VMEM((nz, zrows, cols), BF),
            pltpu.SemaphoreType.DMA((count, 2, nz)),
            pltpu.SemaphoreType.DMA((count, 2, max(len(w) for w in widths))),
            pltpu.SemaphoreType.DMA((nz, m * m)),
        ],
        compiler_params=pltpu.CompilerParams(vmem_limit_bytes=60 << 20),
        cost_estimate=cost(us),
        name=name,
    )(coords, scales, *operands)


def add_parts(keep, got):
    size, cols = keep.shape[0], keep.shape[-1]
    shape = keep.shape[1:]
    flat = math.prod(shape[:-1])
    block = max(16, min(flat, (1 << 19) // (size * cols) // 16 * 16))
    while flat % block:
        block -= 16
    count = len(got) + 1

    def kernel(*refs):
        for k in range(size):
            total = refs[0][k].astype(F32)
            for ref in refs[1:count]:
                total += ref[k].astype(F32)
            refs[count + k][...] = total.astype(BF)

    outs = pl.pallas_call(
        kernel,
        grid=(flat // block,),
        out_shape=[jax.ShapeDtypeStruct((flat, cols), BF)] * size,
        in_specs=[pl.BlockSpec((size, block, cols), lambda i: (0, i, 0))] * count,
        out_specs=[pl.BlockSpec((block, cols), lambda i: (i, 0))] * size,
        compiler_params=pltpu.CompilerParams(vmem_limit_bytes=60 << 20),
        cost_estimate=cost(2),
        name="add_parts",
    )(*[v.reshape(size, flat, cols) for v in [keep, *got]])
    return [out.reshape(shape) for out in outs]


class Reduction:
    def __init__(self, parts, perms, nz, m):
        self.perms, self.sizes = perms, {"b": m, "a": m, "z": nz}
        self.left = ["a", "z"]
        self.pass_on("b", parts)

    def pass_on(self, axis, parts):
        self.keep = parts[0]
        self.got = [send(parts[k], self.perms[axis][k]) for k in range(1, self.sizes[axis])]

    def step(self, *deps):
        if not self.left:
            t = after(self.keep, *deps).astype(F32) if deps else self.keep.astype(F32)
            for part in self.got:
                t = t + part.astype(F32)
            return t
        axis = self.left.pop(0)
        parts = add_parts(after(self.keep, *deps), self.got)
        self.pass_on(axis, parts)
        return parts[-1]


def feed_up(coords, sources, normed, bias, r, m):
    rows, width = normed.shape
    hidden = bias.shape[0]
    half, cols, step = hidden // 2, 512, 256
    tiles = half // cols

    def kernel(coord, a_ref, b_ref, *refs):
        act_ref, slope_ref, w_out, w_ref, sems, osem = refs[-6:]
        j = pl.program_id(0)

        @pl.when(j == 0)
        def _():
            def put(chip, core):
                rows_at = aligned_rows(chip * r, r)
                return [(w_ref.at[core, t, rows_at, :], t * cols, cols) for t in range(tiles)]

            start_pieces(refs, coord, sources, r, m, put, sems)

        for side in range(2):

            @pl.when(j == side * tiles)
            def _():
                wait_bytes(w_ref.at[0], sems.at[side])
                core = coord[3] if side == 0 else 1 - coord[3]
                for t in range(tiles):
                    at = aligned_cols((core * tiles + t) * cols, cols)
                    pltpu.make_async_copy(w_ref.at[core, t], w_out.at[:, at], osem).start()

        @pl.when(j == 2 * tiles - 1)
        def _():
            wait_bytes(w_ref, osem)

        core = jnp.where(j < tiles, coord[3], 1 - coord[3])
        weight = w_ref[core, lax.rem(j, tiles)]
        c0, c1 = math.sqrt(2.0 / math.pi), 0.044715
        for i in range(0, rows, step):
            h = jnp.dot(a_ref[i : i + step, :], weight, preferred_element_type=F32) + b_ref[...]
            square = h * h
            t = jnp.tanh(h * (c0 + (c0 * c1) * square))
            mid = 0.5 * h
            act_ref[i : i + step, :] = (mid + mid * t).astype(BF)
            slope = 0.5 + 0.5 * t + mid * (1.0 - t * t) * (c0 + (3.0 * c0 * c1) * square)
            slope_ref[i : i + step, :] = slope.astype(BF)

    def tile(j, coord):
        return (0, jnp.where(j < tiles, coord[3], 1 - coord[3]) * tiles + lax.rem(j, tiles))

    grid_spec = pltpu.PrefetchScalarGridSpec(
        num_scalar_prefetch=1,
        grid=(2 * tiles,),
        in_specs=[
            pl.BlockSpec((rows, width), lambda j, coord: (0, 0)),
            pl.BlockSpec((1, cols), tile),
        ]
        + [ANY] * len(sources),
        out_specs=[
            pl.BlockSpec((rows, cols), tile),
            pl.BlockSpec((rows, cols), tile),
            ANY,
        ],
        scratch_shapes=[
            pltpu.VMEM((2, tiles, width, cols), BF),
            pltpu.SemaphoreType.DMA((2,)),
            pltpu.SemaphoreType.DMA,
        ],
    )
    return pl.pallas_call(
        kernel,
        grid_spec=grid_spec,
        out_shape=[
            jax.ShapeDtypeStruct((rows, hidden), BF),
            jax.ShapeDtypeStruct((rows, hidden), BF),
            jax.ShapeDtypeStruct((width, hidden), BF),
        ],
        compiler_params=pltpu.CompilerParams(vmem_limit_bytes=60 << 20),
        cost_estimate=cost(25),
        name="feed_up",
    )(coords, normed, bias.reshape(1, hidden), *[source[0] for source in sources])


def feed_back(coords, sources, grad, slope, up, r, m, ratio):
    rows, width = grad.shape
    hidden = up.shape[1]
    half, cols, step = width // 2, 512, 512
    tiles = hidden // cols

    def tile_at(j, coord):
        core = jnp.where(j < tiles // 2, coord[3], 1 - coord[3])
        return core * (tiles // 2) + lax.rem(j, tiles // 2)

    def kernel(coord, g_ref, s_ref, u_ref, *refs):
        mine_ref, other_ref, sum_ref, out_ref, d_out, d_ref, dh_ref, sems, osems = refs[-9:]
        j = pl.program_id(0)

        @pl.when(j == 0)
        def _():
            out_ref[...] = jnp.zeros_like(out_ref)

            def put(chip, core):
                return [
                    (
                        d_ref.at[
                            aligned_rows((chip * ratio + s) * r, r), aligned_cols(core * half, half)
                        ],
                        s * half,
                        half,
                    )
                    for s in range(ratio)
                ]

            start_pieces(refs, coord, sources, r, m, put, sems)
            for side in range(2):
                wait_bytes(d_ref.at[:, pl.ds(0, half)], sems.at[side])
            pltpu.make_async_copy(d_ref, d_out, osems.at[2]).start()

        slot = lax.rem(j, 2)

        @pl.when(j >= 2)
        def _():
            wait_bytes(dh_ref.at[0], osems.at[slot])

        down = d_ref[pl.ds(pl.multiple_of(tile_at(j, coord) * cols, cols), cols), :]
        total = jnp.zeros((1, cols), F32)
        for i in range(0, rows, step):
            part = lax.dot_general(
                g_ref[i : i + step, :], down, (((1,), (1,)), ((), ())), preferred_element_type=F32
            )
            dh = (part * s_ref[i : i + step, :].astype(F32)).astype(BF)
            dh_ref[slot, i : i + step, :] = dh
            total += jnp.sum(dh.astype(F32), 0, keepdims=True)
            out_ref[i : i + step, :] += lax.dot_general(
                dh, u_ref[...], (((1,), (1,)), ((), ())), preferred_element_type=F32
            )
        sum_ref[...] = total

        def copy_out(ref):
            at = aligned_cols(lax.rem(j, tiles // 2) * cols, cols)
            pltpu.make_async_copy(dh_ref.at[slot], ref.at[:, at], osems.at[slot]).start()

        @pl.when(j < tiles // 2)
        def _():
            copy_out(mine_ref)

        @pl.when(j >= tiles // 2)
        def _():
            copy_out(other_ref)

        @pl.when(j == tiles - 1)
        def _():
            for at in range(2):
                wait_bytes(dh_ref.at[0], osems.at[at])
            wait_bytes(d_ref, osems.at[2])

    grid_spec = pltpu.PrefetchScalarGridSpec(
        num_scalar_prefetch=1,
        grid=(tiles,),
        in_specs=[
            pl.BlockSpec((rows, width), lambda j, coord: (0, 0)),
            pl.BlockSpec((rows, cols), lambda j, coord: (0, tile_at(j, coord))),
            pl.BlockSpec((width, cols), lambda j, coord: (0, tile_at(j, coord))),
        ]
        + [ANY] * len(sources),
        out_specs=[
            ANY,
            ANY,
            pl.BlockSpec((1, cols), lambda j, coord: (0, tile_at(j, coord))),
            pl.BlockSpec((rows, width), lambda j, coord: (0, 0)),
            ANY,
        ],
        scratch_shapes=[
            pltpu.VMEM((hidden, width), BF),
            pltpu.VMEM((2, rows, cols), BF),
            pltpu.SemaphoreType.DMA((2,)),
            pltpu.SemaphoreType.DMA((3,)),
        ],
    )
    return pl.pallas_call(
        kernel,
        grid_spec=grid_spec,
        out_shape=[
            jax.ShapeDtypeStruct((rows, hidden // 2), BF),
            jax.ShapeDtypeStruct((rows, hidden // 2), BF),
            jax.ShapeDtypeStruct((1, hidden), F32),
            jax.ShapeDtypeStruct((rows, width), F32),
            jax.ShapeDtypeStruct((hidden, width), BF),
        ],
        compiler_params=pltpu.CompilerParams(vmem_limit_bytes=60 << 20),
        cost_estimate=cost(30),
        name="feed_back",
    )(coords, grad, slope, up, *[source[0] for source in sources])


def norm_back(x, grad, gain):
    mean = jnp.mean(x, -1, keepdims=True)
    centred = x - mean
    inv = lax.rsqrt(jnp.mean(centred * centred, -1, keepdims=True) + EPS_NORM)
    hat = centred * inv
    inner = grad * gain
    back = inv * (
        inner
        - jnp.mean(inner, -1, keepdims=True)
        - hat * jnp.mean(inner * hat, -1, keepdims=True)
    )
    return back, jnp.sum(grad * hat, 0, keepdims=True), jnp.sum(grad, 0, keepdims=True)


def middle_back(coords, cotangent, middle, grad, gain, out):
    rows, width = middle.shape
    block = min(256, rows)

    half = width // 2

    def kernel(coord, c_ref, m_ref, d_ref, g_ref, w_ref, *refs):
        dy_ref, mine_ref, other_ref, a_ref, gain_ref, bias_ref, bo_ref, bd_ref, e_ref = refs

        @pl.when(pl.program_id(0) == 0)
        def _():
            for ref in (gain_ref, bias_ref, bo_ref, bd_ref):
                ref[...] = jnp.zeros_like(ref)

        cot = c_ref[...].astype(F32)
        back, for_gain, for_bias = norm_back(m_ref[...], d_ref[...], g_ref[...])
        dy = cot + back
        low = dy.astype(BF)
        dy_ref[...] = dy
        e_ref[...] = low
        mine_ref[...] = e_ref[:, aligned_cols(coord[3] * half, half)]
        other_ref[...] = e_ref[:, aligned_cols((1 - coord[3]) * half, half)]
        a_ref[...] = lax.dot_general(
            low, w_ref[...], (((1,), (1,)), ((), ())), preferred_element_type=F32
        ).astype(BF)
        gain_ref[...] += for_gain
        bias_ref[...] += for_bias
        bo_ref[...] += jnp.sum(low.astype(F32), 0, keepdims=True)
        bd_ref[...] += jnp.sum(cot, 0, keepdims=True)

    tile = pl.BlockSpec((block, width), lambda i: (i, 0))
    part = pl.BlockSpec((block, half), lambda i: (i, 0))
    line = pl.BlockSpec((1, width), lambda i: (0, 0))
    return pl.pallas_call(
        kernel,
        grid=(rows // block,),
        out_shape=[
            jax.ShapeDtypeStruct((rows, cols), t)
            for cols, t in ((width, F32), (half, BF), (half, BF), (width, BF))
        ]
        + [jax.ShapeDtypeStruct((1, width), F32)] * 4,
        in_specs=[SMEM, tile, tile, tile, line, pl.BlockSpec((width, width), lambda i: (0, 0))],
        out_specs=[tile, part, part, tile] + [line] * 4,
        scratch_shapes=[pltpu.VMEM((block, width), BF)],
        compiler_params=pltpu.CompilerParams(vmem_limit_bytes=60 << 20),
        cost_estimate=cost(7),
        name="middle_back",
    )(coords, cotangent, middle, grad, gain.reshape(1, -1), out)


def input_back(coords, tokens, grad_mid, parts, weight, gain):
    rows, width = tokens.shape
    total = weight.shape[1]
    block = min(256, rows)
    count = len(parts)
    cols = total // count

    def kernel(coord, t_ref, m_ref, w_ref, g_ref, *refs):
        out_ref, gain_ref, bias_ref, sum_ref = refs[count:]

        @pl.when(pl.program_id(0) == 0)
        def _():
            for ref in (gain_ref, bias_ref, sum_ref):
                ref[...] = jnp.zeros_like(ref)

        grad = jnp.zeros((block, width), F32)
        for p in range(count):
            core = coord[3] if p % 2 == 0 else 1 - coord[3]
            part = refs[p][...]
            sum_ref[:, p * cols : (p + 1) * cols] += jnp.sum(part.astype(F32), 0, keepdims=True)
            weight_at = aligned_cols((p // 2 * 2 + core) * cols, cols)
            grad += lax.dot_general(
                part, w_ref[:, weight_at], (((1,), (1,)), ((), ())), preferred_element_type=F32
            )
        back, for_gain, for_bias = norm_back(t_ref[...].astype(F32), grad, g_ref[...])
        out_ref[...] = (m_ref[...] + back).astype(BF)
        gain_ref[...] += for_gain
        bias_ref[...] += for_bias

    tile = pl.BlockSpec((block, width), lambda i: (i, 0))
    line = pl.BlockSpec((1, width), lambda i: (0, 0))
    return pl.pallas_call(
        kernel,
        grid=(rows // block,),
        out_shape=[
            jax.ShapeDtypeStruct((rows, width), BF),
            jax.ShapeDtypeStruct((1, width), F32),
            jax.ShapeDtypeStruct((1, width), F32),
            jax.ShapeDtypeStruct((1, total), F32),
        ],
        in_specs=[SMEM, tile, tile, pl.BlockSpec((width, total), lambda i: (0, 0)), line]
        + [pl.BlockSpec((block, cols), lambda i: (i, 0))] * count,
        out_specs=[tile, line, line, pl.BlockSpec((1, total), lambda i: (0, 0))],
        compiler_params=pltpu.CompilerParams(vmem_limit_bytes=60 << 20),
        cost_estimate=cost(30),
        name="input_back",
    )(coords, tokens, grad_mid, weight, gain.reshape(1, -1), *parts)


def outcome(middle, act, down, bias, before, part, parts):
    rows, width = middle.shape
    hidden = act.shape[1]
    block = 128
    first = part * (rows // parts // block)

    def kernel(m_ref, a_ref, d_ref, b_ref, *refs):
        out = jnp.dot(a_ref[...], d_ref[...], preferred_element_type=F32)
        refs[-1][...] = (m_ref[...] + out + b_ref[...]).astype(BF)

    more = [] if before is None else [before]
    return pl.pallas_call(
        kernel,
        grid=(rows // parts // block,),
        out_shape=jax.ShapeDtypeStruct((rows, width), BF),
        in_specs=[
            pl.BlockSpec((block, width), lambda i: (first + i, 0)),
            pl.BlockSpec((block, hidden), lambda i: (first + i, 0)),
            pl.BlockSpec((hidden, width), lambda i: (0, 0)),
            pl.BlockSpec((1, width), lambda i: (0, 0)),
        ]
        + [ANY] * len(more),
        out_specs=pl.BlockSpec((block, width), lambda i: (first + i, 0)),
        input_output_aliases={4: 0} if more else {},
        compiler_params=pltpu.CompilerParams(vmem_limit_bytes=60 << 20),
        cost_estimate=cost(8),
        name="outcome_" + str(part),
    )(middle, act, down, bias.reshape(1, -1), *more)


def head_stack(block, low_lanes):
    zero = jnp.zeros_like(block)
    return jnp.concatenate(
        [jnp.where(low_lanes, block, zero), jnp.where(low_lanes, zero, block)], 0
    )


def window_block(t, rows):
    return jnp.clip(2 * t - 1, 0, rows // 64 - SPAN // 64)


def window_specs(rows, cols, at=0):
    return [
        pl.BlockSpec((64, cols), lambda t, i=i: (window_block(t, rows) + i, at)) for i in range(SPAN // 64)
    ]


def joined_rows(refs, lanes):
    return jnp.concatenate([ref[:, lanes] for ref in refs], 0)


def attention(project, seg_col, seg_row):
    rows, width = project.shape[0], project.shape[1] // 3
    pairs = width // (2 * HD)
    blocks = SPAN // 64

    def pair_lanes(pair, which):
        hh, rest = divmod(pair, pairs // 2)
        core, within = divmod(rest, pairs // 4)
        quarter = width // 4
        first = (hh * 2 + core) * 3 * quarter + which * quarter + within * 2 * HD
        return slice(first, first + 2 * HD)

    def kernel(row_ref, q_ref, *refs):
        cols, windows, (out_ref, probs_ref) = refs[:blocks], refs[blocks : 2 * blocks], refs[2 * blocks :]
        same = joined_rows(cols, slice(0, 1)) == row_ref[...]
        same = jnp.concatenate([same, same], 1)
        low = lax.broadcasted_iota(jnp.int32, (TILE, 2 * HD), 1) < HD
        for h in range(pairs):
            stack = head_stack(q_ref[:, pair_lanes(h, 0)], low)
            keys = joined_rows(windows, pair_lanes(h, 1))
            scores = lax.dot_general(keys, stack, (((1,), (1,)), ((), ())), preferred_element_type=F32)
            scores = jnp.where(same, scores * HD**-0.5, -1e30)
            expo = jnp.exp(scores - jnp.max(scores, 0, keepdims=True))
            probs = (expo * (1.0 / jnp.sum(expo, 0, keepdims=True))).astype(BF)
            probs_ref[0, h] = probs
            mixed = lax.dot_general(
                probs,
                joined_rows(windows, pair_lanes(h, 2)),
                (((0,), (0,)), ((), ())),
                preferred_element_type=F32,
            )
            out_ref[:, h * 2 * HD : (h + 1) * 2 * HD] = jnp.where(low, mixed[:TILE], mixed[TILE:]).astype(BF)

    return pl.pallas_call(
        kernel,
        grid=(rows // TILE,),
        out_shape=[
            jax.ShapeDtypeStruct((rows, width), BF),
            jax.ShapeDtypeStruct((rows // TILE, pairs, SPAN, 2 * TILE), BF),
        ],
        in_specs=[
            pl.BlockSpec((1, TILE), lambda t: (0, t)),
            pl.BlockSpec((TILE, 3 * width), lambda t: (t, 0)),
        ]
        + window_specs(rows, 1)
        + window_specs(rows, 3 * width),
        out_specs=[
            pl.BlockSpec((TILE, width), lambda t: (t, 0)),
            pl.BlockSpec((1, pairs, SPAN, 2 * TILE), lambda t: (t, 0, 0, 0)),
        ],
        compiler_params=pltpu.CompilerParams(vmem_limit_bytes=60 << 20),
        cost_estimate=cost(14),
        name="attention",
    )(seg_row, project, *[seg_col] * blocks, *[project] * blocks)


def attention_back(coords, project, probs, grad, hh):
    rows, width = project.shape[0], project.shape[1] // 3
    quarter = width // 4
    pairs = width // (2 * HD)
    tiles = rows // TILE
    blocks = SPAN // 64

    def kernel(coord, q_ref, p_ref, g_ref, *refs):
        windows, (mine_ref, other_ref, dk, dv) = refs[:blocks], refs[blocks:]
        t = pl.program_id(0)

        @pl.when(t == 0)
        def _():
            dk[...] = jnp.zeros_like(dk)
            dv[...] = jnp.zeros_like(dv)

        window = pl.ds(pl.multiple_of(window_block(t, rows) * 64, 64), SPAN)
        own = pl.ds(pl.multiple_of(t * TILE, TILE), TILE)
        low = lax.broadcasted_iota(jnp.int32, (TILE, 2 * HD), 1) < HD
        scale = HD**-0.5
        for side, out_ref in enumerate((mine_ref, other_ref)):
            core = coord[3] if side == 0 else 1 - coord[3]
            for within in range(pairs // 4):
                h = within * 2 * HD
                held = slice(side * quarter + h, side * quarter + h + 2 * HD)

                def lanes(which):
                    return aligned_cols(core * 3 * quarter + which * quarter + h, 2 * HD)

                queries = head_stack(q_ref[:, lanes(0)], low)
                grads = head_stack(g_ref[:, aligned_cols(core * quarter + h, 2 * HD)], low)
                soft = p_ref[0, core * (pairs // 4) + within]
                wide = soft.astype(F32)
                grad_probs = lax.dot_general(
                    joined_rows(windows, lanes(2)), grads, (((1,), (1,)), ((), ())),
                    preferred_element_type=F32,
                )
                inner = jnp.sum(wide * grad_probs, 0, keepdims=True)
                grad_scores = (wide * (grad_probs - inner)).astype(BF)
                dv[window, held] += jnp.dot(soft, grads, preferred_element_type=F32)
                dk[window, held] += jnp.dot(grad_scores, queries, preferred_element_type=F32)
                dq = lax.dot_general(
                    grad_scores, joined_rows(windows, lanes(1)), (((0,), (0,)), ((), ())),
                    preferred_element_type=F32,
                )
                out_ref[own, h : h + 2 * HD] = (
                    jnp.where(low, dq[:TILE], dq[TILE:]) * scale
                ).astype(BF)

        @pl.when(t == tiles - 1)
        def _():
            for side, out_ref in enumerate((mine_ref, other_ref)):
                held = slice(side * quarter, (side + 1) * quarter)
                out_ref[:, quarter : 2 * quarter] = (dk[:, held] * scale).astype(BF)
                out_ref[:, 2 * quarter :] = dv[:, held].astype(BF)

    whole = pl.BlockSpec((rows, 3 * quarter), lambda t: (0, 0))
    return pl.pallas_call(
        kernel,
        grid=(tiles,),
        out_shape=[jax.ShapeDtypeStruct((rows, 3 * quarter), BF)] * 2,
        in_specs=[
            SMEM,
            pl.BlockSpec((TILE, 6 * quarter), lambda t: (t, hh)),
            pl.BlockSpec((1, pairs // 2, SPAN, 2 * TILE), lambda t: (t, hh, 0, 0)),
            pl.BlockSpec((TILE, 2 * quarter), lambda t: (t, hh)),
        ]
        + window_specs(rows, 6 * quarter, hh),
        out_specs=[whole, whole],
        scratch_shapes=[pltpu.VMEM((rows, 2 * quarter), F32)] * 2,
        compiler_params=pltpu.CompilerParams(vmem_limit_bytes=60 << 20),
        cost_estimate=cost(16),
        name="attention_back_" + str(hh),
    )(coords, project, probs, grad, *[project] * blocks)


def shards(
    tokens, cotangent, segment_ids, group_counts,
    qkv_weight, out_weight, up_weight, down_weight, small_params,
    qkv_first, out_first, up_first, down_first, small_first,
    qkv_second, out_second, up_second, down_second, small_second,
):
    width = tokens.shape[1]
    hidden = up_weight.shape[1]
    rows = tokens.shape[0]
    n = lax.axis_size("fsdp")
    nz, m = dims(n)
    perms = build_perms(n)
    chip = lax.axis_index("fsdp")
    core = lax.axis_index("grp")
    z, y, x = chip // (m * m), chip // m % m, chip % m
    coords = jnp.stack([z, y, x, core]).astype(jnp.int32)
    r = qkv_weight.shape[0]
    ratio = down_weight.shape[0] // r

    counts = group_counts.astype(F32)
    share = counts / jnp.sum(counts)
    is_local = core >= lax.axis_size("grp") // 2
    mine = jnp.where(is_local, share[1], share[0])
    scales = jnp.stack([mine, jnp.where(is_local, share[0], share[1])])
    scale = mine.reshape(1)
    quarter = width // 4
    hq, ho = 3 * width // 2, width // 2

    gather = Gather(perms, nz, m)
    piece = jnp.broadcast_to(small_params.astype(BF).astype(F32), (2 * n,) + small_params.shape)
    small_full = lax.all_to_all(piece, BOTH, 0, 0, tiled=True)[:n].reshape(-1)
    packed, own_one, own_two, own_three = pack(
        coords, qkv_weight, out_weight, up_weight, down_weight, width
    )
    columns = [0, own_one.shape[2], own_one.shape[2] + own_two.shape[2]]
    near_a = gather.first(packed[0])
    pair_one = gather.far_start(own_one)
    near = gather.second(near_a, pair_one)
    near_got = gather.swapped(near)
    far_one = gather.far(pair_one, ())
    small_full = after(small_full, near_a)
    gain_one, bias_one, bias_query, bias_value, bias_out, gain_two, bias_two, bias_up, bias_down = (
        unpack(small_full, width, hidden)
    )
    normed_one = layer_norm(after(tokens, near_a).astype(F32), gain_one, bias_one).astype(BF)
    qkv_bias = jnp.stack([bias_query, jnp.zeros_like(bias_query), bias_value])
    qkv_bias = qkv_bias.reshape(3, 2, 2, quarter).transpose(1, 2, 0, 3).reshape(-1)
    a_one = gather.first(after(far_one, *near[1:]))
    wide_one = gather.second(a_one, normed_one, qkv_bias)
    one = gather.sources(0, near, near_got, wide_one, gather.swapped(wide_one))
    far_two = gather.far(gather.far_start(after(own_two, pair_one)), (far_one,))
    pair_three = gather.far_start(after(own_three, far_one))

    def exchange(value, *deps):
        return lax.ppermute(after(value, *deps) if deps else value, "grp", SWAP)

    project = project_qkv(coords, one, after(normed_one, far_two, pair_three), qkv_bias, r, m)
    a_two = gather.first(after(far_two, wide_one[-1]), project)
    wide_two = gather.second(a_two, project)
    seg_col, seg_row = segment_ids.reshape(rows, 1), segment_ids.reshape(1, rows)
    att, probs = attention(after(project, a_two), seg_col, seg_row)
    far_three = gather.far(pair_three, (far_two,), (att,))
    middle, normed_two, out_full = project_out(
        coords, one, after(att, far_three), tokens, bias_out, gain_two, bias_two, r, m, hq
    )
    a_three = gather.first(after(far_three, att), middle)
    wide_three = gather.second(a_three, middle)
    two = gather.sources(columns[1], near, near_got, wide_two, gather.swapped(wide_two, project, att))
    got_att = exchange(att)
    act, slope, up_full = feed_up(coords, two, after(normed_two, a_three), bias_up, r, m)
    three = gather.sources(columns[2], near, near_got, wide_three, gather.swapped(wide_three, act))

    got_one = exchange(normed_one, got_att)
    got_two = exchange(normed_two, act)
    own, other = weight_grad(
        coords, scale, [(after(act, got_att, *wide_three[1:]), cotangent)], nz, m, "grad_down", 15
    )
    own_got = exchange(other)
    dh_mine, dh_other, grad_bias_up, grad_normed_two, down_full = feed_back(
        coords, three, after(cotangent, other, got_one), slope, up_full, r, m, ratio
    )
    grad_bias_up = grad_bias_up.reshape(-1)
    dh_got = exchange(dh_other)
    parts = add_parts(after(own, grad_normed_two), [own_got])
    sum_down = Reduction(parts, perms, nz, m)
    (grad_mid, e_mine, e_other, grad_att, *sums) = middle_back(
        coords, cotangent, middle, after(grad_normed_two, parts[-1]), gain_two, out_full
    )
    grad_gain_two, grad_bias_two, grad_bias_out, grad_bias_down = (v.reshape(-1) for v in sums)
    parts = weight_grad_both(
        coords, scales, [(normed_two, got_two, [(after(dh_mine, grad_mid), dh_got)])], nz, m, "grad_up", 14
    )
    sum_up = Reduction(parts, perms, nz, m)
    done = sum_down.step(parts[0])
    grad_att = after(grad_att, done)
    e_got = exchange(e_other, done)
    mine_one, other_one = attention_back(coords, project, probs, grad_att, 0)
    one_got = exchange(other_one)
    done = sum_down.step(mine_one)
    mine_two, other_two = attention_back(coords, project, probs, after(grad_att, done), 1)
    two_got = exchange(other_two)
    done = sum_up.step(mine_two)
    parts = weight_grad_both(
        coords,
        scales,
        [
            (normed_one, got_one, [(after(mine_one, done), one_got), (mine_two, two_got)]),
            (att, got_att, [(e_mine, e_got)]),
        ],
        nz, m, "grad_qkv_out", 16,
    )
    done = sum_up.step(parts[0], *sum_down.got[:2])
    sum_one = Reduction([parts[0]] + [after(part, done) for part in parts[1:]], perms, nz, m)

    qkv_full = assemble(
        after(coords, parts[0], done), one, r, m, (width, 3 * width),
        lambda chip, c: [(chip * r, hh * hq + c * (hq // 2), hq // 2, hh * (hq // 2)) for hh in range(2)],
        "assemble_qkv",
    )
    tokens_grad, *sums = input_back(coords, tokens, grad_mid, [mine_one, other_one, mine_two, other_two], qkv_full, gain_one)
    done = sum_one.step(tokens_grad, *sum_down.got[2:], *sum_up.got[:2])
    sums = after_all(sums, done)
    grad_gain_one, grad_bias_one = sums[0].reshape(-1), sums[1].reshape(-1)
    sums = sums[2].reshape(2, 2, 3, quarter)
    sums = jnp.where(core == 0, sums, sums[:, ::-1]).transpose(2, 0, 1, 3)
    grad_bias_query = sums[0].reshape(-1)
    grad_bias_value = sums[2].reshape(-1)

    grad_small = jnp.concatenate(
        [
            grad_gain_one, grad_bias_one, grad_bias_query, grad_bias_value, grad_bias_out,
            grad_gain_two, grad_bias_two, grad_bias_up, grad_bias_down,
        ]
    )
    grad_small = mine * grad_small.reshape(n, -1)
    grad_small = lax.all_to_all(
        jnp.concatenate([grad_small, grad_small]), BOTH, 0, 0, tiled=True
    )

    top = outcome(middle, after(act, done), down_full, bias_down, None, 0, 2)
    done = sum_one.step(top, *sum_up.got[2:])
    block_output = outcome(middle, act, down_full, bias_down, after(top, done), 1, 2)
    half_down = sum_down.step(block_output)
    half_up = sum_up.step(block_output)
    half_one = sum_one.step(block_output)
    merged_small = jnp.sum(after(grad_small, half_one), 0)
    half_qkv = half_one[:, :hq]
    half_rest = jnp.concatenate([half_up, half_one[:, hq:]], 1)
    hu = hidden // 2

    lows = [piece.astype(BF) for piece in (half_qkv, half_rest, half_down)]
    wide = [piece.astype(F32) for piece in lows]
    small_sq = jnp.where(core == 0, jnp.sum(merged_small * merged_small), 0.0)
    local_sq = sum((jnp.sum(piece * piece) for piece in wide)) + small_sq
    everyone = 2 * n
    shared = lax.all_to_all(jnp.full((everyone, 128), local_sq, F32), BOTH, 0, 0, tiled=True)
    total_sq = jnp.sum(shared[:, 0])
    got = [lax.ppermute(low, "grp", SWAP).astype(F32) for low in lows]

    def joined(i, first, last):
        a, b = wide[i][:, first:last], got[i][:, first:last]
        return jnp.concatenate([jnp.where(core == 0, a, b), jnp.where(core == 0, b, a)], 1)

    def qkv_joined():
        a, b = (v[0].reshape(r, 2, 3, 1, quarter) for v in (wide, got))
        pair = jnp.concatenate([jnp.where(core == 0, a, b), jnp.where(core == 0, b, a)], 3)
        return pair.transpose(0, 2, 1, 3, 4).reshape(r, -1)

    merged = (
        qkv_joined(),
        joined(1, hu, hu + ho),
        joined(1, 0, hu),
        joined(2, 0, ho),
        merged_small,
    )
    clip = jnp.minimum(1.0, CLIP * lax.rsqrt(total_sq))
    olds = (qkv_weight, out_weight, up_weight, down_weight, small_params)
    firsts = (qkv_first, out_first, up_first, down_first, small_first)
    seconds = (qkv_second, out_second, up_second, down_second, small_second)
    decays = (DECAY, DECAY, DECAY, DECAY, 0.0)
    rates = (RATE, RATE, RATE, RATE, RATE_SMALL)
    results = [
        adam(w, f, s, g * clip, dc, rt)
        for w, f, s, g, dc, rt in zip(olds, firsts, seconds, merged, decays, rates)
    ]
    return (
        block_output,
        tokens_grad,
        *[res[0] for res in results],
        *[res[1] for res in results],
        *[res[2] for res in results],
        total_sq,
    )


def solution(mesh):
    token, flat, row, vec = P(BOTH, None), P(BOTH), P("fsdp", None), P("fsdp")
    params = (row, row, row, row, vec)
    return jax.shard_map(
        shards,
        mesh=mesh,
        in_specs=(token, token, flat, P()) + params * 3,
        out_specs=(token, token) + params * 3 + (P(),),
        check_vma=False,
    )
```

```python
import math

import jax
import jax.numpy as jnp
from jax import lax
from jax.experimental import pallas as pl
from jax.experimental.pallas import tpu as pltpu
from jax.sharding import PartitionSpec as P

HD = 64
STEP = 10
EPS_NORM = 1e-06
CLIP = 1.0
RATE = 0.04
RATE_SMALL = 0.25
DECAY = 0.05
BETA_ONE = 0.9
BETA_TWO = 0.999
EPS_ADAM = 1e-08
F32 = jnp.float32
BF = jnp.bfloat16
BOTH = ("grp", "fsdp")
SWAP = [(0, 1), (1, 0)]
ANY = pl.BlockSpec(memory_space=pl.ANY)
SMEM = pl.BlockSpec(memory_space=pltpu.SMEM)
TILE = 128

RATIO = 0.1


def cost(us):
    return pl.CostEstimate(flops=int(us * RATIO * 1e9), bytes_accessed=0, transcendentals=0)


VMEM = pl.BlockSpec(memory_space=pltpu.VMEM)
SPAN = 256


def dims(n):
    m = max(1, math.isqrt(n // 4))
    return n // (m * m), m


def build_perms(n):
    nz, m = dims(n)

    def chip(z, y, x):
        return (z % nz) * m * m + (y % m) * m + x % m

    def build(move):
        return [
            (c * n + chip(z, y, x), c * n + chip(*move(c, z, y, x)))
            for c in range(2)
            for z in range(nz)
            for y in range(m)
            for x in range(m)
        ]

    return {
        "z": [build(lambda c, z, y, x: (z + k, y, x)) for k in range(nz)],
        "zx": [build(lambda c, z, y, x: (z ^ k, y, x)) for k in range(nz)],
        "a": [build(lambda c, z, y, x: (z, y, x + k) if c == 0 else (z, y + k, x)) for k in range(m)],
        "b": [build(lambda c, z, y, x: (z, y + k, x) if c == 0 else (z, y, x + k)) for k in range(m)],
        "x": [build(lambda c, z, y, x: (z, y, x + k)) for k in range(m)],
        "y": [build(lambda c, z, y, x: (z, y + k, x)) for k in range(m)],
    }


def send(value, table):
    return lax.ppermute(value, BOTH, table)


def layer_norm(x, gain, bias):
    mean = jnp.mean(x, -1, keepdims=True)
    centred = x - mean
    var = jnp.mean(centred * centred, -1, keepdims=True)
    return centred * lax.rsqrt(var + EPS_NORM) * gain + bias


def unpack(small, width, hidden):
    pieces = [small[i * width : (i + 1) * width] for i in range(7)]
    return pieces + [small[7 * width : 7 * width + hidden], small[7 * width + hidden :]]


def adam(weight, first, second, grad, decay, rate):
    first = BETA_ONE * first + (1.0 - BETA_ONE) * grad
    second = BETA_TWO * second + (1.0 - BETA_TWO) * grad * grad
    step_size = (
        first / (1.0 - BETA_ONE**STEP) / (jnp.sqrt(second / (1.0 - BETA_TWO**STEP)) + EPS_ADAM)
    )
    return (weight - rate * (step_size + decay * weight), first, second)


def after(value, *deps):
    return lax.optimization_barrier((value, *deps))[0]


def after_all(values, *deps):
    return lax.optimization_barrier((*values, *deps))[: len(values)]


class Gather:
    def __init__(self, perms, nz, m):
        self.perms, self.nz, self.m = perms, nz, m

    def first(self, start, *hold):
        got = [send(start, self.perms["a"][k]) for k in range(1, self.m)]
        return jnp.stack([after(start, *hold) if hold else start] + got)

    def second(self, part, *deps):
        held = after(part, *deps) if deps else part
        return [part] + [send(held, self.perms["b"][k]) for k in range(1, self.m)]

    def swapped(self, parts, *deps):
        deps = deps or [None] * len(parts)
        first, last = deps[0], deps[-1]
        return [
            lax.ppermute(p if dep is None else after(p, dep), "grp", SWAP)
            for p, dep in zip(parts, [first] + [last] * (len(parts) - 1))
        ]

    def far_start(self, own):
        return jnp.concatenate([own, send(own, self.perms["zx"][1])])

    def far(self, got, deps, hold=()):
        step = 2
        while step < self.nz:
            came = send(after(got, *deps), self.perms["zx"][step])
            got = jnp.concatenate([after(got, *hold) if hold else got, came])
            step *= 2
        return got[1:]

    def sources(self, column, near, near_got, wide, wide_got):
        found = []
        for side, (close, parts) in enumerate(((near, wide), (near_got, wide_got))):
            for ib in range(self.m):
                found.append((close[ib], column, side, [((ia,), 0, ia, ib) for ia in range(self.m)]))
                pieces = [((ia, k - 1), k, ia, ib) for ia in range(self.m) for k in range(1, self.nz)]
                found.append((parts[ib], 0, side, pieces))
        return found


def start_pieces(refs, coord, sources, r, m, put, sems):
    z, y, x, c = coord[0], coord[1], coord[2], coord[3]
    for side in range(2):
        core = c if side == 0 else 1 - c
        for ref, (_, base, at, pieces) in zip(refs, sources):
            if at != side:
                continue
            for index, dz, ia, ib in pieces:
                px = lax.rem(x - jnp.where(core == 0, ia, ib) + m, m)
                py = lax.rem(y - jnp.where(core == 0, ib, ia) + m, m)
                chip = (jnp.bitwise_xor(z, dz) * m + py) * m + px
                src = ref.at[index]
                for dst, scol, cols in put(chip, core):
                    pltpu.make_async_copy(src.at[:, pl.ds(base + scol, cols)], dst, sems.at[side]).start()


def wait_bytes(ref, sem):
    pltpu.make_async_copy(ref, ref, sem).wait()


def aligned_rows(row, r):
    return pl.ds(pl.multiple_of(row, 16), r)


def aligned_cols(col, cols):
    return pl.ds(pl.multiple_of(col, 128), cols)


def pack(coords, qkv, out, up, down, width):
    r = qkv.shape[0]
    quarter, half, wide = width // 4, width // 2, up.shape[1] // 2
    ratio = down.shape[0] // r
    groups = [6 * quarter + half, wide, ratio * half]

    def kernel(coord, q_ref, o_ref, u_ref, d_ref, *outs):
        c = coord[3]

        def store(group, col, value):
            low = value.astype(BF)
            cols = low.shape[1]
            outs[1 + group][0, :, col : col + cols] = low
            at = sum(groups[:group]) + col
            outs[0][0, :, at : at + cols] = low

        for hh in range(2):
            for t in range(3):
                cols = aligned_cols(t * width + hh * half + c * quarter, quarter)
                store(0, (hh * 3 + t) * quarter, q_ref[:, cols])
        store(0, 6 * quarter, o_ref[:, aligned_cols(c * half, half)])
        store(1, 0, u_ref[:, aligned_cols(c * wide, wide)])
        for i in range(ratio):
            store(2, i * half, d_ref[i * r : (i + 1) * r, aligned_cols(c * half, half)])

    return pl.pallas_call(
        kernel,
        out_shape=[jax.ShapeDtypeStruct((1, r, cols), BF) for cols in [sum(groups)] + groups],
        in_specs=[SMEM] + [VMEM] * 4,
        out_specs=[VMEM] * 4,
        compiler_params=pltpu.CompilerParams(vmem_limit_bytes=60 << 20),
        cost_estimate=cost(4),
        name="pack",
    )(coords, qkv, out, up, down)


def project_qkv(coords, sources, normed, bias, r, m):
    rows, width = normed.shape
    part = 3 * width // 4

    def kernel(coord, a_ref, b_ref, *refs):
        out_ref, w_out, w_ref, sems, osem = refs[-5:]

        def put(chip, core):
            return [
                (w_ref.at[core, hh, aligned_rows(chip * r, r), :], hh * part, part) for hh in range(2)
            ]

        start_pieces(refs, coord, sources, r, m, put, sems)
        for side in range(2):
            core = coord[3] if side == 0 else 1 - coord[3]
            wait_bytes(w_ref.at[0], sems.at[side])
            for hh in range(2):
                cols = aligned_cols(hh * 2 * part + core * part, part)
                pltpu.make_async_copy(w_ref.at[core, hh], w_out.at[:, cols], osem).start()
                for i in range(0, rows, 256):
                    out = jnp.dot(a_ref[i : i + 256, :], w_ref[core, hh], preferred_element_type=F32)
                    out_ref[i : i + 256, cols] = (out + b_ref[:, cols]).astype(BF)
        wait_bytes(w_ref, osem)

    return pl.pallas_call(
        kernel,
        out_shape=[
            jax.ShapeDtypeStruct((rows, 3 * width), BF),
            jax.ShapeDtypeStruct((width, 3 * width), BF),
        ],
        in_specs=[SMEM, VMEM, VMEM] + [ANY] * len(sources),
        out_specs=[VMEM, ANY],
        scratch_shapes=[
            pltpu.VMEM((2, 2, width, part), BF),
            pltpu.SemaphoreType.DMA((2,)),
            pltpu.SemaphoreType.DMA,
        ],
        compiler_params=pltpu.CompilerParams(vmem_limit_bytes=60 << 20),
        cost_estimate=cost(10),
        name="project_qkv",
    )(coords, normed, bias.reshape(1, -1), *[source[0] for source in sources])


def project_out(coords, sources, att, tokens, bias, gain_two, bias_two, r, m, first):
    rows, width = att.shape
    half = width // 2

    def kernel(coord, a_ref, t_ref, b_ref, g_ref, c_ref, *refs):
        mid_ref, norm_ref, w_ref, sems = refs[-4:]

        def put(chip, core):
            return [(w_ref.at[aligned_rows(chip * r, r), aligned_cols(core * half, half)], first, half)]

        start_pieces(refs, coord, sources, r, m, put, sems)
        for side in range(2):
            wait_bytes(w_ref.at[:, pl.ds(0, half)], sems.at[side])
        for i in range(0, rows, 128):
            part = slice(i, i + 128)
            mid = (
                t_ref[part, :].astype(F32)
                + jnp.dot(a_ref[part, :], w_ref[...], preferred_element_type=F32)
                + b_ref[...]
            )
            mid_ref[part, :] = mid
            norm_ref[part, :] = layer_norm(mid, g_ref[...], c_ref[...]).astype(BF)

    vmem = pl.BlockSpec(memory_space=pltpu.VMEM)
    return pl.pallas_call(
        kernel,
        out_shape=[
            jax.ShapeDtypeStruct((rows, width), F32),
            jax.ShapeDtypeStruct((rows, width), BF),
            jax.ShapeDtypeStruct((width, width), BF),
        ],
        in_specs=[SMEM] + [vmem] * 5 + [ANY] * len(sources),
        out_specs=[vmem] * 3,
        scratch_shapes=[pltpu.SemaphoreType.DMA((2,))],
        compiler_params=pltpu.CompilerParams(vmem_limit_bytes=60 << 20),
        cost_estimate=cost(8),
        name="project_out",
    )(
        coords, att, tokens, bias.reshape(1, -1), gain_two.reshape(1, -1), bias_two.reshape(1, -1),
        *[source[0] for source in sources],
    )


def weight_grad(coords, scale, pairs, nz, m, name, us):
    tokens, total = pairs[0][0].shape
    halves = [right.shape[1] // 2 for _, right in pairs]
    cols = sum(halves)
    r = total // (nz * m * m)
    zrows = total // nz
    mt = min(256, zrows)
    mc = zrows // mt
    count = len(pairs)

    def kernel(coord, scale_ref, *refs):
        x_hbm = refs[0 : 2 * count : 2]
        y_hbm = refs[1 : 2 * count : 2]
        outs = refs[2 * count : 2 * count + 2]
        scratch = refs[2 * count + 2 :]
        xv = scratch[0:count]
        yv = scratch[count : 2 * count]
        acc, xsem, ysem, osem = scratch[2 * count :]
        z, y, x, c = coord[0], coord[1], coord[2], coord[3]
        weight = scale_ref[0]

        def xcopy(p, dz, i):
            pz = lax.rem(z + dz, nz)
            return pltpu.make_async_copy(
                x_hbm[p].at[:, pl.ds(pl.multiple_of(pz * zrows + i * mt, 128), mt)],
                xv[p].at[dz * mc + i],
                xsem.at[p, dz * mc + i],
            )

        def ycopy(p, side):
            owner = c if side == 0 else 1 - c
            return pltpu.make_async_copy(
                y_hbm[p].at[:, pl.ds(pl.multiple_of(owner * halves[p], 128), halves[p])],
                yv[p].at[side],
                ysem.at[p, side],
            )

        for p in range(count):
            xcopy(p, 0, 0).start()
            ycopy(p, 1).start()
            ycopy(p, 0).start()
        for p in range(count):
            for dz in range(nz):
                for i in range(mc):
                    if dz or i:
                        xcopy(p, dz, i).start()
        copies = []
        for dz in range(nz):
            for i in range(mc):
                for p in range(count):
                    low = sum(halves[:p])
                    xcopy(p, dz, i).wait()
                    left = xv[p][dz * mc + i].T
                    for side in (1, 0):
                        if dz == 0 and i == 0:
                            ycopy(p, side).wait()
                        out = jnp.dot(left, yv[p][side], preferred_element_type=F32)
                        acc[side, dz, i * mt : (i + 1) * mt, low : low + halves[p]] = (
                            out * weight
                        ).astype(BF)
            for side in (1, 0):
                owner = c if side == 0 else 1 - c
                for ib in range(m):
                    for ia in range(m):
                        dx = jnp.where(owner == 0, ia, ib)
                        dy = jnp.where(owner == 0, ib, ia)
                        px = lax.rem(x + dx, m)
                        py = lax.rem(y + dy, m)
                        copy = pltpu.make_async_copy(
                            acc.at[side, dz, pl.ds(pl.multiple_of((py * m + px) * r, 16), r), :],
                            outs[side].at[ib, ia, dz],
                            osem.at[side, dz, ib * m + ia],
                        )
                        copy.start()
                        copies.append(copy)
        for copy in copies:
            copy.wait()

    return pl.pallas_call(
        kernel,
        out_shape=[jax.ShapeDtypeStruct((m, m, nz, r, cols), BF)] * 2,
        in_specs=[SMEM, SMEM] + [ANY] * (2 * count),
        out_specs=[ANY] * 2,
        scratch_shapes=[pltpu.VMEM((nz * mc, tokens, mt), BF) for _ in pairs]
        + [pltpu.VMEM((2, tokens, h), BF) for h in halves]
        + [
            pltpu.VMEM((2, nz, zrows, cols), BF),
            pltpu.SemaphoreType.DMA((count, nz * mc)),
            pltpu.SemaphoreType.DMA((count, 2)),
            pltpu.SemaphoreType.DMA((2, nz, m * m)),
        ],
        compiler_params=pltpu.CompilerParams(vmem_limit_bytes=60 << 20),
        cost_estimate=cost(us),
        name=name,
    )(coords, scale, *[v for pair in pairs for v in pair])


def weight_grad_both(coords, scales, pairs, nz, m, name, us):
    tokens, total = pairs[0][0].shape
    widths = [[own.shape[1] for own, _ in pair[2]] for pair in pairs]
    halves = [sum(w) for w in widths]
    cols = sum(halves)
    r = total // (nz * m * m)
    zrows = total // nz
    count = len(pairs)
    operands, places = [], []
    for pair in pairs:
        places.append(len(operands))
        operands += [*pair[:2], *[v for both in pair[2] for v in both]]

    def kernel(coord, scale_ref, *refs):
        ins = refs[: len(operands)]
        outs = refs[len(operands) : len(operands) + m]
        scratch = refs[len(operands) + m :]
        held = scratch[: 4 * count]
        acc, xsem, ysem, osem = scratch[4 * count :]
        z, y, x, c = coord[0], coord[1], coord[2], coord[3]

        def xcopy(p, who, dz):
            pz = lax.rem(z + dz, nz)
            return pltpu.make_async_copy(
                ins[places[p] + who].at[:, pl.ds(pl.multiple_of(pz * zrows, 128), zrows)],
                held[4 * p + who].at[dz],
                xsem.at[p, who, dz],
            )

        def ycopies(p, who):
            dst = held[4 * p + 2 + who]
            found = []
            for k, h in enumerate(widths[p]):
                at = pl.ds(sum(widths[p][:k]), h)
                src = ins[places[p] + 2 + 2 * k + who]
                found.append(pltpu.make_async_copy(src, dst.at[:, at], ysem.at[p, who, k]))
            return found

        for p in range(count):
            for who in range(2):
                xcopy(p, who, 0).start()
                for copy in ycopies(p, who):
                    copy.start()
        for p in range(count):
            for dz in range(1, nz):
                for who in range(2):
                    xcopy(p, who, dz).start()
        copies = []
        for dz in range(nz):
            for p in range(count):
                low = sum(halves[:p])
                out = None
                for who in range(2):
                    xcopy(p, who, dz).wait()
                    if dz == 0:
                        for copy in ycopies(p, who):
                            copy.wait()
                    part = jnp.dot(
                        held[4 * p + who][dz].T, held[4 * p + 2 + who][...], preferred_element_type=F32
                    )
                    out = part * scale_ref[who] if out is None else out + part * scale_ref[who]
                acc[dz, :, low : low + halves[p]] = out.astype(BF)
            for ib in range(m):
                for ia in range(m):
                    px = lax.rem(x + jnp.where(c == 0, ia, ib), m)
                    py = lax.rem(y + jnp.where(c == 0, ib, ia), m)
                    copy = pltpu.make_async_copy(
                        acc.at[dz, aligned_rows((py * m + px) * r, r), :],
                        outs[ib].at[ia, dz],
                        osem.at[dz, ib * m + ia],
                    )
                    copy.start()
                    copies.append(copy)
        for copy in copies:
            copy.wait()

    shapes = []
    for h in halves:
        shapes += [pltpu.VMEM((nz, tokens, zrows), BF)] * 2 + [pltpu.VMEM((tokens, h), BF)] * 2
    return pl.pallas_call(
        kernel,
        out_shape=[jax.ShapeDtypeStruct((m, nz, r, cols), BF)] * m,
        in_specs=[SMEM, SMEM] + [ANY] * len(operands),
        out_specs=[ANY] * m,
        scratch_shapes=shapes
        + [
            pltpu.VMEM((nz, zrows, cols), BF),
            pltpu.SemaphoreType.DMA((count, 2, nz)),
            pltpu.SemaphoreType.DMA((count, 2, max(len(w) for w in widths))),
            pltpu.SemaphoreType.DMA((nz, m * m)),
        ],
        compiler_params=pltpu.CompilerParams(vmem_limit_bytes=60 << 20),
        cost_estimate=cost(us),
        name=name,
    )(coords, scales, *operands)


def add_parts(keep, got):
    size, cols = keep.shape[0], keep.shape[-1]
    shape = keep.shape[1:]
    flat = math.prod(shape[:-1])
    block = max(16, min(flat, (1 << 19) // (size * cols) // 16 * 16))
    while flat % block:
        block -= 16
    count = len(got) + 1

    def kernel(*refs):
        for k in range(size):
            total = refs[0][k].astype(F32)
            for ref in refs[1:count]:
                total += ref[k].astype(F32)
            refs[count + k][...] = total.astype(BF)

    outs = pl.pallas_call(
        kernel,
        grid=(flat // block,),
        out_shape=[jax.ShapeDtypeStruct((flat, cols), BF)] * size,
        in_specs=[pl.BlockSpec((size, block, cols), lambda i: (0, i, 0))] * count,
        out_specs=[pl.BlockSpec((block, cols), lambda i: (i, 0))] * size,
        compiler_params=pltpu.CompilerParams(vmem_limit_bytes=60 << 20),
        cost_estimate=cost(2),
        name="add_parts",
    )(*[v.reshape(size, flat, cols) for v in [keep, *got]])
    return [out.reshape(shape) for out in outs]


class Reduction:
    def __init__(self, parts, perms, nz, m):
        self.perms, self.sizes = perms, {"b": m, "a": m, "z": nz}
        self.left = ["a", "z"]
        self.pass_on("b", parts)

    def pass_on(self, axis, parts):
        self.keep = parts[0]
        self.got = [send(parts[k], self.perms[axis][k]) for k in range(1, self.sizes[axis])]

    def step(self, *deps):
        if not self.left:
            t = after(self.keep, *deps).astype(F32) if deps else self.keep.astype(F32)
            for part in self.got:
                t = t + part.astype(F32)
            return t
        axis = self.left.pop(0)
        parts = add_parts(after(self.keep, *deps), self.got)
        self.pass_on(axis, parts)
        return parts[-1]


def feed_up(coords, sources, normed, bias, r, m):
    rows, width = normed.shape
    hidden = bias.shape[0]
    half, cols, step = hidden // 2, 512, 256
    tiles = half // cols

    def kernel(coord, a_ref, b_ref, *refs):
        act_ref, slope_ref, w_out, w_ref, sems, osem = refs[-6:]
        j = pl.program_id(0)

        @pl.when(j == 0)
        def _():
            def put(chip, core):
                return [(w_ref.at[core, aligned_rows(chip * r, r), :], 0, half)]

            start_pieces(refs, coord, sources, r, m, put, sems)

        for side in range(2):

            @pl.when(j == side * tiles)
            def _():
                wait_bytes(w_ref.at[0], sems.at[side])
                core = coord[3] if side == 0 else 1 - coord[3]
                at = aligned_cols(core * half, half)
                pltpu.make_async_copy(w_ref.at[core], w_out.at[:, at], osem).start()

        @pl.when(j == 2 * tiles - 1)
        def _():
            wait_bytes(w_ref, osem)

        core = jnp.where(j < tiles, coord[3], 1 - coord[3])
        weight = w_ref[core, :, aligned_cols(lax.rem(j, tiles) * cols, cols)]
        c0, c1 = math.sqrt(2.0 / math.pi), 0.044715
        for i in range(0, rows, step):
            h = jnp.dot(a_ref[i : i + step, :], weight, preferred_element_type=F32) + b_ref[...]
            square = h * h
            t = jnp.tanh(h * (c0 + (c0 * c1) * square))
            mid = 0.5 * h
            act_ref[i : i + step, :] = (mid + mid * t).astype(BF)
            slope = 0.5 + 0.5 * t + mid * (1.0 - t * t) * (c0 + (3.0 * c0 * c1) * square)
            slope_ref[i : i + step, :] = slope.astype(BF)

    def tile(j, coord):
        return (0, jnp.where(j < tiles, coord[3], 1 - coord[3]) * tiles + lax.rem(j, tiles))

    grid_spec = pltpu.PrefetchScalarGridSpec(
        num_scalar_prefetch=1,
        grid=(2 * tiles,),
        in_specs=[
            pl.BlockSpec((rows, width), lambda j, coord: (0, 0)),
            pl.BlockSpec((1, cols), tile),
        ]
        + [ANY] * len(sources),
        out_specs=[
            pl.BlockSpec((rows, cols), tile),
            pl.BlockSpec((rows, cols), tile),
            ANY,
        ],
        scratch_shapes=[
            pltpu.VMEM((2, width, half), BF),
            pltpu.SemaphoreType.DMA((2,)),
            pltpu.SemaphoreType.DMA,
        ],
    )
    return pl.pallas_call(
        kernel,
        grid_spec=grid_spec,
        out_shape=[
            jax.ShapeDtypeStruct((rows, hidden), BF),
            jax.ShapeDtypeStruct((rows, hidden), BF),
            jax.ShapeDtypeStruct((width, hidden), BF),
        ],
        compiler_params=pltpu.CompilerParams(vmem_limit_bytes=60 << 20),
        cost_estimate=cost(25),
        name="feed_up",
    )(coords, normed, bias.reshape(1, hidden), *[source[0] for source in sources])


def feed_back(coords, sources, grad, slope, up, r, m, ratio):
    rows, width = grad.shape
    hidden = up.shape[1]
    half, cols, step = width // 2, 512, 512
    tiles = hidden // cols

    def tile_at(j, coord):
        core = jnp.where(j < tiles // 2, coord[3], 1 - coord[3])
        return core * (tiles // 2) + lax.rem(j, tiles // 2)

    def kernel(coord, g_ref, s_ref, u_ref, *refs):
        mine_ref, other_ref, sum_ref, out_ref, d_out, d_ref, dh_ref, sems, osems = refs[-9:]
        j = pl.program_id(0)

        @pl.when(j == 0)
        def _():
            out_ref[...] = jnp.zeros_like(out_ref)

            def put(chip, core):
                return [
                    (
                        d_ref.at[
                            aligned_rows((chip * ratio + s) * r, r), aligned_cols(core * half, half)
                        ],
                        s * half,
                        half,
                    )
                    for s in range(ratio)
                ]

            start_pieces(refs, coord, sources, r, m, put, sems)
            for side in range(2):
                wait_bytes(d_ref.at[:, pl.ds(0, half)], sems.at[side])
            pltpu.make_async_copy(d_ref, d_out, osems.at[2]).start()

        slot = lax.rem(j, 2)

        @pl.when(j >= 2)
        def _():
            wait_bytes(dh_ref.at[0], osems.at[slot])

        down = d_ref[pl.ds(pl.multiple_of(tile_at(j, coord) * cols, cols), cols), :]
        total = jnp.zeros((1, cols), F32)
        for i in range(0, rows, step):
            part = lax.dot_general(
                g_ref[i : i + step, :], down, (((1,), (1,)), ((), ())), preferred_element_type=F32
            )
            dh = (part * s_ref[i : i + step, :].astype(F32)).astype(BF)
            dh_ref[slot, i : i + step, :] = dh
            total += jnp.sum(dh.astype(F32), 0, keepdims=True)
            out_ref[i : i + step, :] += lax.dot_general(
                dh, u_ref[...], (((1,), (1,)), ((), ())), preferred_element_type=F32
            )
        sum_ref[...] = total

        def copy_out(ref):
            at = aligned_cols(lax.rem(j, tiles // 2) * cols, cols)
            pltpu.make_async_copy(dh_ref.at[slot], ref.at[:, at], osems.at[slot]).start()

        @pl.when(j < tiles // 2)
        def _():
            copy_out(mine_ref)

        @pl.when(j >= tiles // 2)
        def _():
            copy_out(other_ref)

        @pl.when(j == tiles - 1)
        def _():
            for at in range(2):
                wait_bytes(dh_ref.at[0], osems.at[at])
            wait_bytes(d_ref, osems.at[2])

    grid_spec = pltpu.PrefetchScalarGridSpec(
        num_scalar_prefetch=1,
        grid=(tiles,),
        in_specs=[
            pl.BlockSpec((rows, width), lambda j, coord: (0, 0)),
            pl.BlockSpec((rows, cols), lambda j, coord: (0, tile_at(j, coord))),
            pl.BlockSpec((width, cols), lambda j, coord: (0, tile_at(j, coord))),
        ]
        + [ANY] * len(sources),
        out_specs=[
            ANY,
            ANY,
            pl.BlockSpec((1, cols), lambda j, coord: (0, tile_at(j, coord))),
            pl.BlockSpec((rows, width), lambda j, coord: (0, 0)),
            ANY,
        ],
        scratch_shapes=[
            pltpu.VMEM((hidden, width), BF),
            pltpu.VMEM((2, rows, cols), BF),
            pltpu.SemaphoreType.DMA((2,)),
            pltpu.SemaphoreType.DMA((3,)),
        ],
    )
    return pl.pallas_call(
        kernel,
        grid_spec=grid_spec,
        out_shape=[
            jax.ShapeDtypeStruct((rows, hidden // 2), BF),
            jax.ShapeDtypeStruct((rows, hidden // 2), BF),
            jax.ShapeDtypeStruct((1, hidden), F32),
            jax.ShapeDtypeStruct((rows, width), F32),
            jax.ShapeDtypeStruct((hidden, width), BF),
        ],
        compiler_params=pltpu.CompilerParams(vmem_limit_bytes=60 << 20),
        cost_estimate=cost(50),
        name="feed_back",
    )(coords, grad, slope, up, *[source[0] for source in sources])


def norm_back(x, grad, gain):
    mean = jnp.mean(x, -1, keepdims=True)
    centred = x - mean
    inv = lax.rsqrt(jnp.mean(centred * centred, -1, keepdims=True) + EPS_NORM)
    hat = centred * inv
    inner = grad * gain
    back = inv * (
        inner
        - jnp.mean(inner, -1, keepdims=True)
        - hat * jnp.mean(inner * hat, -1, keepdims=True)
    )
    return back, jnp.sum(grad * hat, 0, keepdims=True), jnp.sum(grad, 0, keepdims=True)


def middle_back(coords, cotangent, middle, grad, gain, out):
    rows, width = middle.shape
    block = min(256, rows)

    half = width // 2

    def kernel(coord, c_ref, m_ref, d_ref, g_ref, w_ref, *refs):
        dy_ref, mine_ref, other_ref, a_ref, gain_ref, bias_ref, bo_ref, bd_ref, e_ref = refs

        @pl.when(pl.program_id(0) == 0)
        def _():
            for ref in (gain_ref, bias_ref, bo_ref, bd_ref):
                ref[...] = jnp.zeros_like(ref)

        cot = c_ref[...].astype(F32)
        back, for_gain, for_bias = norm_back(m_ref[...], d_ref[...], g_ref[...])
        dy = cot + back
        low = dy.astype(BF)
        dy_ref[...] = dy
        e_ref[...] = low
        mine_ref[...] = e_ref[:, aligned_cols(coord[3] * half, half)]
        other_ref[...] = e_ref[:, aligned_cols((1 - coord[3]) * half, half)]
        a_ref[...] = lax.dot_general(
            low, w_ref[...], (((1,), (1,)), ((), ())), preferred_element_type=F32
        ).astype(BF)
        gain_ref[...] += for_gain
        bias_ref[...] += for_bias
        bo_ref[...] += jnp.sum(low.astype(F32), 0, keepdims=True)
        bd_ref[...] += jnp.sum(cot, 0, keepdims=True)

    tile = pl.BlockSpec((block, width), lambda i: (i, 0))
    part = pl.BlockSpec((block, half), lambda i: (i, 0))
    line = pl.BlockSpec((1, width), lambda i: (0, 0))
    return pl.pallas_call(
        kernel,
        grid=(rows // block,),
        out_shape=[
            jax.ShapeDtypeStruct((rows, cols), t)
            for cols, t in ((width, F32), (half, BF), (half, BF), (width, BF))
        ]
        + [jax.ShapeDtypeStruct((1, width), F32)] * 4,
        in_specs=[SMEM, tile, tile, tile, line, pl.BlockSpec((width, width), lambda i: (0, 0))],
        out_specs=[tile, part, part, tile] + [line] * 4,
        scratch_shapes=[pltpu.VMEM((block, width), BF)],
        compiler_params=pltpu.CompilerParams(vmem_limit_bytes=60 << 20),
        cost_estimate=cost(3),
        name="middle_back",
    )(coords, cotangent, middle, grad, gain.reshape(1, -1), out)


def input_back(coords, tokens, grad_mid, parts, weight, gain):
    rows, width = tokens.shape
    total = weight.shape[1]
    block = min(256, rows)
    count = len(parts)
    cols = total // count

    def kernel(coord, t_ref, m_ref, w_ref, g_ref, *refs):
        out_ref, gain_ref, bias_ref, sum_ref = refs[count:]

        @pl.when(pl.program_id(0) == 0)
        def _():
            for ref in (gain_ref, bias_ref, sum_ref):
                ref[...] = jnp.zeros_like(ref)

        grad = jnp.zeros((block, width), F32)
        for p in range(count):
            core = coord[3] if p % 2 == 0 else 1 - coord[3]
            part = refs[p][...]
            sum_ref[:, p * cols : (p + 1) * cols] += jnp.sum(part.astype(F32), 0, keepdims=True)
            weight_at = aligned_cols((p // 2 * 2 + core) * cols, cols)
            grad += lax.dot_general(
                part, w_ref[:, weight_at], (((1,), (1,)), ((), ())), preferred_element_type=F32
            )
        back, for_gain, for_bias = norm_back(t_ref[...].astype(F32), grad, g_ref[...])
        out_ref[...] = (m_ref[...] + back).astype(BF)
        gain_ref[...] += for_gain
        bias_ref[...] += for_bias

    tile = pl.BlockSpec((block, width), lambda i: (i, 0))
    line = pl.BlockSpec((1, width), lambda i: (0, 0))
    return pl.pallas_call(
        kernel,
        grid=(rows // block,),
        out_shape=[
            jax.ShapeDtypeStruct((rows, width), BF),
            jax.ShapeDtypeStruct((1, width), F32),
            jax.ShapeDtypeStruct((1, width), F32),
            jax.ShapeDtypeStruct((1, total), F32),
        ],
        in_specs=[SMEM, tile, tile, pl.BlockSpec((width, total), lambda i: (0, 0)), line]
        + [pl.BlockSpec((block, cols), lambda i: (i, 0))] * count,
        out_specs=[tile, line, line, pl.BlockSpec((1, total), lambda i: (0, 0))],
        compiler_params=pltpu.CompilerParams(vmem_limit_bytes=60 << 20),
        cost_estimate=cost(30),
        name="input_back",
    )(coords, tokens, grad_mid, weight, gain.reshape(1, -1), *parts)


def outcome(middle, act, down, bias, before, part, parts):
    rows, width = middle.shape
    hidden = act.shape[1]
    block = 128
    first = part * (rows // parts // block)

    def kernel(m_ref, a_ref, d_ref, b_ref, *refs):
        out = jnp.dot(a_ref[...], d_ref[...], preferred_element_type=F32)
        refs[-1][...] = (m_ref[...] + out + b_ref[...]).astype(BF)

    more = [] if before is None else [before]
    return pl.pallas_call(
        kernel,
        grid=(rows // parts // block,),
        out_shape=jax.ShapeDtypeStruct((rows, width), BF),
        in_specs=[
            pl.BlockSpec((block, width), lambda i: (first + i, 0)),
            pl.BlockSpec((block, hidden), lambda i: (first + i, 0)),
            pl.BlockSpec((hidden, width), lambda i: (0, 0)),
            pl.BlockSpec((1, width), lambda i: (0, 0)),
        ]
        + [ANY] * len(more),
        out_specs=pl.BlockSpec((block, width), lambda i: (first + i, 0)),
        input_output_aliases={4: 0} if more else {},
        compiler_params=pltpu.CompilerParams(vmem_limit_bytes=60 << 20),
        cost_estimate=cost(3 if part == 0 else 10),
        name="outcome_" + str(part),
    )(middle, act, down, bias.reshape(1, -1), *more)


def head_stack(block, low_lanes):
    zero = jnp.zeros_like(block)
    return jnp.concatenate(
        [jnp.where(low_lanes, block, zero), jnp.where(low_lanes, zero, block)], 0
    )


def window_block(t, rows):
    return jnp.clip(2 * t - 1, 0, rows // 64 - SPAN // 64)


def window_specs(rows, cols, at=0):
    return [
        pl.BlockSpec((64, cols), lambda t, i=i: (window_block(t, rows) + i, at)) for i in range(SPAN // 64)
    ]


def joined_rows(refs, lanes):
    return jnp.concatenate([ref[:, lanes] for ref in refs], 0)


def attention(project, seg_col, seg_row):
    rows, width = project.shape[0], project.shape[1] // 3
    pairs = width // (2 * HD)
    blocks = SPAN // 64

    def pair_lanes(pair, which):
        hh, rest = divmod(pair, pairs // 2)
        core, within = divmod(rest, pairs // 4)
        quarter = width // 4
        first = (hh * 2 + core) * 3 * quarter + which * quarter + within * 2 * HD
        return slice(first, first + 2 * HD)

    def kernel(row_ref, q_ref, *refs):
        cols, windows, (out_ref, probs_ref) = refs[:blocks], refs[blocks : 2 * blocks], refs[2 * blocks :]
        same = joined_rows(cols, slice(0, 1)) == row_ref[...]
        same = jnp.concatenate([same, same], 1)
        low = lax.broadcasted_iota(jnp.int32, (TILE, 2 * HD), 1) < HD
        for h in range(pairs):
            stack = head_stack(q_ref[:, pair_lanes(h, 0)], low)
            keys = joined_rows(windows, pair_lanes(h, 1))
            scores = lax.dot_general(keys, stack, (((1,), (1,)), ((), ())), preferred_element_type=F32)
            scores = jnp.where(same, scores * HD**-0.5, -1e30)
            expo = jnp.exp(scores - jnp.max(scores, 0, keepdims=True))
            probs = (expo * (1.0 / jnp.sum(expo, 0, keepdims=True))).astype(BF)
            probs_ref[0, h] = probs
            mixed = lax.dot_general(
                probs,
                joined_rows(windows, pair_lanes(h, 2)),
                (((0,), (0,)), ((), ())),
                preferred_element_type=F32,
            )
            out_ref[:, h * 2 * HD : (h + 1) * 2 * HD] = jnp.where(low, mixed[:TILE], mixed[TILE:]).astype(BF)

    return pl.pallas_call(
        kernel,
        grid=(rows // TILE,),
        out_shape=[
            jax.ShapeDtypeStruct((rows, width), BF),
            jax.ShapeDtypeStruct((rows // TILE, pairs, SPAN, 2 * TILE), BF),
        ],
        in_specs=[
            pl.BlockSpec((1, TILE), lambda t: (0, t)),
            pl.BlockSpec((TILE, 3 * width), lambda t: (t, 0)),
        ]
        + window_specs(rows, 1)
        + window_specs(rows, 3 * width),
        out_specs=[
            pl.BlockSpec((TILE, width), lambda t: (t, 0)),
            pl.BlockSpec((1, pairs, SPAN, 2 * TILE), lambda t: (t, 0, 0, 0)),
        ],
        compiler_params=pltpu.CompilerParams(vmem_limit_bytes=60 << 20),
        cost_estimate=cost(14),
        name="attention",
    )(seg_row, project, *[seg_col] * blocks, *[project] * blocks)


def attention_back(coords, project, probs, grad, hh):
    rows, width = project.shape[0], project.shape[1] // 3
    quarter = width // 4
    pairs = width // (2 * HD)
    tiles = rows // TILE
    blocks = SPAN // 64

    def kernel(coord, q_ref, p_ref, g_ref, *refs):
        windows, (mine_ref, other_ref, dk, dv) = refs[:blocks], refs[blocks:]
        t = pl.program_id(0)

        @pl.when(t == 0)
        def _():
            dk[...] = jnp.zeros_like(dk)
            dv[...] = jnp.zeros_like(dv)

        window = pl.ds(pl.multiple_of(window_block(t, rows) * 64, 64), SPAN)
        own = pl.ds(pl.multiple_of(t * TILE, TILE), TILE)
        low = lax.broadcasted_iota(jnp.int32, (TILE, 2 * HD), 1) < HD
        scale = HD**-0.5
        for side, out_ref in enumerate((mine_ref, other_ref)):
            core = coord[3] if side == 0 else 1 - coord[3]
            for within in range(pairs // 4):
                h = within * 2 * HD
                held = slice(side * quarter + h, side * quarter + h + 2 * HD)

                def lanes(which):
                    return aligned_cols(core * 3 * quarter + which * quarter + h, 2 * HD)

                queries = head_stack(q_ref[:, lanes(0)], low)
                grads = head_stack(g_ref[:, aligned_cols(core * quarter + h, 2 * HD)], low)
                soft = p_ref[0, core * (pairs // 4) + within]
                wide = soft.astype(F32)
                grad_probs = lax.dot_general(
                    joined_rows(windows, lanes(2)), grads, (((1,), (1,)), ((), ())),
                    preferred_element_type=F32,
                )
                inner = jnp.sum(wide * grad_probs, 0, keepdims=True)
                grad_scores = (wide * (grad_probs - inner)).astype(BF)
                dv[window, held] += jnp.dot(soft, grads, preferred_element_type=F32)
                dk[window, held] += jnp.dot(grad_scores, queries, preferred_element_type=F32)
                dq = lax.dot_general(
                    grad_scores, joined_rows(windows, lanes(1)), (((0,), (0,)), ((), ())),
                    preferred_element_type=F32,
                )
                out_ref[own, h : h + 2 * HD] = (
                    jnp.where(low, dq[:TILE], dq[TILE:]) * scale
                ).astype(BF)

        @pl.when(t == tiles - 1)
        def _():
            for side, out_ref in enumerate((mine_ref, other_ref)):
                held = slice(side * quarter, (side + 1) * quarter)
                out_ref[:, quarter : 2 * quarter] = (dk[:, held] * scale).astype(BF)
                out_ref[:, 2 * quarter :] = dv[:, held].astype(BF)

    whole = pl.BlockSpec((rows, 3 * quarter), lambda t: (0, 0))
    return pl.pallas_call(
        kernel,
        grid=(tiles,),
        out_shape=[jax.ShapeDtypeStruct((rows, 3 * quarter), BF)] * 2,
        in_specs=[
            SMEM,
            pl.BlockSpec((TILE, 6 * quarter), lambda t: (t, hh)),
            pl.BlockSpec((1, pairs // 2, SPAN, 2 * TILE), lambda t: (t, hh, 0, 0)),
            pl.BlockSpec((TILE, 2 * quarter), lambda t: (t, hh)),
        ]
        + window_specs(rows, 6 * quarter, hh),
        out_specs=[whole, whole],
        scratch_shapes=[pltpu.VMEM((rows, 2 * quarter), F32)] * 2,
        compiler_params=pltpu.CompilerParams(vmem_limit_bytes=60 << 20),
        cost_estimate=cost(16),
        name="attention_back_" + str(hh),
    )(coords, project, probs, grad, *[project] * blocks)


def update(coords, clip, lows, got, weights, firsts, seconds):
    r, width = weights[1].shape
    hidden = weights[2].shape[1]
    ratio = weights[3].shape[0] // r
    quarter, half = width // 4, width // 2
    steps = max(1, r // 16)
    block = r // steps

    def kernel(coord, clip_ref, *refs):
        halves = refs[0:3], refs[3:6]
        olds = refs[6:18]
        news = refs[18:30]
        scale = clip_ref[0]
        for side in range(2):
            core = coord[3] if side == 0 else 1 - coord[3]
            qkv, rest, down = halves[side]

            def put(i, source, first, cols, col):
                at = aligned_cols(col, cols)
                grad = source[:, first : first + cols].astype(F32) * scale
                found = adam(olds[i][:, at], olds[4 + i][:, at], olds[8 + i][:, at], grad, DECAY, RATE)
                for k in range(3):
                    news[4 * k + i][:, at] = found[k]

            for hh in range(2):
                for t in range(3):
                    put(0, qkv, (hh * 3 + t) * quarter, quarter, t * width + hh * half + core * quarter)
            put(1, rest, hidden // 2, half, core * half)
            put(2, rest, 0, hidden // 2, core * (hidden // 2))
            put(3, down, 0, half, core * half)

    def rows_of(v):
        return pl.BlockSpec((v.shape[0] // steps, v.shape[1]), lambda i: (i, 0))

    arrays = [*weights, *firsts, *seconds]
    return pl.pallas_call(
        kernel,
        grid=(steps,),
        out_shape=[jax.ShapeDtypeStruct(v.shape, F32) for v in arrays],
        in_specs=[SMEM, SMEM] + [rows_of(v) for v in (*lows, *got, *arrays)],
        out_specs=[rows_of(v) for v in arrays],
        compiler_params=pltpu.CompilerParams(vmem_limit_bytes=60 << 20),
        cost_estimate=cost(10),
        name="update",
    )(coords, clip, *lows, *got, *arrays)


def shards(
    tokens, cotangent, segment_ids, group_counts,
    qkv_weight, out_weight, up_weight, down_weight, small_params,
    qkv_first, out_first, up_first, down_first, small_first,
    qkv_second, out_second, up_second, down_second, small_second,
):
    width = tokens.shape[1]
    hidden = up_weight.shape[1]
    rows = tokens.shape[0]
    n = lax.axis_size("fsdp")
    nz, m = dims(n)
    perms = build_perms(n)
    chip = lax.axis_index("fsdp")
    core = lax.axis_index("grp")
    z, y, x = chip // (m * m), chip // m % m, chip % m
    coords = jnp.stack([z, y, x, core]).astype(jnp.int32)
    r = qkv_weight.shape[0]
    ratio = down_weight.shape[0] // r

    counts = group_counts.astype(F32)
    share = counts / jnp.sum(counts)
    is_local = core >= lax.axis_size("grp") // 2
    mine = jnp.where(is_local, share[1], share[0])
    scales = jnp.stack([mine, jnp.where(is_local, share[0], share[1])])
    scale = mine.reshape(1)
    quarter = width // 4
    hq, ho = 3 * width // 2, width // 2

    gather = Gather(perms, nz, m)
    piece = jnp.broadcast_to(small_params.astype(BF).astype(F32), (2 * n,) + small_params.shape)
    small_full = lax.all_to_all(piece, BOTH, 0, 0, tiled=True)[:n].reshape(-1)
    packed, own_one, own_two, own_three = pack(
        coords, qkv_weight, out_weight, up_weight, down_weight, width
    )
    columns = [0, own_one.shape[2], own_one.shape[2] + own_two.shape[2]]
    near_a = gather.first(packed[0])
    pair_one = gather.far_start(own_one)
    near = gather.second(near_a, pair_one)
    near_got = gather.swapped(near)
    far_one = gather.far(pair_one, ())
    pair_two = gather.far_start(after(own_two, near_a))
    pair_three = gather.far_start(after(own_three, near_a))
    small_full = after(small_full, near_a)
    gain_one, bias_one, bias_query, bias_value, bias_out, gain_two, bias_two, bias_up, bias_down = (
        unpack(small_full, width, hidden)
    )
    normed_one = layer_norm(after(tokens, near_a).astype(F32), gain_one, bias_one).astype(BF)
    qkv_bias = jnp.stack([bias_query, jnp.zeros_like(bias_query), bias_value])
    qkv_bias = qkv_bias.reshape(3, 2, 2, quarter).transpose(1, 2, 0, 3).reshape(-1)
    a_one = gather.first(after(far_one, *near[1:]))
    wide_one = gather.second(a_one, normed_one, qkv_bias, pair_two, pair_three)
    far_two = gather.far(pair_two, (far_one,))
    one = gather.sources(0, near, near_got, wide_one, gather.swapped(wide_one, far_two, a_one))

    def exchange(value, *deps):
        return lax.ppermute(after(value, *deps) if deps else value, "grp", SWAP)

    project, qkv_full = project_qkv(coords, one, after(normed_one, far_two), qkv_bias, r, m)
    a_two = gather.first(after(far_two, wide_one[-1]), project)
    wide_two = gather.second(a_two, project)
    seg_col, seg_row = segment_ids.reshape(rows, 1), segment_ids.reshape(1, rows)
    att, probs = attention(after(project, a_two), seg_col, seg_row)
    far_three = gather.far(pair_three, (far_two,), (att,))
    middle, normed_two, out_full = project_out(
        coords, one, after(att, far_three), tokens, bias_out, gain_two, bias_two, r, m, hq
    )
    a_three = gather.first(after(far_three, att), middle)
    wide_three = gather.second(a_three, middle)
    two = gather.sources(columns[1], near, near_got, wide_two, gather.swapped(wide_two, project, att))
    got_att = exchange(att)
    act, slope, up_full = feed_up(coords, two, after(normed_two, a_three), bias_up, r, m)
    swap_three = gather.swapped(wide_three, act)
    three = gather.sources(columns[2], near, near_got, wide_three, swap_three)

    got_one = exchange(normed_one, act)
    got_two = exchange(normed_two, act)
    own, other = weight_grad(
        coords, scale, [(after(act, got_att, *wide_three[1:]), cotangent)], nz, m, "grad_down", 15
    )
    own_got = exchange(other, *swap_three)
    dh_mine, dh_other, grad_bias_up, grad_normed_two, down_full = feed_back(
        coords, three, after(cotangent, other), slope, up_full, r, m, ratio
    )
    grad_bias_up = grad_bias_up.reshape(-1)
    dh_got = exchange(dh_other)
    parts = add_parts(after(own, grad_normed_two), [own_got])
    sum_down = Reduction(parts, perms, nz, m)
    (grad_mid, e_mine, e_other, grad_att, *sums) = middle_back(
        coords, cotangent, middle, after(grad_normed_two, parts[-1]), gain_two, out_full
    )
    grad_gain_two, grad_bias_two, grad_bias_out, grad_bias_down = (v.reshape(-1) for v in sums)
    e_got = exchange(e_other)
    top = outcome(middle, after(act, grad_mid), down_full, bias_down, None, 0, 2)
    done = sum_down.step(top)
    parts = weight_grad_both(
        coords,
        scales,
        [
            (normed_two, got_two, [(after(dh_mine, done), dh_got)]),
            (att, got_att, [(e_mine, e_got)]),
        ],
        nz, m, "grad_up_out", 17,
    )
    done = sum_down.step(parts[0])
    sum_up = Reduction([parts[0]] + [after(part, done) for part in parts[1:]], perms, nz, m)
    mine_one, other_one = attention_back(coords, project, probs, after(grad_att, done), 0)
    one_got = exchange(other_one)
    mine_two, other_two = attention_back(coords, project, probs, after(grad_att, mine_one, sum_down.got[0]), 1)
    two_got = exchange(other_two)
    done = sum_up.step(mine_two)
    parts = weight_grad_both(
        coords,
        scales,
        [(normed_one, got_one, [(after(mine_one, done), one_got), (mine_two, two_got)])],
        nz, m, "grad_qkv", 14,
    )
    done = sum_up.step(parts[0], sum_down.got[1])
    sum_one = Reduction([parts[0]] + [after(part, done) for part in parts[1:]], perms, nz, m)

    tokens_grad, *sums = input_back(coords, tokens, grad_mid, [mine_one, other_one, mine_two, other_two], after(qkv_full, done), gain_one)
    done = sum_one.step(tokens_grad, sum_up.got[0], *sum_down.got[2:])
    sums = after_all(sums, done)
    grad_gain_one, grad_bias_one = sums[0].reshape(-1), sums[1].reshape(-1)
    sums = sums[2].reshape(2, 2, 3, quarter)
    sums = jnp.where(core == 0, sums, sums[:, ::-1]).transpose(2, 0, 1, 3)
    grad_bias_query = sums[0].reshape(-1)
    grad_bias_value = sums[2].reshape(-1)

    grad_small = jnp.concatenate(
        [
            grad_gain_one, grad_bias_one, grad_bias_query, grad_bias_value, grad_bias_out,
            grad_gain_two, grad_bias_two, grad_bias_up, grad_bias_down,
        ]
    )
    grad_small = mine * grad_small.reshape(n, -1)

    low = outcome(middle, after(act, done), down_full, bias_down, top, 1, 2)
    done = sum_one.step(low)
    grad_small = lax.all_to_all(
        after(jnp.concatenate([grad_small, grad_small]), done, sum_one.got[0]), BOTH, 0, 0, tiled=True
    )
    half_up = sum_up.step(done)
    half_down = sum_down.step(done)
    block_output = low
    half_qkv = sum_one.step(half_up, half_down)
    merged_small = jnp.sum(after(grad_small, half_qkv), 0)
    hu = hidden // 2

    lows = [piece.astype(BF) for piece in (half_qkv, half_up, half_down)]
    small_sq = jnp.where(core == 0, jnp.sum(merged_small * merged_small), 0.0)
    local_sq = sum((jnp.sum(jnp.square(piece.astype(F32))) for piece in lows)) + small_sq
    everyone = 2 * n
    shared = lax.all_to_all(jnp.full((everyone, 128), local_sq, F32), BOTH, 0, 0, tiled=True)
    total_sq = jnp.sum(shared[:, 0])
    got = [lax.ppermute(low, "grp", SWAP) for low in lows]
    clip = jnp.minimum(1.0, CLIP * lax.rsqrt(total_sq))
    news = update(
        coords,
        clip.reshape(1),
        lows,
        got,
        (qkv_weight, out_weight, up_weight, down_weight),
        (qkv_first, out_first, up_first, down_first),
        (qkv_second, out_second, up_second, down_second),
    )
    small = adam(small_params, small_first, small_second, merged_small * clip, 0.0, RATE_SMALL)
    return (
        block_output,
        tokens_grad,
        *news[0:4],
        small[0],
        *news[4:8],
        small[1],
        *news[8:12],
        small[2],
        total_sq,
    )


def solution(mesh):
    token, flat, row, vec = P(BOTH, None), P(BOTH), P("fsdp", None), P("fsdp")
    params = (row, row, row, row, vec)
    return jax.shard_map(
        shards,
        mesh=mesh,
        in_specs=(token, token, flat, P()) + params * 3,
        out_specs=(token, token) + params * 3 + (P(),),
        check_vma=False,
    )
```

```python
import math

import jax
import jax.numpy as jnp
from jax import lax
from jax.experimental import pallas as pl
from jax.experimental.pallas import tpu as pltpu
from jax.sharding import PartitionSpec as P

HD = 64
STEP = 10
EPS_NORM = 1e-06
CLIP = 1.0
RATE = 0.04
RATE_SMALL = 0.25
DECAY = 0.05
BETA_ONE = 0.9
BETA_TWO = 0.999
EPS_ADAM = 1e-08
F32 = jnp.float32
BF = jnp.bfloat16
BOTH = ("grp", "fsdp")
SWAP = [(0, 1), (1, 0)]
ANY = pl.BlockSpec(memory_space=pl.ANY)
SMEM = pl.BlockSpec(memory_space=pltpu.SMEM)
TILE = 128

RATIO = 0.1


def cost(us):
    return pl.CostEstimate(flops=int(us * RATIO * 1e9), bytes_accessed=0, transcendentals=0)


VMEM = pl.BlockSpec(memory_space=pltpu.VMEM)
SPAN = 256


def dims(n):
    m = max(1, math.isqrt(n // 4))
    return n // (m * m), m


def build_perms(n):
    nz, m = dims(n)

    def chip(z, y, x):
        return (z % nz) * m * m + (y % m) * m + x % m

    def build(move):
        return [
            (c * n + chip(z, y, x), c * n + chip(*move(c, z, y, x)))
            for c in range(2)
            for z in range(nz)
            for y in range(m)
            for x in range(m)
        ]

    return {
        "z": [build(lambda c, z, y, x: (z + k, y, x)) for k in range(nz)],
        "zx": [build(lambda c, z, y, x: (z ^ k, y, x)) for k in range(nz)],
        "a": [build(lambda c, z, y, x: (z, y, x + k) if c == 0 else (z, y + k, x)) for k in range(m)],
        "b": [build(lambda c, z, y, x: (z, y + k, x) if c == 0 else (z, y, x + k)) for k in range(m)],
        "x": [build(lambda c, z, y, x: (z, y, x + k)) for k in range(m)],
        "y": [build(lambda c, z, y, x: (z, y + k, x)) for k in range(m)],
    }


def send(value, table):
    return lax.ppermute(value, BOTH, table)


def layer_norm(x, gain, bias):
    mean = jnp.mean(x, -1, keepdims=True)
    centred = x - mean
    var = jnp.mean(centred * centred, -1, keepdims=True)
    return centred * lax.rsqrt(var + EPS_NORM) * gain + bias


def unpack(small, width, hidden):
    pieces = [small[i * width : (i + 1) * width] for i in range(7)]
    return pieces + [small[7 * width : 7 * width + hidden], small[7 * width + hidden :]]


def adam(weight, first, second, grad, decay, rate):
    first = BETA_ONE * first + (1.0 - BETA_ONE) * grad
    second = BETA_TWO * second + (1.0 - BETA_TWO) * grad * grad
    step_size = (
        first / (1.0 - BETA_ONE**STEP) / (jnp.sqrt(second / (1.0 - BETA_TWO**STEP)) + EPS_ADAM)
    )
    return (weight - rate * (step_size + decay * weight), first, second)


def after(value, *deps):
    return lax.optimization_barrier((value, *deps))[0]


def after_all(values, *deps):
    return lax.optimization_barrier((*values, *deps))[: len(values)]


class Gather:
    def __init__(self, perms, nz, m):
        self.perms, self.nz, self.m = perms, nz, m

    def first(self, start, *hold):
        got = [send(start, self.perms["a"][k]) for k in range(1, self.m)]
        return jnp.stack([after(start, *hold) if hold else start] + got)

    def second(self, part, *deps):
        held = after(part, *deps) if deps else part
        return [part] + [send(held, self.perms["b"][k]) for k in range(1, self.m)]

    def swapped(self, parts, *deps):
        deps = deps or [None] * len(parts)
        first, last = deps[0], deps[-1]
        return [
            lax.ppermute(p if dep is None else after(p, dep), "grp", SWAP)
            for p, dep in zip(parts, [first] + [last] * (len(parts) - 1))
        ]

    def far_start(self, own, *hold):
        came = send(own, self.perms["zx"][1])
        return jnp.concatenate([after(own, *hold) if hold else own, came])

    def far(self, got, deps, hold=()):
        step = 2
        while step < self.nz:
            came = send(after(got, *deps), self.perms["zx"][step])
            got = jnp.concatenate([after(got, *hold) if hold else got, came])
            step *= 2
        return got[1:]

    def sources(self, column, near, near_got, wide, wide_got):
        found = []
        for side, (close, parts) in enumerate(((near, wide), (near_got, wide_got))):
            for ib in range(self.m):
                found.append((close[ib], column, side, [((ia,), 0, ia, ib) for ia in range(self.m)]))
                pieces = [((ia, k - 1), k, ia, ib) for ia in range(self.m) for k in range(1, self.nz)]
                found.append((parts[ib], 0, side, pieces))
        return found


def start_pieces(refs, coord, sources, r, m, put, sems):
    z, y, x, c = coord[0], coord[1], coord[2], coord[3]
    for side in range(2):
        core = c if side == 0 else 1 - c
        for ref, (_, base, at, pieces) in zip(refs, sources):
            if at != side:
                continue
            for index, dz, ia, ib in pieces:
                px = lax.rem(x - jnp.where(core == 0, ia, ib) + m, m)
                py = lax.rem(y - jnp.where(core == 0, ib, ia) + m, m)
                chip = (jnp.bitwise_xor(z, dz) * m + py) * m + px
                src = ref.at[index]
                for dst, scol, cols in put(chip, core):
                    pltpu.make_async_copy(src.at[:, pl.ds(base + scol, cols)], dst, sems.at[side]).start()


def wait_bytes(ref, sem):
    pltpu.make_async_copy(ref, ref, sem).wait()


def aligned_rows(row, r):
    return pl.ds(pl.multiple_of(row, 16), r)


def aligned_cols(col, cols):
    return pl.ds(pl.multiple_of(col, 128), cols)


def pack(coords, qkv, out, up, down, width):
    r = qkv.shape[0]
    quarter, half, wide = width // 4, width // 2, up.shape[1] // 2
    ratio = down.shape[0] // r
    groups = [6 * quarter + half, wide, ratio * half]

    def kernel(coord, q_ref, o_ref, u_ref, d_ref, *outs):
        c = coord[3]

        def store(group, col, value):
            low = value.astype(BF)
            cols = low.shape[1]
            at = sum(groups[:group]) + col
            outs[0][0, :, at : at + cols] = low
            at -= groups[0] if group else 0
            outs[2 if group else 1][0, :, at : at + cols] = low

        for hh in range(2):
            for t in range(3):
                cols = aligned_cols(t * width + hh * half + c * quarter, quarter)
                store(0, (hh * 3 + t) * quarter, q_ref[:, cols])
        store(0, 6 * quarter, o_ref[:, aligned_cols(c * half, half)])
        store(1, 0, u_ref[:, aligned_cols(c * wide, wide)])
        for i in range(ratio):
            store(2, i * half, d_ref[i * r : (i + 1) * r, aligned_cols(c * half, half)])

    return pl.pallas_call(
        kernel,
        out_shape=[jax.ShapeDtypeStruct((1, r, cols), BF)
            for cols in (sum(groups), groups[0], groups[1] + groups[2])
        ],
        in_specs=[SMEM] + [VMEM] * 4,
        out_specs=[VMEM] * 3,
        compiler_params=pltpu.CompilerParams(vmem_limit_bytes=60 << 20),
        cost_estimate=cost(4),
        name="pack",
    )(coords, qkv, out, up, down)


def project_qkv(coords, sources, normed, bias, r, m):
    rows, width = normed.shape
    part = 3 * width // 4

    def kernel(coord, a_ref, b_ref, *refs):
        out_ref, w_out, w_ref, sems, osem = refs[-5:]

        def put(chip, core):
            return [
                (w_ref.at[core, hh, aligned_rows(chip * r, r), :], hh * part, part) for hh in range(2)
            ]

        start_pieces(refs, coord, sources, r, m, put, sems)
        for side in range(2):
            core = coord[3] if side == 0 else 1 - coord[3]
            wait_bytes(w_ref.at[0], sems.at[side])
            for hh in range(2):
                cols = aligned_cols(hh * 2 * part + core * part, part)
                pltpu.make_async_copy(w_ref.at[core, hh], w_out.at[:, cols], osem).start()
                for i in range(0, rows, 256):
                    out = jnp.dot(a_ref[i : i + 256, :], w_ref[core, hh], preferred_element_type=F32)
                    out_ref[i : i + 256, cols] = (out + b_ref[:, cols]).astype(BF)
        wait_bytes(w_ref, osem)

    return pl.pallas_call(
        kernel,
        out_shape=[
            jax.ShapeDtypeStruct((rows, 3 * width), BF),
            jax.ShapeDtypeStruct((width, 3 * width), BF),
        ],
        in_specs=[SMEM, VMEM, VMEM] + [ANY] * len(sources),
        out_specs=[VMEM, ANY],
        scratch_shapes=[
            pltpu.VMEM((2, 2, width, part), BF),
            pltpu.SemaphoreType.DMA((2,)),
            pltpu.SemaphoreType.DMA,
        ],
        compiler_params=pltpu.CompilerParams(vmem_limit_bytes=60 << 20),
        cost_estimate=cost(10),
        name="project_qkv",
    )(coords, normed, bias.reshape(1, -1), *[source[0] for source in sources])


def project_out(coords, sources, att, tokens, bias, gain_two, bias_two, r, m, first):
    rows, width = att.shape
    half = width // 2

    def kernel(coord, a_ref, t_ref, b_ref, g_ref, c_ref, *refs):
        mid_ref, norm_ref, w_ref, sems = refs[-4:]

        def put(chip, core):
            return [(w_ref.at[aligned_rows(chip * r, r), aligned_cols(core * half, half)], first, half)]

        start_pieces(refs, coord, sources, r, m, put, sems)
        for side in range(2):
            wait_bytes(w_ref.at[:, pl.ds(0, half)], sems.at[side])
        for i in range(0, rows, 128):
            part = slice(i, i + 128)
            mid = (
                t_ref[part, :].astype(F32)
                + jnp.dot(a_ref[part, :], w_ref[...], preferred_element_type=F32)
                + b_ref[...]
            )
            mid_ref[part, :] = mid
            norm_ref[part, :] = layer_norm(mid, g_ref[...], c_ref[...]).astype(BF)

    vmem = pl.BlockSpec(memory_space=pltpu.VMEM)
    return pl.pallas_call(
        kernel,
        out_shape=[
            jax.ShapeDtypeStruct((rows, width), F32),
            jax.ShapeDtypeStruct((rows, width), BF),
            jax.ShapeDtypeStruct((width, width), BF),
        ],
        in_specs=[SMEM] + [vmem] * 5 + [ANY] * len(sources),
        out_specs=[vmem] * 3,
        scratch_shapes=[pltpu.SemaphoreType.DMA((2,))],
        compiler_params=pltpu.CompilerParams(vmem_limit_bytes=60 << 20),
        cost_estimate=cost(8),
        name="project_out",
    )(
        coords, att, tokens, bias.reshape(1, -1), gain_two.reshape(1, -1), bias_two.reshape(1, -1),
        *[source[0] for source in sources],
    )


def weight_grad(coords, scale, pairs, nz, m, name, us):
    tokens, total = pairs[0][0].shape
    halves = [right.shape[1] // 2 for _, right in pairs]
    cols = sum(halves)
    r = total // (nz * m * m)
    zrows = total // nz
    mt = min(1024, zrows)
    mc = zrows // mt
    count = len(pairs)

    def kernel(coord, scale_ref, *refs):
        x_hbm = refs[0 : 2 * count : 2]
        y_hbm = refs[1 : 2 * count : 2]
        outs = refs[2 * count : 2 * count + 2]
        scratch = refs[2 * count + 2 :]
        xv = scratch[0:count]
        yv = scratch[count : 2 * count]
        acc, xsem, ysem, osem = scratch[2 * count :]
        z, y, x, c = coord[0], coord[1], coord[2], coord[3]
        weight = scale_ref[0]

        def xcopy(p, dz, i):
            pz = lax.rem(z + dz, nz)
            return pltpu.make_async_copy(
                x_hbm[p].at[:, pl.ds(pl.multiple_of(pz * zrows + i * mt, 128), mt)],
                xv[p].at[dz * mc + i],
                xsem.at[p, dz * mc + i],
            )

        def ycopy(p, side):
            owner = c if side == 0 else 1 - c
            return pltpu.make_async_copy(
                y_hbm[p].at[:, pl.ds(pl.multiple_of(owner * halves[p], 128), halves[p])],
                yv[p].at[:, aligned_cols(owner * halves[p], halves[p])],
                ysem.at[p, side],
            )

        for p in range(count):
            xcopy(p, 0, 0).start()
            ycopy(p, 1).start()
            ycopy(p, 0).start()
        for p in range(count):
            for dz in range(nz):
                for i in range(mc):
                    if dz or i:
                        xcopy(p, dz, i).start()
        copies = []
        for dz in range(nz):
            for i in range(mc):
                for p in range(count):
                    low = sum(halves[:p])
                    xcopy(p, dz, i).wait()
                    left = xv[p][dz * mc + i].T
                    if dz == 0 and i == 0:
                        ycopy(p, 1).wait()
                        ycopy(p, 0).wait()
                    both = jnp.dot(left, yv[p][...], preferred_element_type=F32) * weight
                    acc[dz, i * mt : (i + 1) * mt, :] = both.astype(BF)
            for side in (1, 0):
                owner = c if side == 0 else 1 - c
                for ib in range(m):
                    for ia in range(m):
                        dx = jnp.where(owner == 0, ia, ib)
                        dy = jnp.where(owner == 0, ib, ia)
                        px = lax.rem(x + dx, m)
                        py = lax.rem(y + dy, m)
                        copy = pltpu.make_async_copy(
                            acc.at[dz, aligned_rows((py * m + px) * r, r), aligned_cols(owner * cols, cols)],
                            outs[side].at[ib, ia, dz],
                            osem.at[side, dz, ib * m + ia],
                        )
                        copy.start()
                        copies.append(copy)
        for copy in copies:
            copy.wait()

    return pl.pallas_call(
        kernel,
        out_shape=[jax.ShapeDtypeStruct((m, m, nz, r, cols), BF)] * 2,
        in_specs=[SMEM, SMEM] + [ANY] * (2 * count),
        out_specs=[ANY] * 2,
        scratch_shapes=[pltpu.VMEM((nz * mc, tokens, mt), BF) for _ in pairs]
        + [pltpu.VMEM((tokens, 2 * h), BF) for h in halves]
        + [
            pltpu.VMEM((nz, zrows, 2 * cols), BF),
            pltpu.SemaphoreType.DMA((count, nz * mc)),
            pltpu.SemaphoreType.DMA((count, 2)),
            pltpu.SemaphoreType.DMA((2, nz, m * m)),
        ],
        compiler_params=pltpu.CompilerParams(vmem_limit_bytes=60 << 20),
        cost_estimate=cost(us),
        name=name,
    )(coords, scale, *[v for pair in pairs for v in pair])


def weight_grad_both(coords, scales, pairs, nz, m, name, us):
    tokens, total = pairs[0][0].shape
    widths = [[own.shape[1] for own, _ in pair[2]] for pair in pairs]
    halves = [sum(w) for w in widths]
    cols = sum(halves)
    r = total // (nz * m * m)
    zrows = total // nz
    count = len(pairs)
    group = 2 if nz % 2 == 0 else 1
    operands, places = [], []
    for pair in pairs:
        places.append(len(operands))
        operands += [*pair[:2], *[v for both in pair[2] for v in both]]

    def kernel(coord, scale_ref, *refs):
        ins = refs[: len(operands)]
        outs = refs[len(operands) : len(operands) + m]
        scratch = refs[len(operands) + m :]
        held = scratch[: 4 * count]
        acc, xsem, ysem, osem = scratch[4 * count :]
        z, y, x, c = coord[0], coord[1], coord[2], coord[3]

        def xcopy(p, who, dz):
            pz = lax.rem(z + dz, nz)
            return pltpu.make_async_copy(
                ins[places[p] + who].at[:, pl.ds(pl.multiple_of(pz * zrows, 128), zrows)],
                held[4 * p + who].at[dz],
                xsem.at[p, who, dz],
            )

        def ycopies(p, who):
            dst = held[4 * p + 2 + who]
            found = []
            for k, h in enumerate(widths[p]):
                at = pl.ds(sum(widths[p][:k]), h)
                src = ins[places[p] + 2 + 2 * k + who]
                found.append(pltpu.make_async_copy(src, dst.at[:, at], ysem.at[p, who, k]))
            return found

        for p in range(count):
            for who in range(2):
                xcopy(p, who, 0).start()
                for copy in ycopies(p, who):
                    copy.start()
        for p in range(count):
            for dz in range(1, nz):
                for who in range(2):
                    xcopy(p, who, dz).start()
        copies = []
        for dz in range(nz):
            for p in range(count):
                low = sum(halves[:p])
                if dz % group:
                    continue
                out = None
                for who in range(2):
                    for k in range(group):
                        xcopy(p, who, dz + k).wait()
                    if dz == 0:
                        for copy in ycopies(p, who):
                            copy.wait()
                    left = jnp.concatenate([held[4 * p + who][dz + k].T for k in range(group)], 0)
                    part = jnp.dot(left, held[4 * p + 2 + who][...], preferred_element_type=F32)
                    part = part * scale_ref[who]
                    out = part if out is None else out + part
                out = out.astype(BF)
                for k in range(group):
                    acc[dz + k, :, low : low + halves[p]] = out[k * zrows : (k + 1) * zrows]
            for ib in range(m):
                for ia in range(m):
                    px = lax.rem(x + jnp.where(c == 0, ia, ib), m)
                    py = lax.rem(y + jnp.where(c == 0, ib, ia), m)
                    copy = pltpu.make_async_copy(
                        acc.at[dz, aligned_rows((py * m + px) * r, r), :],
                        outs[ib].at[ia, dz],
                        osem.at[dz, ib * m + ia],
                    )
                    copy.start()
                    copies.append(copy)
        for copy in copies:
            copy.wait()

    shapes = []
    for h in halves:
        shapes += [pltpu.VMEM((nz, tokens, zrows), BF)] * 2 + [pltpu.VMEM((tokens, h), BF)] * 2
    return pl.pallas_call(
        kernel,
        out_shape=[jax.ShapeDtypeStruct((m, nz, r, cols), BF)] * m,
        in_specs=[SMEM, SMEM] + [ANY] * len(operands),
        out_specs=[ANY] * m,
        scratch_shapes=shapes
        + [
            pltpu.VMEM((nz, zrows, cols), BF),
            pltpu.SemaphoreType.DMA((count, 2, nz)),
            pltpu.SemaphoreType.DMA((count, 2, max(len(w) for w in widths))),
            pltpu.SemaphoreType.DMA((nz, m * m)),
        ],
        compiler_params=pltpu.CompilerParams(vmem_limit_bytes=60 << 20),
        cost_estimate=cost(us),
        name=name,
    )(coords, scales, *operands)


def add_parts(keep, got):
    size, cols = keep.shape[0], keep.shape[-1]
    shape = keep.shape[1:]
    flat = math.prod(shape[:-1])
    block = max(16, min(flat, (1 << 19) // (size * cols) // 16 * 16))
    while flat % block:
        block -= 16
    count = len(got) + 1

    def kernel(*refs):
        for k in range(size):
            total = refs[0][k].astype(F32)
            for ref in refs[1:count]:
                total += ref[k].astype(F32)
            refs[count + k][...] = total.astype(BF)

    outs = pl.pallas_call(
        kernel,
        grid=(flat // block,),
        out_shape=[jax.ShapeDtypeStruct((flat, cols), BF)] * size,
        in_specs=[pl.BlockSpec((size, block, cols), lambda i: (0, i, 0))] * count,
        out_specs=[pl.BlockSpec((block, cols), lambda i: (i, 0))] * size,
        compiler_params=pltpu.CompilerParams(vmem_limit_bytes=60 << 20),
        cost_estimate=cost(2),
        name="add_parts",
    )(*[v.reshape(size, flat, cols) for v in [keep, *got]])
    return [out.reshape(shape) for out in outs]


class Reduction:
    def __init__(self, parts, perms, nz, m):
        self.perms, self.sizes = perms, {"b": m, "a": m, "z": nz}
        self.left = ["a", "z"]
        self.pass_on("b", parts)

    def pass_on(self, axis, parts):
        self.keep = parts[0]
        self.got = [send(parts[k], self.perms[axis][k]) for k in range(1, self.sizes[axis])]

    def step(self, *deps):
        if not self.left:
            t = after(self.keep, *deps).astype(F32) if deps else self.keep.astype(F32)
            for part in self.got:
                t = t + part.astype(F32)
            return t
        axis = self.left.pop(0)
        parts = add_parts(after(self.keep, *deps), self.got)
        self.pass_on(axis, parts)
        return parts[-1]


def feed_up(coords, sources, normed, bias, r, m):
    rows, width = normed.shape
    hidden = bias.shape[0]
    half, cols, step = hidden // 2, 512, 256
    tiles = half // cols

    def kernel(coord, a_ref, b_ref, *refs):
        act_ref, slope_ref, w_out, w_ref, sems, osem = refs[-6:]
        j = pl.program_id(0)

        @pl.when(j == 0)
        def _():
            def put(chip, core):
                return [(w_ref.at[core, aligned_rows(chip * r, r), :], 0, half)]

            start_pieces(refs, coord, sources, r, m, put, sems)

        for side in range(2):

            @pl.when(j == side * tiles)
            def _():
                wait_bytes(w_ref.at[0], sems.at[side])
                core = coord[3] if side == 0 else 1 - coord[3]
                at = aligned_cols(core * half, half)
                pltpu.make_async_copy(w_ref.at[core], w_out.at[:, at], osem).start()

        @pl.when(j == 2 * tiles - 1)
        def _():
            wait_bytes(w_ref, osem)

        core = jnp.where(j < tiles, coord[3], 1 - coord[3])
        weight = w_ref[core, :, aligned_cols(lax.rem(j, tiles) * cols, cols)]
        c0, c1 = math.sqrt(2.0 / math.pi), 0.044715
        for i in range(0, rows, step):
            h = jnp.dot(a_ref[i : i + step, :], weight, preferred_element_type=F32) + b_ref[...]
            square = h * h
            t = jnp.tanh(h * (c0 + (c0 * c1) * square))
            mid = 0.5 * h
            act_ref[i : i + step, :] = (mid + mid * t).astype(BF)
            slope = 0.5 + 0.5 * t + mid * (1.0 - t * t) * (c0 + (3.0 * c0 * c1) * square)
            slope_ref[i : i + step, :] = slope.astype(BF)

    def tile(j, coord):
        return (0, jnp.where(j < tiles, coord[3], 1 - coord[3]) * tiles + lax.rem(j, tiles))

    grid_spec = pltpu.PrefetchScalarGridSpec(
        num_scalar_prefetch=1,
        grid=(2 * tiles,),
        in_specs=[
            pl.BlockSpec((rows, width), lambda j, coord: (0, 0)),
            pl.BlockSpec((1, cols), tile),
        ]
        + [ANY] * len(sources),
        out_specs=[
            pl.BlockSpec((rows, cols), tile),
            pl.BlockSpec((rows, cols), tile),
            ANY,
        ],
        scratch_shapes=[
            pltpu.VMEM((2, width, half), BF),
            pltpu.SemaphoreType.DMA((2,)),
            pltpu.SemaphoreType.DMA,
        ],
    )
    return pl.pallas_call(
        kernel,
        grid_spec=grid_spec,
        out_shape=[
            jax.ShapeDtypeStruct((rows, hidden), BF),
            jax.ShapeDtypeStruct((rows, hidden), BF),
            jax.ShapeDtypeStruct((width, hidden), BF),
        ],
        compiler_params=pltpu.CompilerParams(vmem_limit_bytes=60 << 20),
        cost_estimate=cost(25),
        name="feed_up",
    )(coords, normed, bias.reshape(1, hidden), *[source[0] for source in sources])


def feed_back(coords, sources, grad, slope, up, r, m, ratio):
    rows, width = grad.shape
    hidden = up.shape[1]
    half, cols, step = width // 2, 512, 512
    tiles = hidden // cols

    def tile_at(j, coord):
        core = jnp.where(j < tiles // 2, coord[3], 1 - coord[3])
        return core * (tiles // 2) + lax.rem(j, tiles // 2)

    def kernel(coord, g_ref, s_ref, u_ref, *refs):
        mine_ref, other_ref, sum_ref, out_ref, d_out, d_ref, dh_ref, sems, osems = refs[-9:]
        j = pl.program_id(0)

        @pl.when(j == 0)
        def _():
            out_ref[...] = jnp.zeros_like(out_ref)

            def put(chip, core):
                return [
                    (
                        d_ref.at[
                            aligned_rows((chip * ratio + s) * r, r), aligned_cols(core * half, half)
                        ],
                        s * half,
                        half,
                    )
                    for s in range(ratio)
                ]

            start_pieces(refs, coord, sources, r, m, put, sems)
            for side in range(2):
                wait_bytes(d_ref.at[:, pl.ds(0, half)], sems.at[side])
            pltpu.make_async_copy(d_ref, d_out, osems.at[2]).start()

        slot = lax.rem(j, 2)

        @pl.when(j >= 2)
        def _():
            wait_bytes(dh_ref.at[0], osems.at[slot])

        down = d_ref[pl.ds(pl.multiple_of(tile_at(j, coord) * cols, cols), cols), :]
        total = jnp.zeros((1, cols), F32)
        for i in range(0, rows, step):
            part = lax.dot_general(
                g_ref[i : i + step, :], down, (((1,), (1,)), ((), ())), preferred_element_type=F32
            )
            dh = (part * s_ref[i : i + step, :].astype(F32)).astype(BF)
            dh_ref[slot, i : i + step, :] = dh
            total += jnp.sum(dh.astype(F32), 0, keepdims=True)
            out_ref[i : i + step, :] += lax.dot_general(
                dh, u_ref[...], (((1,), (1,)), ((), ())), preferred_element_type=F32
            )
        sum_ref[...] = total

        def copy_out(ref):
            at = aligned_cols(lax.rem(j, tiles // 2) * cols, cols)
            pltpu.make_async_copy(dh_ref.at[slot], ref.at[:, at], osems.at[slot]).start()

        @pl.when(j < tiles // 2)
        def _():
            copy_out(mine_ref)

        @pl.when(j >= tiles // 2)
        def _():
            copy_out(other_ref)

        @pl.when(j == tiles - 1)
        def _():
            for at in range(2):
                wait_bytes(dh_ref.at[0], osems.at[at])
            wait_bytes(d_ref, osems.at[2])

    grid_spec = pltpu.PrefetchScalarGridSpec(
        num_scalar_prefetch=1,
        grid=(tiles,),
        in_specs=[
            pl.BlockSpec((rows, width), lambda j, coord: (0, 0)),
            pl.BlockSpec((rows, cols), lambda j, coord: (0, tile_at(j, coord))),
            pl.BlockSpec((width, cols), lambda j, coord: (0, tile_at(j, coord))),
        ]
        + [ANY] * len(sources),
        out_specs=[
            ANY,
            ANY,
            pl.BlockSpec((1, cols), lambda j, coord: (0, tile_at(j, coord))),
            pl.BlockSpec((rows, width), lambda j, coord: (0, 0)),
            ANY,
        ],
        scratch_shapes=[
            pltpu.VMEM((hidden, width), BF),
            pltpu.VMEM((2, rows, cols), BF),
            pltpu.SemaphoreType.DMA((2,)),
            pltpu.SemaphoreType.DMA((3,)),
        ],
    )
    return pl.pallas_call(
        kernel,
        grid_spec=grid_spec,
        out_shape=[
            jax.ShapeDtypeStruct((rows, hidden // 2), BF),
            jax.ShapeDtypeStruct((rows, hidden // 2), BF),
            jax.ShapeDtypeStruct((1, hidden), F32),
            jax.ShapeDtypeStruct((rows, width), F32),
            jax.ShapeDtypeStruct((hidden, width), BF),
        ],
        compiler_params=pltpu.CompilerParams(vmem_limit_bytes=60 << 20),
        cost_estimate=cost(50),
        name="feed_back",
    )(coords, grad, slope, up, *[source[0] for source in sources])


def norm_back(x, grad, gain):
    mean = jnp.mean(x, -1, keepdims=True)
    centred = x - mean
    inv = lax.rsqrt(jnp.mean(centred * centred, -1, keepdims=True) + EPS_NORM)
    hat = centred * inv
    inner = grad * gain
    back = inv * (
        inner
        - jnp.mean(inner, -1, keepdims=True)
        - hat * jnp.mean(inner * hat, -1, keepdims=True)
    )
    return back, jnp.sum(grad * hat, 0, keepdims=True), jnp.sum(grad, 0, keepdims=True)


def middle_back(coords, cotangent, middle, grad, gain, out):
    rows, width = middle.shape
    block = min(256, rows)

    half = width // 2

    def kernel(coord, c_ref, m_ref, d_ref, g_ref, w_ref, *refs):
        dy_ref, mine_ref, other_ref, a_ref, gain_ref, bias_ref, bo_ref, bd_ref, e_ref = refs

        @pl.when(pl.program_id(0) == 0)
        def _():
            for ref in (gain_ref, bias_ref, bo_ref, bd_ref):
                ref[...] = jnp.zeros_like(ref)

        cot = c_ref[...].astype(F32)
        back, for_gain, for_bias = norm_back(m_ref[...], d_ref[...], g_ref[...])
        dy = cot + back
        low = dy.astype(BF)
        dy_ref[...] = dy
        e_ref[...] = low
        mine_ref[...] = e_ref[:, aligned_cols(coord[3] * half, half)]
        other_ref[...] = e_ref[:, aligned_cols((1 - coord[3]) * half, half)]
        a_ref[...] = lax.dot_general(
            low, w_ref[...], (((1,), (1,)), ((), ())), preferred_element_type=F32
        ).astype(BF)
        gain_ref[...] += for_gain
        bias_ref[...] += for_bias
        bo_ref[...] += jnp.sum(low.astype(F32), 0, keepdims=True)
        bd_ref[...] += jnp.sum(cot, 0, keepdims=True)

    tile = pl.BlockSpec((block, width), lambda i: (i, 0))
    part = pl.BlockSpec((block, half), lambda i: (i, 0))
    line = pl.BlockSpec((1, width), lambda i: (0, 0))
    return pl.pallas_call(
        kernel,
        grid=(rows // block,),
        out_shape=[
            jax.ShapeDtypeStruct((rows, cols), t)
            for cols, t in ((width, F32), (half, BF), (half, BF), (width, BF))
        ]
        + [jax.ShapeDtypeStruct((1, width), F32)] * 4,
        in_specs=[SMEM, tile, tile, tile, line, pl.BlockSpec((width, width), lambda i: (0, 0))],
        out_specs=[tile, part, part, tile] + [line] * 4,
        scratch_shapes=[pltpu.VMEM((block, width), BF)],
        compiler_params=pltpu.CompilerParams(vmem_limit_bytes=60 << 20),
        cost_estimate=cost(3),
        name="middle_back",
    )(coords, cotangent, middle, grad, gain.reshape(1, -1), out)


def input_back(coords, tokens, grad_mid, parts, weight, gain):
    rows, width = tokens.shape
    total = weight.shape[1]
    block = min(256, rows)
    count = len(parts)
    cols = total // count

    def kernel(coord, t_ref, m_ref, w_ref, g_ref, *refs):
        out_ref, gain_ref, bias_ref, sum_ref = refs[count:]

        @pl.when(pl.program_id(0) == 0)
        def _():
            for ref in (gain_ref, bias_ref, sum_ref):
                ref[...] = jnp.zeros_like(ref)

        grad = jnp.zeros((block, width), F32)
        for p in range(count):
            core = coord[3] if p % 2 == 0 else 1 - coord[3]
            part = refs[p][...]
            sum_ref[:, p * cols : (p + 1) * cols] += jnp.sum(part.astype(F32), 0, keepdims=True)
            weight_at = aligned_cols((p // 2 * 2 + core) * cols, cols)
            grad += lax.dot_general(
                part, w_ref[:, weight_at], (((1,), (1,)), ((), ())), preferred_element_type=F32
            )
        back, for_gain, for_bias = norm_back(t_ref[...].astype(F32), grad, g_ref[...])
        out_ref[...] = (m_ref[...] + back).astype(BF)
        gain_ref[...] += for_gain
        bias_ref[...] += for_bias

    tile = pl.BlockSpec((block, width), lambda i: (i, 0))
    line = pl.BlockSpec((1, width), lambda i: (0, 0))
    return pl.pallas_call(
        kernel,
        grid=(rows // block,),
        out_shape=[
            jax.ShapeDtypeStruct((rows, width), BF),
            jax.ShapeDtypeStruct((1, width), F32),
            jax.ShapeDtypeStruct((1, width), F32),
            jax.ShapeDtypeStruct((1, total), F32),
        ],
        in_specs=[SMEM, tile, tile, pl.BlockSpec((width, total), lambda i: (0, 0)), line]
        + [pl.BlockSpec((block, cols), lambda i: (i, 0))] * count,
        out_specs=[tile, line, line, pl.BlockSpec((1, total), lambda i: (0, 0))],
        compiler_params=pltpu.CompilerParams(vmem_limit_bytes=60 << 20),
        cost_estimate=cost(30),
        name="input_back",
    )(coords, tokens, grad_mid, weight, gain.reshape(1, -1), *parts)


def outcome(middle, act, down, bias, before, part, parts):
    rows, width = middle.shape
    hidden = act.shape[1]
    block = 128
    first = part * (rows // parts // block)

    def kernel(m_ref, a_ref, d_ref, b_ref, *refs):
        out = jnp.dot(a_ref[...], d_ref[...], preferred_element_type=F32)
        refs[-1][...] = (m_ref[...] + out + b_ref[...]).astype(BF)

    more = [] if before is None else [before]
    return pl.pallas_call(
        kernel,
        grid=(rows // parts // block,),
        out_shape=jax.ShapeDtypeStruct((rows, width), BF),
        in_specs=[
            pl.BlockSpec((block, width), lambda i: (first + i, 0)),
            pl.BlockSpec((block, hidden), lambda i: (first + i, 0)),
            pl.BlockSpec((hidden, width), lambda i: (0, 0)),
            pl.BlockSpec((1, width), lambda i: (0, 0)),
        ]
        + [ANY] * len(more),
        out_specs=pl.BlockSpec((block, width), lambda i: (first + i, 0)),
        input_output_aliases={4: 0} if more else {},
        compiler_params=pltpu.CompilerParams(vmem_limit_bytes=60 << 20),
        cost_estimate=cost(3 if part == 0 else 10),
        name="outcome_" + str(part),
    )(middle, act, down, bias.reshape(1, -1), *more)


def head_stack(block, low_lanes):
    zero = jnp.zeros_like(block)
    return jnp.concatenate(
        [jnp.where(low_lanes, block, zero), jnp.where(low_lanes, zero, block)], 0
    )


def window_block(t, rows):
    return jnp.clip(2 * t - 1, 0, rows // 64 - SPAN // 64)


def window_specs(rows, cols, at=0):
    return [
        pl.BlockSpec((64, cols), lambda t, i=i: (window_block(t, rows) + i, at)) for i in range(SPAN // 64)
    ]


def joined_rows(refs, lanes):
    return jnp.concatenate([ref[:, lanes] for ref in refs], 0)


def attention(project, seg_col, seg_row):
    rows, width = project.shape[0], project.shape[1] // 3
    pairs = width // (2 * HD)
    blocks = SPAN // 64

    def pair_lanes(pair, which):
        hh, rest = divmod(pair, pairs // 2)
        core, within = divmod(rest, pairs // 4)
        quarter = width // 4
        first = (hh * 2 + core) * 3 * quarter + which * quarter + within * 2 * HD
        return slice(first, first + 2 * HD)

    def kernel(row_ref, q_ref, *refs):
        cols, windows, (out_ref, probs_ref) = refs[:blocks], refs[blocks : 2 * blocks], refs[2 * blocks :]
        same = joined_rows(cols, slice(0, 1)) == row_ref[...]
        same = jnp.concatenate([same, same], 1)
        low = lax.broadcasted_iota(jnp.int32, (TILE, 2 * HD), 1) < HD
        for h in range(pairs):
            stack = head_stack(q_ref[:, pair_lanes(h, 0)] * HD**-0.5, low)
            keys = joined_rows(windows, pair_lanes(h, 1))
            scores = lax.dot_general(keys, stack, (((1,), (1,)), ((), ())), preferred_element_type=F32)
            scores = jnp.where(same, scores, -1e30)
            expo = jnp.exp(scores - jnp.max(scores, 0, keepdims=True))
            probs = (expo * (1.0 / jnp.sum(expo, 0, keepdims=True))).astype(BF)
            probs_ref[0, h] = probs
            mixed = lax.dot_general(
                probs,
                joined_rows(windows, pair_lanes(h, 2)),
                (((0,), (0,)), ((), ())),
                preferred_element_type=F32,
            )
            out_ref[:, h * 2 * HD : (h + 1) * 2 * HD] = jnp.where(low, mixed[:TILE], mixed[TILE:]).astype(BF)

    return pl.pallas_call(
        kernel,
        grid=(rows // TILE,),
        out_shape=[
            jax.ShapeDtypeStruct((rows, width), BF),
            jax.ShapeDtypeStruct((rows // TILE, pairs, SPAN, 2 * TILE), BF),
        ],
        in_specs=[
            pl.BlockSpec((1, TILE), lambda t: (0, t)),
            pl.BlockSpec((TILE, 3 * width), lambda t: (t, 0)),
        ]
        + window_specs(rows, 1)
        + window_specs(rows, 3 * width),
        out_specs=[
            pl.BlockSpec((TILE, width), lambda t: (t, 0)),
            pl.BlockSpec((1, pairs, SPAN, 2 * TILE), lambda t: (t, 0, 0, 0)),
        ],
        compiler_params=pltpu.CompilerParams(vmem_limit_bytes=60 << 20),
        cost_estimate=cost(14),
        name="attention",
    )(seg_row, project, *[seg_col] * blocks, *[project] * blocks)


def attention_back(coords, project, probs, grad, hh):
    rows, width = project.shape[0], project.shape[1] // 3
    quarter = width // 4
    pairs = width // (2 * HD)
    tiles = rows // TILE
    blocks = SPAN // 64

    def kernel(coord, q_ref, p_ref, g_ref, *refs):
        windows, (mine_ref, other_ref, dk, dv) = refs[:blocks], refs[blocks:]
        t = pl.program_id(0)

        @pl.when(t == 0)
        def _():
            dk[...] = jnp.zeros_like(dk)
            dv[...] = jnp.zeros_like(dv)

        window = pl.ds(pl.multiple_of(window_block(t, rows) * 64, 64), SPAN)
        own = pl.ds(pl.multiple_of(t * TILE, TILE), TILE)
        low = lax.broadcasted_iota(jnp.int32, (TILE, 2 * HD), 1) < HD
        scale = HD**-0.5
        for side, out_ref in enumerate((mine_ref, other_ref)):
            core = coord[3] if side == 0 else 1 - coord[3]
            for within in range(pairs // 4):
                h = within * 2 * HD
                held = slice(side * quarter + h, side * quarter + h + 2 * HD)

                def lanes(which):
                    return aligned_cols(core * 3 * quarter + which * quarter + h, 2 * HD)

                queries = head_stack(q_ref[:, lanes(0)], low)
                grads = head_stack(g_ref[:, aligned_cols(core * quarter + h, 2 * HD)], low)
                soft = p_ref[0, core * (pairs // 4) + within]
                wide = soft.astype(F32)
                grad_probs = lax.dot_general(
                    joined_rows(windows, lanes(2)), grads, (((1,), (1,)), ((), ())),
                    preferred_element_type=F32,
                )
                inner = jnp.sum(wide * grad_probs, 0, keepdims=True)
                grad_scores = (wide * (grad_probs - inner)).astype(BF)
                dv[window, held] += jnp.dot(soft, grads, preferred_element_type=F32)
                dk[window, held] += jnp.dot(grad_scores, queries, preferred_element_type=F32)
                dq = lax.dot_general(
                    grad_scores, joined_rows(windows, lanes(1)), (((0,), (0,)), ((), ())),
                    preferred_element_type=F32,
                )
                out_ref[own, h : h + 2 * HD] = (
                    jnp.where(low, dq[:TILE], dq[TILE:]) * scale
                ).astype(BF)

        @pl.when(t == tiles - 1)
        def _():
            for side, out_ref in enumerate((mine_ref, other_ref)):
                held = slice(side * quarter, (side + 1) * quarter)
                out_ref[:, quarter : 2 * quarter] = (dk[:, held] * scale).astype(BF)
                out_ref[:, 2 * quarter :] = dv[:, held].astype(BF)

    whole = pl.BlockSpec((rows, 3 * quarter), lambda t: (0, 0))
    return pl.pallas_call(
        kernel,
        grid=(tiles,),
        out_shape=[jax.ShapeDtypeStruct((rows, 3 * quarter), BF)] * 2,
        in_specs=[
            SMEM,
            pl.BlockSpec((TILE, 6 * quarter), lambda t: (t, hh)),
            pl.BlockSpec((1, pairs // 2, SPAN, 2 * TILE), lambda t: (t, hh, 0, 0)),
            pl.BlockSpec((TILE, 2 * quarter), lambda t: (t, hh)),
        ]
        + window_specs(rows, 6 * quarter, hh),
        out_specs=[whole, whole],
        scratch_shapes=[pltpu.VMEM((rows, 2 * quarter), F32)] * 2,
        compiler_params=pltpu.CompilerParams(vmem_limit_bytes=60 << 20),
        cost_estimate=cost(16),
        name="attention_back_" + str(hh),
    )(coords, project, probs, grad, *[project] * blocks)


def update(coords, clip, lows, got, weights, firsts, seconds):
    r, width = weights[1].shape
    hidden = weights[2].shape[1]
    ratio = weights[3].shape[0] // r
    quarter, half = width // 4, width // 2
    steps = max(1, r // 16)
    block = r // steps

    def kernel(coord, clip_ref, *refs):
        halves = refs[0:3], refs[3:6]
        olds = refs[6:18]
        news = refs[18:30]
        scale = clip_ref[0]
        for side in range(2):
            core = coord[3] if side == 0 else 1 - coord[3]
            qkv, rest, down = halves[side]

            def put(i, source, first, cols, col):
                at = aligned_cols(col, cols)
                grad = source[:, first : first + cols].astype(F32) * scale
                found = adam(olds[i][:, at], olds[4 + i][:, at], olds[8 + i][:, at], grad, DECAY, RATE)
                for k in range(3):
                    news[4 * k + i][:, at] = found[k]

            for hh in range(2):
                for t in range(3):
                    put(0, qkv, (hh * 3 + t) * quarter, quarter, t * width + hh * half + core * quarter)
            put(1, rest, hidden // 2, half, core * half)
            put(2, rest, 0, hidden // 2, core * (hidden // 2))
            put(3, down, 0, half, core * half)

    def rows_of(v):
        return pl.BlockSpec((v.shape[0] // steps, v.shape[1]), lambda i: (i, 0))

    arrays = [*weights, *firsts, *seconds]
    return pl.pallas_call(
        kernel,
        grid=(steps,),
        out_shape=[jax.ShapeDtypeStruct(v.shape, F32) for v in arrays],
        in_specs=[SMEM, SMEM] + [rows_of(v) for v in (*lows, *got, *arrays)],
        out_specs=[rows_of(v) for v in arrays],
        compiler_params=pltpu.CompilerParams(vmem_limit_bytes=60 << 20),
        cost_estimate=cost(10),
        name="update",
    )(coords, clip, *lows, *got, *arrays)


def shards(
    tokens, cotangent, segment_ids, group_counts,
    qkv_weight, out_weight, up_weight, down_weight, small_params,
    qkv_first, out_first, up_first, down_first, small_first,
    qkv_second, out_second, up_second, down_second, small_second,
):
    width = tokens.shape[1]
    hidden = up_weight.shape[1]
    rows = tokens.shape[0]
    n = lax.axis_size("fsdp")
    nz, m = dims(n)
    perms = build_perms(n)
    chip = lax.axis_index("fsdp")
    core = lax.axis_index("grp")
    z, y, x = chip // (m * m), chip // m % m, chip % m
    coords = jnp.stack([z, y, x, core]).astype(jnp.int32)
    r = qkv_weight.shape[0]
    ratio = down_weight.shape[0] // r

    counts = group_counts.astype(F32)
    share = counts / jnp.sum(counts)
    is_local = core >= lax.axis_size("grp") // 2
    mine = jnp.where(is_local, share[1], share[0])
    scales = jnp.stack([mine, jnp.where(is_local, share[0], share[1])])
    scale = mine.reshape(1)
    quarter = width // 4
    hq, ho = 3 * width // 2, width // 2

    gather = Gather(perms, nz, m)
    piece = jnp.broadcast_to(small_params.astype(BF).astype(F32), (2 * n,) + small_params.shape)
    small_full = lax.all_to_all(piece, BOTH, 0, 0, tiled=True)[:n].reshape(-1)
    packed, own_one, own_rest = pack(
        coords, qkv_weight, out_weight, up_weight, down_weight, width
    )
    columns = [0, own_one.shape[2], own_one.shape[2] + hidden // 2]
    near_a = gather.first(packed[0])
    pair_one = gather.far_start(own_one)
    near = gather.second(near_a, pair_one)
    near_got = gather.swapped(near)
    far_one = gather.far(pair_one, (), (small_full,))
    small_full = after(small_full, *near[1:])
    gain_one, bias_one, bias_query, bias_value, bias_out, gain_two, bias_two, bias_up, bias_down = (
        unpack(small_full, width, hidden)
    )
    normed_one = layer_norm(after(tokens, *near[1:]).astype(F32), gain_one, bias_one).astype(BF)
    qkv_bias = jnp.stack([bias_query, jnp.zeros_like(bias_query), bias_value])
    qkv_bias = qkv_bias.reshape(3, 2, 2, quarter).transpose(1, 2, 0, 3).reshape(-1)
    a_one = gather.first(after(far_one, *near[1:]))
    pair_rest = gather.far_start(after(own_rest, near_a), a_one)
    pair_two, pair_three = pair_rest[:, :, : hidden // 2], pair_rest[:, :, hidden // 2 :]
    wide_one = gather.second(a_one, normed_one, qkv_bias, pair_rest)
    far_two = gather.far(pair_two, (far_one,))
    one = gather.sources(0, near, near_got, wide_one, gather.swapped(wide_one, far_two, a_one))

    def exchange(value, *deps):
        return lax.ppermute(after(value, *deps) if deps else value, "grp", SWAP)

    project, qkv_full = project_qkv(coords, one, after(normed_one, far_two), qkv_bias, r, m)
    far_three = gather.far(pair_three, (far_two,), (project,))
    a_two = gather.first(after(far_two, wide_one[-1]), project, far_three)
    wide_two = gather.second(a_two, project)
    seg_col, seg_row = segment_ids.reshape(rows, 1), segment_ids.reshape(1, rows)
    att, probs = attention(after(project, a_two), seg_col, seg_row)
    middle, normed_two, out_full = project_out(
        coords, one, att, tokens, bias_out, gain_two, bias_two, r, m, hq
    )
    a_three = gather.first(after(far_three, project), middle)
    wide_three = gather.second(a_three, middle)
    two = gather.sources(columns[1], near, near_got, wide_two, gather.swapped(wide_two, project, att))
    got_att = exchange(att)
    act, slope, up_full = feed_up(coords, two, after(normed_two, a_three), bias_up, r, m)
    swap_three = gather.swapped(wide_three, act)
    three = gather.sources(columns[2], near, near_got, wide_three, swap_three)

    got_one = exchange(normed_one, act)
    got_two = exchange(normed_two, act)
    own, other = weight_grad(
        coords, scale, [(after(act, got_att, *wide_three[1:]), cotangent)], nz, m, "grad_down", 15
    )
    own_got = exchange(other, *swap_three)
    dh_mine, dh_other, grad_bias_up, grad_normed_two, down_full = feed_back(
        coords, three, after(cotangent, other), slope, up_full, r, m, ratio
    )
    grad_bias_up = grad_bias_up.reshape(-1)
    dh_got = exchange(dh_other)
    parts = add_parts(after(own, grad_normed_two), [own_got])
    sum_down = Reduction(parts, perms, nz, m)
    (grad_mid, e_mine, e_other, grad_att, *sums) = middle_back(
        coords, cotangent, middle, after(grad_normed_two, parts[-1]), gain_two, out_full
    )
    grad_gain_two, grad_bias_two, grad_bias_out, grad_bias_down = (v.reshape(-1) for v in sums)
    e_got = exchange(e_other)
    top = outcome(middle, after(act, grad_mid), down_full, bias_down, None, 0, 2)
    done = sum_down.step(top)
    parts = weight_grad_both(
        coords,
        scales,
        [
            (normed_two, got_two, [(after(dh_mine, done), dh_got)]),
            (att, got_att, [(e_mine, e_got)]),
        ],
        nz, m, "grad_up_out", 17,
    )
    done = sum_down.step(parts[0])
    sum_up = Reduction([parts[0]] + [after(part, done) for part in parts[1:]], perms, nz, m)
    mine_one, other_one = attention_back(coords, project, probs, after(grad_att, done), 0)
    one_got = exchange(other_one, sum_down.got[0], *sum_down.got[2:])
    mine_two, other_two = attention_back(coords, project, probs, after(grad_att, mine_one, sum_down.got[0], *sum_down.got[2:]), 1)
    two_got = exchange(other_two, sum_down.got[1])
    done = sum_up.step(mine_two)
    parts = weight_grad_both(
        coords,
        scales,
        [(normed_one, got_one, [(after(mine_one, done), one_got), (mine_two, two_got)])],
        nz, m, "grad_qkv", 14,
    )
    done = sum_up.step(parts[0])
    sum_one = Reduction([parts[0]] + [after(part, done) for part in parts[1:]], perms, nz, m)

    tokens_grad, *sums = input_back(coords, tokens, grad_mid, [mine_one, other_one, mine_two, other_two], after(qkv_full, done), gain_one)
    done = sum_one.step(tokens_grad, sum_up.got[0])
    sums = after_all(sums, done)
    grad_gain_one, grad_bias_one = sums[0].reshape(-1), sums[1].reshape(-1)
    sums = sums[2].reshape(2, 2, 3, quarter)
    sums = jnp.where(core == 0, sums, sums[:, ::-1]).transpose(2, 0, 1, 3)
    grad_bias_query = sums[0].reshape(-1)
    grad_bias_value = sums[2].reshape(-1)

    grad_small = jnp.concatenate(
        [
            grad_gain_one, grad_bias_one, grad_bias_query, grad_bias_value, grad_bias_out,
            grad_gain_two, grad_bias_two, grad_bias_up, grad_bias_down,
        ]
    )
    grad_small = mine * grad_small.reshape(n, -1)

    low = outcome(middle, after(act, done), down_full, bias_down, top, 1, 2)
    done = sum_one.step(low)
    grad_small = lax.all_to_all(
        after(jnp.concatenate([grad_small, grad_small]), done, sum_one.got[0]), BOTH, 0, 0, tiled=True
    )
    half_up = sum_up.step(done)
    half_down = sum_down.step(done)
    block_output = low
    half_qkv = sum_one.step(half_up, half_down)
    merged_small = jnp.sum(after(grad_small, half_qkv), 0)
    hu = hidden // 2

    lows = [piece.astype(BF) for piece in (half_qkv, half_up, half_down)]
    small_sq = jnp.where(core == 0, jnp.sum(merged_small * merged_small), 0.0)
    local_sq = sum((jnp.sum(jnp.square(piece.astype(F32))) for piece in lows)) + small_sq
    everyone = 2 * n
    shared = lax.all_to_all(jnp.full((everyone, 128), local_sq, F32), BOTH, 0, 0, tiled=True)
    total_sq = jnp.sum(shared[:, 0])
    got = [lax.ppermute(low, "grp", SWAP) for low in lows]
    clip = jnp.minimum(1.0, CLIP * lax.rsqrt(total_sq))
    news = update(
        coords,
        clip.reshape(1),
        lows,
        got,
        (qkv_weight, out_weight, up_weight, down_weight),
        (qkv_first, out_first, up_first, down_first),
        (qkv_second, out_second, up_second, down_second),
    )
    small = adam(small_params, small_first, small_second, merged_small * clip, 0.0, RATE_SMALL)
    return (
        block_output,
        tokens_grad,
        *news[0:4],
        small[0],
        *news[4:8],
        small[1],
        *news[8:12],
        small[2],
        total_sq,
    )


def solution(mesh):
    token, flat, row, vec = P(BOTH, None), P(BOTH), P("fsdp", None), P("fsdp")
    params = (row, row, row, row, vec)
    return jax.shard_map(
        shards,
        mesh=mesh,
        in_specs=(token, token, flat, P()) + params * 3,
        out_specs=(token, token) + params * 3 + (P(),),
        check_vma=False,
    )
```

```python
import math

import jax
import jax.numpy as jnp
from jax import lax
from jax.experimental import pallas as pl
from jax.experimental.pallas import tpu as pltpu
from jax.sharding import PartitionSpec as P

HD = 64
STEP = 10
EPS_NORM = 1e-06
CLIP = 1.0
RATE = 0.04
RATE_SMALL = 0.25
DECAY = 0.05
BETA_ONE = 0.9
BETA_TWO = 0.999
EPS_ADAM = 1e-08
F32 = jnp.float32
BF = jnp.bfloat16
BOTH = ("grp", "fsdp")
SWAP = [(0, 1), (1, 0)]
ANY = pl.BlockSpec(memory_space=pl.ANY)
SMEM = pl.BlockSpec(memory_space=pltpu.SMEM)
TILE = 128

RATIO = 0.1


def cost(us):
    return pl.CostEstimate(flops=int(us * RATIO * 1e9), bytes_accessed=0, transcendentals=0)


VMEM = pl.BlockSpec(memory_space=pltpu.VMEM)
SPAN = 256


def dims(n):
    m = max(1, math.isqrt(n // 4))
    return n // (m * m), m


def build_perms(n):
    nz, m = dims(n)

    def chip(z, y, x):
        return (z % nz) * m * m + (y % m) * m + x % m

    def build(move):
        return [
            (c * n + chip(z, y, x), c * n + chip(*move(c, z, y, x)))
            for c in range(2)
            for z in range(nz)
            for y in range(m)
            for x in range(m)
        ]

    return {
        "z": [build(lambda c, z, y, x: (z + k, y, x)) for k in range(nz)],
        "zx": [build(lambda c, z, y, x: (z ^ k, y, x)) for k in range(nz)],
        "a": [build(lambda c, z, y, x: (z, y, x + k) if c == 0 else (z, y + k, x)) for k in range(m)],
        "b": [build(lambda c, z, y, x: (z, y + k, x) if c == 0 else (z, y, x + k)) for k in range(m)],
        "x": [build(lambda c, z, y, x: (z, y, x + k)) for k in range(m)],
        "y": [build(lambda c, z, y, x: (z, y + k, x)) for k in range(m)],
    }


def send(value, table):
    return lax.ppermute(value, BOTH, table)


def layer_norm(x, gain, bias):
    mean = jnp.mean(x, -1, keepdims=True)
    centred = x - mean
    var = jnp.mean(centred * centred, -1, keepdims=True)
    return centred * lax.rsqrt(var + EPS_NORM) * gain + bias


def unpack(small, width, hidden):
    pieces = [small[i * width : (i + 1) * width] for i in range(7)]
    return pieces + [small[7 * width : 7 * width + hidden], small[7 * width + hidden :]]


def adam(weight, first, second, grad, decay, rate):
    first = BETA_ONE * first + (1.0 - BETA_ONE) * grad
    second = BETA_TWO * second + (1.0 - BETA_TWO) * grad * grad
    step_size = (
        first / (1.0 - BETA_ONE**STEP) / (jnp.sqrt(second / (1.0 - BETA_TWO**STEP)) + EPS_ADAM)
    )
    return (weight - rate * (step_size + decay * weight), first, second)


def after(value, *deps):
    return lax.optimization_barrier((value, *deps))[0]


def after_all(values, *deps):
    return lax.optimization_barrier((*values, *deps))[: len(values)]


def stacked(parts):
    def kernel(*refs):
        out, sems = refs[-2:]
        copies = [
            pltpu.make_async_copy(ref, out.at[k], sems.at[k]) for k, ref in enumerate(refs[: len(parts)])
        ]
        for copy in copies:
            copy.start()
        for copy in copies:
            copy.wait()

    return pl.pallas_call(
        kernel,
        out_shape=jax.ShapeDtypeStruct((len(parts),) + parts[0].shape, parts[0].dtype),
        in_specs=[ANY] * len(parts),
        out_specs=VMEM,
        scratch_shapes=[pltpu.SemaphoreType.DMA((len(parts),))],
        compiler_params=pltpu.CompilerParams(vmem_limit_bytes=60 << 20),
        cost_estimate=cost(0),
        name="stacked",
    )(*parts)


class Gather:
    def __init__(self, perms, nz, m):
        self.perms, self.nz, self.m = perms, nz, m

    def first(self, start, *hold):
        got = [send(start, self.perms["a"][k]) for k in range(1, self.m)]
        if hold:
            return stacked([after(start, *hold)] + got)
        return jnp.stack([start] + got)

    def second(self, part, *deps):
        held = after(part, *deps) if deps else part
        return [part] + [send(held, self.perms["b"][k]) for k in range(1, self.m)]

    def swapped(self, parts, *deps):
        deps = deps or [None] * len(parts)
        first, last = deps[0], deps[-1]
        return [
            lax.ppermute(p if dep is None else after(p, dep), "grp", SWAP)
            for p, dep in zip(parts, [first] + [last] * (len(parts) - 1))
        ]

    def far_start(self, own, *hold):
        came = send(own, self.perms["zx"][1])
        return jnp.concatenate([after(own, *hold) if hold else own, came])

    def far(self, got, deps, hold=()):
        step = 2
        while step < self.nz:
            came = send(after(got, *deps), self.perms["zx"][step])
            got = jnp.concatenate([after(got, *hold) if hold else got, came])
            step *= 2
        return got[1:]

    def sources(self, column, near, near_got, wide, wide_got):
        found = []
        for side, (close, parts) in enumerate(((near, wide), (near_got, wide_got))):
            for ib in range(self.m):
                found.append((close[ib], column, side, [((ia,), 0, ia, ib) for ia in range(self.m)]))
                pieces = [((ia, k - 1), k, ia, ib) for ia in range(self.m) for k in range(1, self.nz)]
                found.append((parts[ib], 0, side, pieces))
        return found


def start_pieces(refs, coord, sources, r, m, put, sems):
    z, y, x, c = coord[0], coord[1], coord[2], coord[3]
    for side in range(2):
        core = c if side == 0 else 1 - c
        for ref, (_, base, at, pieces) in zip(refs, sources):
            if at != side:
                continue
            for index, dz, ia, ib in pieces:
                px = lax.rem(x - jnp.where(core == 0, ia, ib) + m, m)
                py = lax.rem(y - jnp.where(core == 0, ib, ia) + m, m)
                chip = (jnp.bitwise_xor(z, dz) * m + py) * m + px
                src = ref.at[index]
                for dst, scol, cols in put(chip, core):
                    pltpu.make_async_copy(src.at[:, pl.ds(base + scol, cols)], dst, sems.at[side]).start()


def wait_bytes(ref, sem):
    pltpu.make_async_copy(ref, ref, sem).wait()


def aligned_rows(row, r):
    return pl.ds(pl.multiple_of(row, 16), r)


def aligned_cols(col, cols):
    return pl.ds(pl.multiple_of(col, 128), cols)


def pack(coords, qkv, out, up, down, width):
    r = qkv.shape[0]
    quarter, half, wide = width // 4, width // 2, up.shape[1] // 2
    ratio = down.shape[0] // r
    groups = [6 * quarter + half, wide, ratio * half]

    def kernel(coord, q_ref, o_ref, u_ref, d_ref, *outs):
        c = coord[3]

        def store(group, col, value):
            low = value.astype(BF)
            cols = low.shape[1]
            at = sum(groups[:group]) + col
            outs[0][0, :, at : at + cols] = low
            at -= groups[0] if group else 0
            outs[2 if group else 1][0, :, at : at + cols] = low

        for hh in range(2):
            for t in range(3):
                cols = aligned_cols(t * width + hh * half + c * quarter, quarter)
                store(0, (hh * 3 + t) * quarter, q_ref[:, cols])
        store(0, 6 * quarter, o_ref[:, aligned_cols(c * half, half)])
        store(1, 0, u_ref[:, aligned_cols(c * wide, wide)])
        for i in range(ratio):
            store(2, i * half, d_ref[i * r : (i + 1) * r, aligned_cols(c * half, half)])

    return pl.pallas_call(
        kernel,
        out_shape=[jax.ShapeDtypeStruct((1, r, cols), BF)
            for cols in (sum(groups), groups[0], groups[1] + groups[2])
        ],
        in_specs=[SMEM] + [VMEM] * 4,
        out_specs=[VMEM] * 3,
        compiler_params=pltpu.CompilerParams(vmem_limit_bytes=60 << 20),
        cost_estimate=cost(4),
        name="pack",
    )(coords, qkv, out, up, down)


def project_qkv(coords, sources, normed, bias, r, m):
    rows, width = normed.shape
    part = 3 * width // 4
    block = min(256, rows)
    steps = rows // block

    def kernel(coord, a_ref, b_ref, *refs):
        out_ref, w_out, w_ref, sems, osem = refs[-5:]
        i = pl.program_id(0)

        @pl.when(i == 0)
        def _():
            def put(chip, core):
                return [
                    (w_ref.at[core, hh, aligned_rows(chip * r, r), :], hh * part, part)
                    for hh in range(2)
                ]

            start_pieces(refs, coord, sources, r, m, put, sems)

        for side in range(2):
            core = coord[3] if side == 0 else 1 - coord[3]

            @pl.when(i == 0)
            def _():
                wait_bytes(w_ref.at[0], sems.at[side])
                for hh in range(2):
                    cols = aligned_cols((hh * 2 + core) * part, part)
                    pltpu.make_async_copy(w_ref.at[core, hh], w_out.at[:, cols], osem).start()

            for hh in range(2):
                cols = aligned_cols((hh * 2 + core) * part, part)
                out = jnp.dot(a_ref[...], w_ref[core, hh], preferred_element_type=F32)
                out_ref[:, cols] = (out + b_ref[:, cols]).astype(BF)

        @pl.when(i == steps - 1)
        def _():
            wait_bytes(w_ref, osem)

    return pl.pallas_call(
        kernel,
        grid=(steps,),
        out_shape=[
            jax.ShapeDtypeStruct((rows, 3 * width), BF),
            jax.ShapeDtypeStruct((width, 3 * width), BF),
        ],
        in_specs=[
            SMEM,
            pl.BlockSpec((block, width), lambda i: (i, 0)),
            pl.BlockSpec((1, 3 * width), lambda i: (0, 0)),
        ]
        + [ANY] * len(sources),
        out_specs=[pl.BlockSpec((block, 3 * width), lambda i: (i, 0)), ANY],
        scratch_shapes=[
            pltpu.VMEM((2, 2, width, part), BF),
            pltpu.SemaphoreType.DMA((2,)),
            pltpu.SemaphoreType.DMA,
        ],
        compiler_params=pltpu.CompilerParams(vmem_limit_bytes=60 << 20),
        cost_estimate=cost(10),
        name="project_qkv",
    )(coords, normed, bias.reshape(1, -1), *[source[0] for source in sources])


def project_out(coords, sources, att, tokens, bias, gain_two, bias_two, r, m, first):
    rows, width = att.shape
    half = width // 2
    block = min(128, rows)
    steps = rows // block

    def kernel(coord, a_ref, t_ref, b_ref, g_ref, c_ref, *refs):
        mid_ref, norm_ref, w_out, w_ref, sems, osem = refs[-6:]
        i = pl.program_id(0)

        @pl.when(i == 0)
        def _():
            def put(chip, core):
                return [
                    (w_ref.at[aligned_rows(chip * r, r), aligned_cols(core * half, half)], first, half)
                ]

            start_pieces(refs, coord, sources, r, m, put, sems)
            for side in range(2):
                wait_bytes(w_ref.at[:, pl.ds(0, half)], sems.at[side])
            pltpu.make_async_copy(w_ref, w_out, osem).start()

        mid = (
            t_ref[...].astype(F32)
            + jnp.dot(a_ref[...], w_ref[...], preferred_element_type=F32)
            + b_ref[...]
        )
        mid_ref[...] = mid
        norm_ref[...] = layer_norm(mid, g_ref[...], c_ref[...]).astype(BF)

        @pl.when(i == steps - 1)
        def _():
            wait_bytes(w_ref, osem)

    tile = pl.BlockSpec((block, width), lambda i: (i, 0))
    line = pl.BlockSpec((1, width), lambda i: (0, 0))
    return pl.pallas_call(
        kernel,
        grid=(steps,),
        out_shape=[
            jax.ShapeDtypeStruct((rows, width), F32),
            jax.ShapeDtypeStruct((rows, width), BF),
            jax.ShapeDtypeStruct((width, width), BF),
        ],
        in_specs=[SMEM, tile, tile, line, line, line] + [ANY] * len(sources),
        out_specs=[tile, tile, ANY],
        scratch_shapes=[
            pltpu.VMEM((width, width), BF),
            pltpu.SemaphoreType.DMA((2,)),
            pltpu.SemaphoreType.DMA,
        ],
        compiler_params=pltpu.CompilerParams(vmem_limit_bytes=60 << 20),
        cost_estimate=cost(8),
        name="project_out",
    )(
        coords, att, tokens, bias.reshape(1, -1), gain_two.reshape(1, -1), bias_two.reshape(1, -1),
        *[source[0] for source in sources],
    )


def weight_grad(coords, scale, pairs, nz, m, name, us):
    tokens, total = pairs[0][0].shape
    halves = [right.shape[1] // 2 for _, right in pairs]
    cols = sum(halves)
    r = total // (nz * m * m)
    zrows = total // nz
    mt = min(1024, zrows)
    mc = zrows // mt
    count = len(pairs)

    def kernel(coord, scale_ref, *refs):
        x_hbm = refs[0 : 2 * count : 2]
        y_hbm = refs[1 : 2 * count : 2]
        outs = refs[2 * count : 2 * count + 2]
        scratch = refs[2 * count + 2 :]
        xv = scratch[0:count]
        yv = scratch[count : 2 * count]
        acc, xsem, ysem, osem = scratch[2 * count :]
        z, y, x, c = coord[0], coord[1], coord[2], coord[3]
        weight = scale_ref[0]

        def xcopy(p, dz, i):
            pz = lax.rem(z + dz, nz)
            return pltpu.make_async_copy(
                x_hbm[p].at[:, pl.ds(pl.multiple_of(pz * zrows + i * mt, 128), mt)],
                xv[p].at[dz * mc + i],
                xsem.at[p, dz * mc + i],
            )

        def ycopy(p, side):
            owner = c if side == 0 else 1 - c
            return pltpu.make_async_copy(
                y_hbm[p].at[:, pl.ds(pl.multiple_of(owner * halves[p], 128), halves[p])],
                yv[p].at[:, aligned_cols(owner * halves[p], halves[p])],
                ysem.at[p, side],
            )

        for p in range(count):
            xcopy(p, 0, 0).start()
            ycopy(p, 1).start()
            ycopy(p, 0).start()
        for p in range(count):
            for dz in range(nz):
                for i in range(mc):
                    if dz or i:
                        xcopy(p, dz, i).start()
        copies = []
        for dz in range(nz):
            for i in range(mc):
                for p in range(count):
                    low = sum(halves[:p])
                    xcopy(p, dz, i).wait()
                    left = xv[p][dz * mc + i].T
                    if dz == 0 and i == 0:
                        ycopy(p, 1).wait()
                        ycopy(p, 0).wait()
                    both = jnp.dot(left, yv[p][...], preferred_element_type=F32) * weight
                    acc[dz, i * mt : (i + 1) * mt, :] = both.astype(BF)
            for side in (1, 0):
                owner = c if side == 0 else 1 - c
                for ib in range(m):
                    for ia in range(m):
                        dx = jnp.where(owner == 0, ia, ib)
                        dy = jnp.where(owner == 0, ib, ia)
                        px = lax.rem(x + dx, m)
                        py = lax.rem(y + dy, m)
                        copy = pltpu.make_async_copy(
                            acc.at[dz, aligned_rows((py * m + px) * r, r), aligned_cols(owner * cols, cols)],
                            outs[side].at[ib, ia, dz],
                            osem.at[side, dz, ib * m + ia],
                        )
                        copy.start()
                        copies.append(copy)
        for copy in copies:
            copy.wait()

    return pl.pallas_call(
        kernel,
        out_shape=[jax.ShapeDtypeStruct((m, m, nz, r, cols), BF)] * 2,
        in_specs=[SMEM, SMEM] + [ANY] * (2 * count),
        out_specs=[ANY] * 2,
        scratch_shapes=[pltpu.VMEM((nz * mc, tokens, mt), BF) for _ in pairs]
        + [pltpu.VMEM((tokens, 2 * h), BF) for h in halves]
        + [
            pltpu.VMEM((nz, zrows, 2 * cols), BF),
            pltpu.SemaphoreType.DMA((count, nz * mc)),
            pltpu.SemaphoreType.DMA((count, 2)),
            pltpu.SemaphoreType.DMA((2, nz, m * m)),
        ],
        compiler_params=pltpu.CompilerParams(vmem_limit_bytes=60 << 20),
        cost_estimate=cost(us),
        name=name,
    )(coords, scale, *[v for pair in pairs for v in pair])


def weight_grad_both(coords, scales, pairs, nz, m, name, us):
    tokens, total = pairs[0][0].shape
    widths = [[own.shape[1] for own, _ in pair[2]] for pair in pairs]
    halves = [sum(w) for w in widths]
    cols = sum(halves)
    r = total // (nz * m * m)
    zrows = total // nz
    count = len(pairs)
    group = 2 if nz % 2 == 0 else 1
    operands, places = [], []
    for pair in pairs:
        places.append(len(operands))
        operands += [*pair[:2], *[v for both in pair[2] for v in both]]

    def kernel(coord, scale_ref, *refs):
        ins = refs[: len(operands)]
        outs = refs[len(operands) : len(operands) + m]
        scratch = refs[len(operands) + m :]
        held = scratch[: 4 * count]
        acc, xsem, ysem, osem = scratch[4 * count :]
        z, y, x, c = coord[0], coord[1], coord[2], coord[3]

        def xcopy(p, who, dz):
            pz = lax.rem(z + dz, nz)
            return pltpu.make_async_copy(
                ins[places[p] + who].at[:, pl.ds(pl.multiple_of(pz * zrows, 128), zrows)],
                held[4 * p + who].at[dz],
                xsem.at[p, who, dz],
            )

        def ycopies(p, who):
            dst = held[4 * p + 2 + who]
            found = []
            for k, h in enumerate(widths[p]):
                at = pl.ds(sum(widths[p][:k]), h)
                src = ins[places[p] + 2 + 2 * k + who]
                found.append(pltpu.make_async_copy(src, dst.at[:, at], ysem.at[p, who, k]))
            return found

        for p in range(count):
            for who in range(2):
                xcopy(p, who, 0).start()
                for copy in ycopies(p, who):
                    copy.start()
        for p in range(count):
            for dz in range(1, nz):
                for who in range(2):
                    xcopy(p, who, dz).start()
        copies = []
        for dz in range(nz):
            for p in range(count):
                low = sum(halves[:p])
                if dz % group:
                    continue
                out = None
                for who in range(2):
                    for k in range(group):
                        xcopy(p, who, dz + k).wait()
                    if dz == 0:
                        for copy in ycopies(p, who):
                            copy.wait()
                    left = jnp.concatenate([held[4 * p + who][dz + k].T for k in range(group)], 0)
                    part = jnp.dot(left, held[4 * p + 2 + who][...], preferred_element_type=F32)
                    part = part * scale_ref[who]
                    out = part if out is None else out + part
                out = out.astype(BF)
                for k in range(group):
                    acc[dz + k, :, low : low + halves[p]] = out[k * zrows : (k + 1) * zrows]
            for ib in range(m):
                for ia in range(m):
                    px = lax.rem(x + jnp.where(c == 0, ia, ib), m)
                    py = lax.rem(y + jnp.where(c == 0, ib, ia), m)
                    copy = pltpu.make_async_copy(
                        acc.at[dz, aligned_rows((py * m + px) * r, r), :],
                        outs[ib].at[ia, dz],
                        osem.at[dz, ib * m + ia],
                    )
                    copy.start()
                    copies.append(copy)
        for copy in copies:
            copy.wait()

    shapes = []
    for h in halves:
        shapes += [pltpu.VMEM((nz, tokens, zrows), BF)] * 2 + [pltpu.VMEM((tokens, h), BF)] * 2
    return pl.pallas_call(
        kernel,
        out_shape=[jax.ShapeDtypeStruct((m, nz, r, cols), BF)] * m,
        in_specs=[SMEM, SMEM] + [ANY] * len(operands),
        out_specs=[ANY] * m,
        scratch_shapes=shapes
        + [
            pltpu.VMEM((nz, zrows, cols), BF),
            pltpu.SemaphoreType.DMA((count, 2, nz)),
            pltpu.SemaphoreType.DMA((count, 2, max(len(w) for w in widths))),
            pltpu.SemaphoreType.DMA((nz, m * m)),
        ],
        compiler_params=pltpu.CompilerParams(vmem_limit_bytes=60 << 20),
        cost_estimate=cost(us),
        name=name,
    )(coords, scales, *operands)


def add_parts(keep, got):
    size, cols = keep.shape[0], keep.shape[-1]
    shape = keep.shape[1:]
    flat = math.prod(shape[:-1])
    block = max(16, min(flat, (1 << 20) // (size * cols) // 16 * 16))
    while flat % block:
        block -= 16
    count = len(got) + 1

    def kernel(*refs):
        for k in range(size):
            total = refs[0][k].astype(F32)
            for ref in refs[1:count]:
                total += ref[k].astype(F32)
            refs[count + k][...] = total.astype(BF)

    outs = pl.pallas_call(
        kernel,
        grid=(flat // block,),
        out_shape=[jax.ShapeDtypeStruct((flat, cols), BF)] * size,
        in_specs=[pl.BlockSpec((size, block, cols), lambda i: (0, i, 0))] * count,
        out_specs=[pl.BlockSpec((block, cols), lambda i: (i, 0))] * size,
        compiler_params=pltpu.CompilerParams(vmem_limit_bytes=60 << 20),
        cost_estimate=cost(2),
        name="add_parts",
    )(*[v.reshape(size, flat, cols) for v in [keep, *got]])
    return [out.reshape(shape) for out in outs]


class Reduction:
    def __init__(self, parts, perms, nz, m):
        self.perms, self.sizes = perms, {"b": m, "a": m, "z": nz}
        self.left = ["a", "z"]
        self.pass_on("b", parts)

    def pass_on(self, axis, parts):
        self.keep = parts[0]
        self.got = [send(parts[k], self.perms[axis][k]) for k in range(1, self.sizes[axis])]

    def step(self, *deps):
        if not self.left:
            t = after(self.keep, *deps).astype(F32) if deps else self.keep.astype(F32)
            for part in self.got:
                t = t + part.astype(F32)
            return t
        axis = self.left.pop(0)
        parts = add_parts(after(self.keep, *deps), self.got)
        self.pass_on(axis, parts)
        return parts[-1]


def feed_up(coords, sources, normed, bias, r, m):
    rows, width = normed.shape
    hidden = bias.shape[0]
    half, cols, step = hidden // 2, 512, 256
    tiles = half // cols

    def kernel(coord, a_ref, b_ref, *refs):
        act_ref, slope_ref, w_out, w_ref, sems, osem = refs[-6:]
        j = pl.program_id(0)

        @pl.when(j == 0)
        def _():
            def put(chip, core):
                return [(w_ref.at[core, aligned_rows(chip * r, r), :], 0, half)]

            start_pieces(refs, coord, sources, r, m, put, sems)

        for side in range(2):

            @pl.when(j == side * tiles)
            def _():
                wait_bytes(w_ref.at[0], sems.at[side])
                core = coord[3] if side == 0 else 1 - coord[3]
                at = aligned_cols(core * half, half)
                pltpu.make_async_copy(w_ref.at[core], w_out.at[:, at], osem).start()

        @pl.when(j == 2 * tiles - 1)
        def _():
            wait_bytes(w_ref, osem)

        core = jnp.where(j < tiles, coord[3], 1 - coord[3])
        weight = w_ref[core, :, aligned_cols(lax.rem(j, tiles) * cols, cols)]
        c0, c1 = math.sqrt(2.0 / math.pi), 0.044715
        for i in range(0, rows, step):
            h = jnp.dot(a_ref[i : i + step, :], weight, preferred_element_type=F32) + b_ref[...]
            square = h * h
            gate = 0.5 + 0.5 * jnp.tanh(h * (c0 + (c0 * c1) * square))
            act = h * gate
            act_ref[i : i + step, :] = act.astype(BF)
            slope = gate + (act - act * gate) * (2.0 * c0 + (6.0 * c0 * c1) * square)
            slope_ref[i : i + step, :] = slope.astype(BF)

    def tile(j, coord):
        return (0, jnp.where(j < tiles, coord[3], 1 - coord[3]) * tiles + lax.rem(j, tiles))

    grid_spec = pltpu.PrefetchScalarGridSpec(
        num_scalar_prefetch=1,
        grid=(2 * tiles,),
        in_specs=[
            pl.BlockSpec((rows, width), lambda j, coord: (0, 0)),
            pl.BlockSpec((1, cols), tile),
        ]
        + [ANY] * len(sources),
        out_specs=[
            pl.BlockSpec((rows, cols), tile),
            pl.BlockSpec((rows, cols), tile),
            ANY,
        ],
        scratch_shapes=[
            pltpu.VMEM((2, width, half), BF),
            pltpu.SemaphoreType.DMA((2,)),
            pltpu.SemaphoreType.DMA,
        ],
    )
    return pl.pallas_call(
        kernel,
        grid_spec=grid_spec,
        out_shape=[
            jax.ShapeDtypeStruct((rows, hidden), BF),
            jax.ShapeDtypeStruct((rows, hidden), BF),
            jax.ShapeDtypeStruct((width, hidden), BF),
        ],
        compiler_params=pltpu.CompilerParams(vmem_limit_bytes=60 << 20),
        cost_estimate=cost(25),
        name="feed_up",
    )(coords, normed, bias.reshape(1, hidden), *[source[0] for source in sources])


def feed_back(coords, sources, grad, slope, up, r, m, ratio):
    rows, width = grad.shape
    hidden = up.shape[1]
    half, cols, step = width // 2, 512, 512
    tiles = hidden // cols

    def tile_at(j, coord):
        core = jnp.where(j < tiles // 2, coord[3], 1 - coord[3])
        return core * (tiles // 2) + lax.rem(j, tiles // 2)

    def kernel(coord, g_ref, s_ref, u_ref, *refs):
        mine_ref, other_ref, sum_ref, out_ref, d_out, d_ref, dh_ref, sems, osems = refs[-9:]
        j = pl.program_id(0)

        @pl.when(j == 0)
        def _():
            out_ref[...] = jnp.zeros_like(out_ref)

            def put(chip, core):
                return [
                    (
                        d_ref.at[
                            aligned_rows((chip * ratio + s) * r, r), aligned_cols(core * half, half)
                        ],
                        s * half,
                        half,
                    )
                    for s in range(ratio)
                ]

            start_pieces(refs, coord, sources, r, m, put, sems)
            for side in range(2):
                wait_bytes(d_ref.at[:, pl.ds(0, half)], sems.at[side])
            pltpu.make_async_copy(d_ref, d_out, osems.at[2]).start()

        slot = lax.rem(j, 2)

        @pl.when(j >= 2)
        def _():
            wait_bytes(dh_ref.at[0], osems.at[slot])

        down = d_ref[pl.ds(pl.multiple_of(tile_at(j, coord) * cols, cols), cols), :]
        total = jnp.zeros((1, cols), F32)
        for i in range(0, rows, step):
            part = lax.dot_general(
                g_ref[i : i + step, :], down, (((1,), (1,)), ((), ())), preferred_element_type=F32
            )
            dh = (part * s_ref[i : i + step, :].astype(F32)).astype(BF)
            dh_ref[slot, i : i + step, :] = dh
            total += jnp.sum(dh.astype(F32), 0, keepdims=True)
            out_ref[i : i + step, :] += lax.dot_general(
                dh, u_ref[...], (((1,), (1,)), ((), ())), preferred_element_type=F32
            )
        sum_ref[...] = total

        def copy_out(ref):
            at = aligned_cols(lax.rem(j, tiles // 2) * cols, cols)
            pltpu.make_async_copy(dh_ref.at[slot], ref.at[:, at], osems.at[slot]).start()

        @pl.when(j < tiles // 2)
        def _():
            copy_out(mine_ref)

        @pl.when(j >= tiles // 2)
        def _():
            copy_out(other_ref)

        @pl.when(j == tiles - 1)
        def _():
            for at in range(2):
                wait_bytes(dh_ref.at[0], osems.at[at])
            wait_bytes(d_ref, osems.at[2])

    grid_spec = pltpu.PrefetchScalarGridSpec(
        num_scalar_prefetch=1,
        grid=(tiles,),
        in_specs=[
            pl.BlockSpec((rows, width), lambda j, coord: (0, 0)),
            pl.BlockSpec((rows, cols), lambda j, coord: (0, tile_at(j, coord))),
            pl.BlockSpec((width, cols), lambda j, coord: (0, tile_at(j, coord))),
        ]
        + [ANY] * len(sources),
        out_specs=[
            ANY,
            ANY,
            pl.BlockSpec((1, cols), lambda j, coord: (0, tile_at(j, coord))),
            pl.BlockSpec((rows, width), lambda j, coord: (0, 0)),
            ANY,
        ],
        scratch_shapes=[
            pltpu.VMEM((hidden, width), BF),
            pltpu.VMEM((2, rows, cols), BF),
            pltpu.SemaphoreType.DMA((2,)),
            pltpu.SemaphoreType.DMA((3,)),
        ],
    )
    return pl.pallas_call(
        kernel,
        grid_spec=grid_spec,
        out_shape=[
            jax.ShapeDtypeStruct((rows, hidden // 2), BF),
            jax.ShapeDtypeStruct((rows, hidden // 2), BF),
            jax.ShapeDtypeStruct((1, hidden), F32),
            jax.ShapeDtypeStruct((rows, width), F32),
            jax.ShapeDtypeStruct((hidden, width), BF),
        ],
        compiler_params=pltpu.CompilerParams(vmem_limit_bytes=60 << 20),
        cost_estimate=cost(50),
        name="feed_back",
    )(coords, grad, slope, up, *[source[0] for source in sources])


def norm_back(x, grad, gain):
    mean = jnp.mean(x, -1, keepdims=True)
    centred = x - mean
    inv = lax.rsqrt(jnp.mean(centred * centred, -1, keepdims=True) + EPS_NORM)
    hat = centred * inv
    inner = grad * gain
    back = inv * (
        inner
        - jnp.mean(inner, -1, keepdims=True)
        - hat * jnp.mean(inner * hat, -1, keepdims=True)
    )
    return back, jnp.sum(grad * hat, 0, keepdims=True), jnp.sum(grad, 0, keepdims=True)


def middle_back(coords, cotangent, middle, grad, gain, out):
    rows, width = middle.shape
    block = min(256, rows)

    half = width // 2

    def kernel(coord, c_ref, m_ref, d_ref, g_ref, w_ref, *refs):
        dy_ref, mine_ref, other_ref, a_ref, gain_ref, bias_ref, bo_ref, bd_ref, e_ref = refs

        @pl.when(pl.program_id(0) == 0)
        def _():
            for ref in (gain_ref, bias_ref, bo_ref, bd_ref):
                ref[...] = jnp.zeros_like(ref)

        cot = c_ref[...].astype(F32)
        back, for_gain, for_bias = norm_back(m_ref[...], d_ref[...], g_ref[...])
        dy = cot + back
        low = dy.astype(BF)
        dy_ref[...] = dy
        e_ref[...] = low
        mine_ref[...] = e_ref[:, aligned_cols(coord[3] * half, half)]
        other_ref[...] = e_ref[:, aligned_cols((1 - coord[3]) * half, half)]
        a_ref[...] = lax.dot_general(
            low, w_ref[...], (((1,), (1,)), ((), ())), preferred_element_type=F32
        ).astype(BF)
        gain_ref[...] += for_gain
        bias_ref[...] += for_bias
        bo_ref[...] += jnp.sum(low.astype(F32), 0, keepdims=True)
        bd_ref[...] += jnp.sum(cot, 0, keepdims=True)

    tile = pl.BlockSpec((block, width), lambda i: (i, 0))
    part = pl.BlockSpec((block, half), lambda i: (i, 0))
    line = pl.BlockSpec((1, width), lambda i: (0, 0))
    return pl.pallas_call(
        kernel,
        grid=(rows // block,),
        out_shape=[
            jax.ShapeDtypeStruct((rows, cols), t)
            for cols, t in ((width, F32), (half, BF), (half, BF), (width, BF))
        ]
        + [jax.ShapeDtypeStruct((1, width), F32)] * 4,
        in_specs=[SMEM, tile, tile, tile, line, pl.BlockSpec((width, width), lambda i: (0, 0))],
        out_specs=[tile, part, part, tile] + [line] * 4,
        scratch_shapes=[pltpu.VMEM((block, width), BF)],
        compiler_params=pltpu.CompilerParams(vmem_limit_bytes=60 << 20),
        cost_estimate=cost(3),
        name="middle_back",
    )(coords, cotangent, middle, grad, gain.reshape(1, -1), out)


def input_back(coords, tokens, grad_mid, parts, weight, gain):
    rows, width = tokens.shape
    total = weight.shape[1]
    block = min(256, rows)
    count = len(parts)
    cols = total // count

    def kernel(coord, t_ref, m_ref, w_ref, g_ref, *refs):
        out_ref, gain_ref, bias_ref, sum_ref = refs[count:]

        @pl.when(pl.program_id(0) == 0)
        def _():
            for ref in (gain_ref, bias_ref, sum_ref):
                ref[...] = jnp.zeros_like(ref)

        grad = jnp.zeros((block, width), F32)
        for p in range(count):
            core = coord[3] if p % 2 == 0 else 1 - coord[3]
            part = refs[p][...]
            sum_ref[:, p * cols : (p + 1) * cols] += jnp.sum(part.astype(F32), 0, keepdims=True)
            weight_at = aligned_cols((p // 2 * 2 + core) * cols, cols)
            grad += lax.dot_general(
                part, w_ref[:, weight_at], (((1,), (1,)), ((), ())), preferred_element_type=F32
            )
        back, for_gain, for_bias = norm_back(t_ref[...].astype(F32), grad, g_ref[...])
        out_ref[...] = (m_ref[...] + back).astype(BF)
        gain_ref[...] += for_gain
        bias_ref[...] += for_bias

    tile = pl.BlockSpec((block, width), lambda i: (i, 0))
    line = pl.BlockSpec((1, width), lambda i: (0, 0))
    return pl.pallas_call(
        kernel,
        grid=(rows // block,),
        out_shape=[
            jax.ShapeDtypeStruct((rows, width), BF),
            jax.ShapeDtypeStruct((1, width), F32),
            jax.ShapeDtypeStruct((1, width), F32),
            jax.ShapeDtypeStruct((1, total), F32),
        ],
        in_specs=[SMEM, tile, tile, pl.BlockSpec((width, total), lambda i: (0, 0)), line]
        + [pl.BlockSpec((block, cols), lambda i: (i, 0))] * count,
        out_specs=[tile, line, line, pl.BlockSpec((1, total), lambda i: (0, 0))],
        compiler_params=pltpu.CompilerParams(vmem_limit_bytes=60 << 20),
        cost_estimate=cost(30),
        name="input_back",
    )(coords, tokens, grad_mid, weight, gain.reshape(1, -1), *parts)


def outcome(middle, act, down, bias, before, part, parts):
    rows, width = middle.shape
    hidden = act.shape[1]
    block = 128
    first = part * (rows // parts // block)

    def kernel(m_ref, a_ref, d_ref, b_ref, *refs):
        out = jnp.dot(a_ref[...], d_ref[...], preferred_element_type=F32)
        refs[-1][...] = (m_ref[...] + out + b_ref[...]).astype(BF)

    more = [] if before is None else [before]
    return pl.pallas_call(
        kernel,
        grid=(rows // parts // block,),
        out_shape=jax.ShapeDtypeStruct((rows, width), BF),
        in_specs=[
            pl.BlockSpec((block, width), lambda i: (first + i, 0)),
            pl.BlockSpec((block, hidden), lambda i: (first + i, 0)),
            pl.BlockSpec((hidden, width), lambda i: (0, 0)),
            pl.BlockSpec((1, width), lambda i: (0, 0)),
        ]
        + [ANY] * len(more),
        out_specs=pl.BlockSpec((block, width), lambda i: (first + i, 0)),
        input_output_aliases={4: 0} if more else {},
        compiler_params=pltpu.CompilerParams(vmem_limit_bytes=60 << 20),
        cost_estimate=cost(3 if part == 0 else 10),
        name="outcome_" + str(part),
    )(middle, act, down, bias.reshape(1, -1), *more)


def head_stack(block, low_lanes):
    zero = jnp.zeros_like(block)
    return jnp.concatenate(
        [jnp.where(low_lanes, block, zero), jnp.where(low_lanes, zero, block)], 0
    )


def window_block(t, rows):
    return jnp.clip(2 * t - 1, 0, rows // 64 - SPAN // 64)


def window_specs(rows, cols, at=0):
    return [
        pl.BlockSpec((64, cols), lambda t, i=i: (window_block(t, rows) + i, at)) for i in range(SPAN // 64)
    ]


def joined_rows(refs, lanes):
    return jnp.concatenate([ref[:, lanes] for ref in refs], 0)


def attention(project, seg_col, seg_row):
    rows, width = project.shape[0], project.shape[1] // 3
    pairs = width // (2 * HD)
    blocks = SPAN // 64

    def pair_lanes(pair, which):
        hh, rest = divmod(pair, pairs // 2)
        core, within = divmod(rest, pairs // 4)
        quarter = width // 4
        first = (hh * 2 + core) * 3 * quarter + which * quarter + within * 2 * HD
        return slice(first, first + 2 * HD)

    def kernel(row_ref, q_ref, *refs):
        cols, windows, (out_ref, probs_ref) = refs[:blocks], refs[blocks : 2 * blocks], refs[2 * blocks :]
        same = joined_rows(cols, slice(0, 1)) == row_ref[...]
        same = jnp.concatenate([same, same], 1)
        low = lax.broadcasted_iota(jnp.int32, (TILE, 2 * HD), 1) < HD
        for h in range(pairs):
            stack = head_stack(q_ref[:, pair_lanes(h, 0)] * HD**-0.5, low)
            keys = joined_rows(windows, pair_lanes(h, 1))
            scores = lax.dot_general(keys, stack, (((1,), (1,)), ((), ())), preferred_element_type=F32)
            scores = jnp.where(same, scores, -1e30)
            expo = jnp.exp(scores - jnp.max(scores, 0, keepdims=True))
            probs = (expo * (1.0 / jnp.sum(expo, 0, keepdims=True))).astype(BF)
            probs_ref[0, h] = probs
            mixed = lax.dot_general(
                probs,
                joined_rows(windows, pair_lanes(h, 2)),
                (((0,), (0,)), ((), ())),
                preferred_element_type=F32,
            )
            out_ref[:, h * 2 * HD : (h + 1) * 2 * HD] = jnp.where(low, mixed[:TILE], mixed[TILE:]).astype(BF)

    return pl.pallas_call(
        kernel,
        grid=(rows // TILE,),
        out_shape=[
            jax.ShapeDtypeStruct((rows, width), BF),
            jax.ShapeDtypeStruct((rows // TILE, pairs, SPAN, 2 * TILE), BF),
        ],
        in_specs=[
            pl.BlockSpec((1, TILE), lambda t: (0, t)),
            pl.BlockSpec((TILE, 3 * width), lambda t: (t, 0)),
        ]
        + window_specs(rows, 1)
        + window_specs(rows, 3 * width),
        out_specs=[
            pl.BlockSpec((TILE, width), lambda t: (t, 0)),
            pl.BlockSpec((1, pairs, SPAN, 2 * TILE), lambda t: (t, 0, 0, 0)),
        ],
        compiler_params=pltpu.CompilerParams(vmem_limit_bytes=60 << 20),
        cost_estimate=cost(14),
        name="attention",
    )(seg_row, project, *[seg_col] * blocks, *[project] * blocks)


def attention_back(coords, project, probs, grad, hh):
    rows, width = project.shape[0], project.shape[1] // 3
    quarter = width // 4
    pairs = width // (2 * HD)
    tiles = rows // TILE
    blocks = SPAN // 64

    def kernel(coord, q_ref, p_ref, g_ref, *refs):
        windows, (mine_ref, other_ref, dk, dv) = refs[:blocks], refs[blocks:]
        t = pl.program_id(0)

        @pl.when(t == 0)
        def _():
            dk[...] = jnp.zeros_like(dk)
            dv[...] = jnp.zeros_like(dv)

        window = pl.ds(pl.multiple_of(window_block(t, rows) * 64, 64), SPAN)
        own = pl.ds(pl.multiple_of(t * TILE, TILE), TILE)
        low = lax.broadcasted_iota(jnp.int32, (TILE, 2 * HD), 1) < HD
        scale = HD**-0.5
        for side, out_ref in enumerate((mine_ref, other_ref)):
            core = coord[3] if side == 0 else 1 - coord[3]
            for within in range(pairs // 4):
                h = within * 2 * HD
                held = slice(side * quarter + h, side * quarter + h + 2 * HD)

                def lanes(which):
                    return aligned_cols(core * 3 * quarter + which * quarter + h, 2 * HD)

                queries = head_stack(q_ref[:, lanes(0)], low)
                grads = head_stack(g_ref[:, aligned_cols(core * quarter + h, 2 * HD)], low)
                soft = p_ref[0, core * (pairs // 4) + within]
                wide = soft.astype(F32)
                grad_probs = lax.dot_general(
                    joined_rows(windows, lanes(2)), grads, (((1,), (1,)), ((), ())),
                    preferred_element_type=F32,
                )
                inner = jnp.sum(wide * grad_probs, 0, keepdims=True)
                grad_scores = (wide * (grad_probs - inner)).astype(BF)
                dv[window, held] += jnp.dot(soft, grads, preferred_element_type=F32)
                dk[window, held] += jnp.dot(grad_scores, queries, preferred_element_type=F32)
                dq = lax.dot_general(
                    grad_scores, joined_rows(windows, lanes(1)), (((0,), (0,)), ((), ())),
                    preferred_element_type=F32,
                )
                out_ref[own, h : h + 2 * HD] = (
                    jnp.where(low, dq[:TILE], dq[TILE:]) * scale
                ).astype(BF)

        @pl.when(t == tiles - 1)
        def _():
            for side, out_ref in enumerate((mine_ref, other_ref)):
                held = slice(side * quarter, (side + 1) * quarter)
                out_ref[:, quarter : 2 * quarter] = (dk[:, held] * scale).astype(BF)
                out_ref[:, 2 * quarter :] = dv[:, held].astype(BF)

    whole = pl.BlockSpec((rows, 3 * quarter), lambda t: (0, 0))
    return pl.pallas_call(
        kernel,
        grid=(tiles,),
        out_shape=[jax.ShapeDtypeStruct((rows, 3 * quarter), BF)] * 2,
        in_specs=[
            SMEM,
            pl.BlockSpec((TILE, 6 * quarter), lambda t: (t, hh)),
            pl.BlockSpec((1, pairs // 2, SPAN, 2 * TILE), lambda t: (t, hh, 0, 0)),
            pl.BlockSpec((TILE, 2 * quarter), lambda t: (t, hh)),
        ]
        + window_specs(rows, 6 * quarter, hh),
        out_specs=[whole, whole],
        scratch_shapes=[pltpu.VMEM((rows, 2 * quarter), F32)] * 2,
        compiler_params=pltpu.CompilerParams(vmem_limit_bytes=60 << 20),
        cost_estimate=cost(16),
        name="attention_back_" + str(hh),
    )(coords, project, probs, grad, *[project] * blocks)


def update(coords, clip, lows, got, weights, firsts, seconds):
    r, width = weights[1].shape
    hidden = weights[2].shape[1]
    ratio = weights[3].shape[0] // r
    quarter, half = width // 4, width // 2
    steps = max(1, r // 16)
    block = r // steps

    def kernel(coord, clip_ref, *refs):
        halves = refs[0:3], refs[3:6]
        olds = refs[6:18]
        news = refs[18:30]
        scale = clip_ref[0]
        for side in range(2):
            core = coord[3] if side == 0 else 1 - coord[3]
            qkv, rest, down = halves[side]

            def put(i, source, first, cols, col):
                at = aligned_cols(col, cols)
                grad = source[:, first : first + cols].astype(F32) * scale
                found = adam(olds[i][:, at], olds[4 + i][:, at], olds[8 + i][:, at], grad, DECAY, RATE)
                for k in range(3):
                    news[4 * k + i][:, at] = found[k]

            for hh in range(2):
                for t in range(3):
                    put(0, qkv, (hh * 3 + t) * quarter, quarter, t * width + hh * half + core * quarter)
            put(1, rest, hidden // 2, half, core * half)
            put(2, rest, 0, hidden // 2, core * (hidden // 2))
            put(3, down, 0, half, core * half)

    def rows_of(v):
        return pl.BlockSpec((v.shape[0] // steps, v.shape[1]), lambda i: (i, 0))

    arrays = [*weights, *firsts, *seconds]
    return pl.pallas_call(
        kernel,
        grid=(steps,),
        out_shape=[jax.ShapeDtypeStruct(v.shape, F32) for v in arrays],
        in_specs=[SMEM, SMEM] + [rows_of(v) for v in (*lows, *got, *arrays)],
        out_specs=[rows_of(v) for v in arrays],
        compiler_params=pltpu.CompilerParams(vmem_limit_bytes=60 << 20),
        cost_estimate=cost(10),
        name="update",
    )(coords, clip, *lows, *got, *arrays)


def shards(
    tokens, cotangent, segment_ids, group_counts,
    qkv_weight, out_weight, up_weight, down_weight, small_params,
    qkv_first, out_first, up_first, down_first, small_first,
    qkv_second, out_second, up_second, down_second, small_second,
):
    width = tokens.shape[1]
    hidden = up_weight.shape[1]
    rows = tokens.shape[0]
    n = lax.axis_size("fsdp")
    nz, m = dims(n)
    perms = build_perms(n)
    chip = lax.axis_index("fsdp")
    core = lax.axis_index("grp")
    z, y, x = chip // (m * m), chip // m % m, chip % m
    coords = jnp.stack([z, y, x, core]).astype(jnp.int32)
    r = qkv_weight.shape[0]
    ratio = down_weight.shape[0] // r

    counts = group_counts.astype(F32)
    share = counts / jnp.sum(counts)
    is_local = core >= lax.axis_size("grp") // 2
    mine = jnp.where(is_local, share[1], share[0])
    scales = jnp.stack([mine, jnp.where(is_local, share[0], share[1])])
    scale = mine.reshape(1)
    quarter = width // 4
    hq, ho = 3 * width // 2, width // 2

    gather = Gather(perms, nz, m)
    piece = jnp.broadcast_to(small_params.astype(BF).astype(F32), (2 * n,) + small_params.shape)
    small_full = lax.all_to_all(piece, BOTH, 0, 0, tiled=True)[:n].reshape(-1)
    packed, own_one, own_rest = pack(
        coords, qkv_weight, out_weight, up_weight, down_weight, width
    )
    columns = [0, own_one.shape[2], own_one.shape[2] + hidden // 2]
    near_a = gather.first(packed[0])
    pair_one = gather.far_start(own_one)
    near = gather.second(near_a, pair_one)
    near_got = gather.swapped(near)
    far_one = gather.far(pair_one, (), (small_full,))
    small_full = after(small_full, *near[1:])
    gain_one, bias_one, bias_query, bias_value, bias_out, gain_two, bias_two, bias_up, bias_down = (
        unpack(small_full, width, hidden)
    )
    normed_one = layer_norm(after(tokens, *near[1:]).astype(F32), gain_one, bias_one).astype(BF)
    qkv_bias = jnp.stack([bias_query, jnp.zeros_like(bias_query), bias_value])
    qkv_bias = qkv_bias.reshape(3, 2, 2, quarter).transpose(1, 2, 0, 3).reshape(-1)
    a_one = gather.first(after(far_one, *near[1:]))
    pair_rest = gather.far_start(after(own_rest, near_a), a_one)
    pair_two, pair_three = pair_rest[:, :, : hidden // 2], pair_rest[:, :, hidden // 2 :]
    wide_one = gather.second(a_one, normed_one, qkv_bias, pair_rest)
    far_two = gather.far(pair_two, (far_one,))
    one = gather.sources(0, near, near_got, wide_one, gather.swapped(wide_one, far_two, a_one))

    def exchange(value, *deps):
        return lax.ppermute(after(value, *deps) if deps else value, "grp", SWAP)

    project, qkv_full = project_qkv(coords, one, after(normed_one, far_two), qkv_bias, r, m)
    a_two = gather.first(after(far_two, wide_one[-1]), project)
    wide_two = gather.second(a_two, project)
    seg_col, seg_row = segment_ids.reshape(rows, 1), segment_ids.reshape(1, rows)
    att, probs = attention(after(project, a_two), seg_col, seg_row)
    far_three = gather.far(pair_three, (far_two,), (att,))
    middle, normed_two, out_full = project_out(
        coords, one, after(att, far_three), tokens, bias_out, gain_two, bias_two, r, m, hq
    )
    a_three = gather.first(after(far_three, att), middle)
    wide_three = gather.second(a_three, middle)
    two = gather.sources(columns[1], near, near_got, wide_two, gather.swapped(wide_two, project, att))
    got_att = exchange(att)
    act, slope, up_full = feed_up(coords, two, after(normed_two, a_three), bias_up, r, m)
    swap_three = gather.swapped(wide_three, act)
    three = gather.sources(columns[2], near, near_got, wide_three, swap_three)

    got_one = exchange(normed_one, act)
    got_two = exchange(normed_two, act)
    own, other = weight_grad(
        coords, scale, [(after(act, got_att, *wide_three[1:]), cotangent)], nz, m, "grad_down", 15
    )
    own_got = exchange(other, *swap_three)
    dh_mine, dh_other, grad_bias_up, grad_normed_two, down_full = feed_back(
        coords, three, after(cotangent, other), slope, up_full, r, m, ratio
    )
    grad_bias_up = grad_bias_up.reshape(-1)
    dh_got = exchange(dh_other)
    parts = add_parts(after(own, grad_normed_two), [own_got])
    sum_down = Reduction(parts, perms, nz, m)
    (grad_mid, e_mine, e_other, grad_att, *sums) = middle_back(
        coords, cotangent, middle, after(grad_normed_two, parts[-1]), gain_two, out_full
    )
    grad_gain_two, grad_bias_two, grad_bias_out, grad_bias_down = (v.reshape(-1) for v in sums)
    e_got = exchange(e_other)
    top = outcome(middle, after(act, grad_mid), down_full, bias_down, None, 0, 2)
    done = sum_down.step(top)
    parts = weight_grad_both(
        coords,
        scales,
        [
            (normed_two, got_two, [(after(dh_mine, done), dh_got)]),
            (att, got_att, [(e_mine, e_got)]),
        ],
        nz, m, "grad_up_out", 17,
    )
    done = sum_down.step(parts[0])
    sum_up = Reduction([parts[0]] + [after(part, done) for part in parts[1:]], perms, nz, m)
    mine_one, other_one = attention_back(coords, project, probs, after(grad_att, done), 0)
    one_got = exchange(other_one, sum_down.got[0], *sum_down.got[2:])
    mine_two, other_two = attention_back(coords, project, probs, after(grad_att, mine_one, sum_down.got[0], *sum_down.got[2:]), 1)
    two_got = exchange(other_two, sum_down.got[1])
    done = sum_up.step(mine_two)
    parts = weight_grad_both(
        coords,
        scales,
        [(normed_one, got_one, [(after(mine_one, done), one_got), (mine_two, two_got)])],
        nz, m, "grad_qkv", 14,
    )
    done = sum_up.step(parts[0])
    sum_one = Reduction([parts[0]] + [after(part, done) for part in parts[1:]], perms, nz, m)

    tokens_grad, *sums = input_back(coords, tokens, grad_mid, [mine_one, other_one, mine_two, other_two], after(qkv_full, done), gain_one)
    done = sum_one.step(tokens_grad, sum_up.got[0])
    sums = after_all(sums, done)
    grad_gain_one, grad_bias_one = sums[0].reshape(-1), sums[1].reshape(-1)
    sums = sums[2].reshape(2, 2, 3, quarter)
    sums = jnp.where(core == 0, sums, sums[:, ::-1]).transpose(2, 0, 1, 3)
    grad_bias_query = sums[0].reshape(-1)
    grad_bias_value = sums[2].reshape(-1)

    grad_small = jnp.concatenate(
        [
            grad_gain_one, grad_bias_one, grad_bias_query, grad_bias_value, grad_bias_out,
            grad_gain_two, grad_bias_two, grad_bias_up, grad_bias_down,
        ]
    )
    grad_small = mine * grad_small.reshape(n, -1)

    low = outcome(middle, after(act, done), down_full, bias_down, top, 1, 2)
    done = sum_one.step(low)
    grad_small = lax.all_to_all(
        after(jnp.concatenate([grad_small, grad_small]), done, sum_one.got[0]), BOTH, 0, 0, tiled=True
    )
    half_up = sum_up.step(done)
    half_down = sum_down.step(done)
    block_output = low
    half_qkv = sum_one.step(half_up, half_down)
    merged_small = jnp.sum(after(grad_small, half_qkv), 0)
    hu = hidden // 2

    lows = [piece.astype(BF) for piece in (half_qkv, half_up, half_down)]
    small_sq = jnp.where(core == 0, jnp.sum(merged_small * merged_small), 0.0)
    local_sq = sum((jnp.sum(jnp.square(piece.astype(F32))) for piece in lows)) + small_sq
    everyone = 2 * n
    shared = lax.all_to_all(jnp.full((everyone, 128), local_sq, F32), BOTH, 0, 0, tiled=True)
    total_sq = jnp.sum(shared[:, 0])
    got = [lax.ppermute(low, "grp", SWAP) for low in lows]
    clip = jnp.minimum(1.0, CLIP * lax.rsqrt(total_sq))
    news = update(
        coords,
        clip.reshape(1),
        lows,
        got,
        (qkv_weight, out_weight, up_weight, down_weight),
        (qkv_first, out_first, up_first, down_first),
        (qkv_second, out_second, up_second, down_second),
    )
    small = adam(small_params, small_first, small_second, merged_small * clip, 0.0, RATE_SMALL)
    return (
        block_output,
        tokens_grad,
        *news[0:4],
        small[0],
        *news[4:8],
        small[1],
        *news[8:12],
        small[2],
        total_sq,
    )


def solution(mesh):
    token, flat, row, vec = P(BOTH, None), P(BOTH), P("fsdp", None), P("fsdp")
    params = (row, row, row, row, vec)
    return jax.shard_map(
        shards,
        mesh=mesh,
        in_specs=(token, token, flat, P()) + params * 3,
        out_specs=(token, token) + params * 3 + (P(),),
        check_vma=False,
    )
```

```python
import math

import jax
import jax.numpy as jnp
from jax import lax
from jax.experimental import pallas as pl
from jax.experimental.pallas import tpu as pltpu
from jax.sharding import PartitionSpec as P

HD = 64
STEP = 10
EPS_NORM = 1e-06
CLIP = 1.0
RATE = 0.04
RATE_SMALL = 0.25
DECAY = 0.05
BETA_ONE = 0.9
BETA_TWO = 0.999
EPS_ADAM = 1e-08
F32 = jnp.float32
BF = jnp.bfloat16
BOTH = ("grp", "fsdp")
SWAP = [(0, 1), (1, 0)]
ANY = pl.BlockSpec(memory_space=pl.ANY)
SMEM = pl.BlockSpec(memory_space=pltpu.SMEM)
TILE = 128

RATIO = 0.1


def cost(us):
    return pl.CostEstimate(flops=int(us * RATIO * 1e9), bytes_accessed=0, transcendentals=0)


VMEM = pl.BlockSpec(memory_space=pltpu.VMEM)
SPAN = 256


def dims(n):
    m = max(1, math.isqrt(n // 4))
    return n // (m * m), m


def build_perms(n):
    nz, m = dims(n)

    def chip(z, y, x):
        return (z % nz) * m * m + (y % m) * m + x % m

    def build(move):
        return [
            (c * n + chip(z, y, x), c * n + chip(*move(c, z, y, x)))
            for c in range(2)
            for z in range(nz)
            for y in range(m)
            for x in range(m)
        ]

    return {
        "z": [build(lambda c, z, y, x: (z + k, y, x)) for k in range(nz)],
        "zx": [build(lambda c, z, y, x: (z ^ k, y, x)) for k in range(nz)],
        "a": [build(lambda c, z, y, x: (z, y, x + k) if c == 0 else (z, y + k, x)) for k in range(m)],
        "b": [build(lambda c, z, y, x: (z, y + k, x) if c == 0 else (z, y, x + k)) for k in range(m)],
        "x": [build(lambda c, z, y, x: (z, y, x + k)) for k in range(m)],
        "y": [build(lambda c, z, y, x: (z, y + k, x)) for k in range(m)],
    }


def send(value, table):
    return lax.ppermute(value, BOTH, table)


def layer_norm(x, gain, bias):
    mean = jnp.mean(x, -1, keepdims=True)
    centred = x - mean
    var = jnp.mean(centred * centred, -1, keepdims=True)
    return centred * lax.rsqrt(var + EPS_NORM) * gain + bias


def unpack(small, width, hidden):
    pieces = [small[i * width : (i + 1) * width] for i in range(7)]
    return pieces + [small[7 * width : 7 * width + hidden], small[7 * width + hidden :]]


def adam(weight, first, second, grad, decay, rate):
    first = BETA_ONE * first + (1.0 - BETA_ONE) * grad
    second = BETA_TWO * second + (1.0 - BETA_TWO) * grad * grad
    step_size = (
        first / (1.0 - BETA_ONE**STEP) / (jnp.sqrt(second / (1.0 - BETA_TWO**STEP)) + EPS_ADAM)
    )
    return (weight - rate * (step_size + decay * weight), first, second)


def after(value, *deps):
    return lax.optimization_barrier((value, *deps))[0]


def after_all(values, *deps):
    return lax.optimization_barrier((*values, *deps))[: len(values)]


def stacked(parts):
    def kernel(*refs):
        out, sems = refs[-2:]
        copies = [
            pltpu.make_async_copy(ref, out.at[k], sems.at[k]) for k, ref in enumerate(refs[: len(parts)])
        ]
        for copy in copies:
            copy.start()
        for copy in copies:
            copy.wait()

    return pl.pallas_call(
        kernel,
        out_shape=jax.ShapeDtypeStruct((len(parts),) + parts[0].shape, parts[0].dtype),
        in_specs=[ANY] * len(parts),
        out_specs=VMEM,
        scratch_shapes=[pltpu.SemaphoreType.DMA((len(parts),))],
        compiler_params=pltpu.CompilerParams(vmem_limit_bytes=60 << 20),
        cost_estimate=cost(0),
        name="stacked",
    )(*parts)


class Gather:
    def __init__(self, perms, nz, m):
        self.perms, self.nz, self.m = perms, nz, m

    def first(self, start, *hold):
        got = [send(start, self.perms["a"][k]) for k in range(1, self.m)]
        if hold:
            return stacked([after(start, *hold)] + got)
        return jnp.stack([start] + got)

    def second(self, part, *deps):
        held = after(part, *deps) if deps else part
        return [part] + [send(held, self.perms["b"][k]) for k in range(1, self.m)]

    def swapped(self, parts, *deps):
        deps = deps or [None] * len(parts)
        first, last = deps[0], deps[-1]
        return [
            lax.ppermute(p if dep is None else after(p, dep), "grp", SWAP)
            for p, dep in zip(parts, [first] + [last] * (len(parts) - 1))
        ]

    def far_start(self, own, *hold):
        came = send(own, self.perms["zx"][1])
        return jnp.concatenate([after(own, *hold) if hold else own, came])

    def far(self, got, deps, hold=()):
        step = 2
        while step < self.nz:
            came = send(after(got, *deps), self.perms["zx"][step])
            got = jnp.concatenate([after(got, *hold) if hold else got, came])
            step *= 2
        return got[1:]

    def sources(self, column, near, near_got, wide, wide_got):
        found = []
        for side, (close, parts) in enumerate(((near, wide), (near_got, wide_got))):
            for ib in range(self.m):
                found.append((close[ib], column, side, [((ia,), 0, ia, ib) for ia in range(self.m)]))
                pieces = [((ia, k - 1), k, ia, ib) for ia in range(self.m) for k in range(1, self.nz)]
                found.append((parts[ib], 0, side, pieces))
        return found


def start_pieces(refs, coord, sources, r, m, put, sems):
    z, y, x, c = coord[0], coord[1], coord[2], coord[3]
    for side in range(2):
        core = c if side == 0 else 1 - c
        for ref, (_, base, at, pieces) in zip(refs, sources):
            if at != side:
                continue
            for index, dz, ia, ib in pieces:
                px = lax.rem(x - jnp.where(core == 0, ia, ib) + m, m)
                py = lax.rem(y - jnp.where(core == 0, ib, ia) + m, m)
                chip = (jnp.bitwise_xor(z, dz) * m + py) * m + px
                src = ref.at[index]
                for dst, scol, cols in put(chip, core):
                    pltpu.make_async_copy(src.at[:, pl.ds(base + scol, cols)], dst, sems.at[side]).start()


def wait_bytes(ref, sem):
    pltpu.make_async_copy(ref, ref, sem).wait()


def aligned_rows(row, r):
    return pl.ds(pl.multiple_of(row, 16), r)


def aligned_cols(col, cols):
    return pl.ds(pl.multiple_of(col, 128), cols)


def pack(coords, qkv, out, up, down, width):
    r = qkv.shape[0]
    quarter, half, wide = width // 4, width // 2, up.shape[1] // 2
    ratio = down.shape[0] // r
    groups = [6 * quarter + half, wide, ratio * half]

    def kernel(coord, q_ref, o_ref, u_ref, d_ref, *outs):
        c = coord[3]

        def store(group, col, value):
            low = value.astype(BF)
            cols = low.shape[1]
            at = sum(groups[:group]) + col
            outs[0][0, :, at : at + cols] = low
            at -= groups[0] if group else 0
            outs[2 if group else 1][0, :, at : at + cols] = low

        for hh in range(2):
            for t in range(3):
                cols = aligned_cols(t * width + hh * half + c * quarter, quarter)
                store(0, (hh * 3 + t) * quarter, q_ref[:, cols])
        store(0, 6 * quarter, o_ref[:, aligned_cols(c * half, half)])
        store(1, 0, u_ref[:, aligned_cols(c * wide, wide)])
        for i in range(ratio):
            store(2, i * half, d_ref[i * r : (i + 1) * r, aligned_cols(c * half, half)])

    return pl.pallas_call(
        kernel,
        out_shape=[jax.ShapeDtypeStruct((1, r, cols), BF)
            for cols in (sum(groups), groups[0], groups[1] + groups[2])
        ],
        in_specs=[SMEM] + [VMEM] * 4,
        out_specs=[VMEM] * 3,
        compiler_params=pltpu.CompilerParams(vmem_limit_bytes=60 << 20),
        cost_estimate=cost(4),
        name="pack",
    )(coords, qkv, out, up, down)


def project_qkv(coords, sources, normed, bias, r, m):
    rows, width = normed.shape
    part = 3 * width // 4
    block = min(256, rows)
    steps = rows // block

    def kernel(coord, a_ref, b_ref, *refs):
        out_ref, w_out, w_ref, sems, osem = refs[-5:]
        i = pl.program_id(0)

        @pl.when(i == 0)
        def _():
            def put(chip, core):
                return [
                    (w_ref.at[core, hh, aligned_rows(chip * r, r), :], hh * part, part)
                    for hh in range(2)
                ]

            start_pieces(refs, coord, sources, r, m, put, sems)

        for side in range(2):
            core = coord[3] if side == 0 else 1 - coord[3]

            @pl.when(i == 0)
            def _():
                wait_bytes(w_ref.at[0], sems.at[side])
                for hh in range(2):
                    cols = aligned_cols((hh * 2 + core) * part, part)
                    pltpu.make_async_copy(w_ref.at[core, hh], w_out.at[:, cols], osem).start()

            for hh in range(2):
                cols = aligned_cols((hh * 2 + core) * part, part)
                out = jnp.dot(a_ref[...], w_ref[core, hh], preferred_element_type=F32)
                out_ref[:, cols] = (out + b_ref[:, cols]).astype(BF)

        @pl.when(i == steps - 1)
        def _():
            wait_bytes(w_ref, osem)

    return pl.pallas_call(
        kernel,
        grid=(steps,),
        out_shape=[
            jax.ShapeDtypeStruct((rows, 3 * width), BF),
            jax.ShapeDtypeStruct((width, 3 * width), BF),
        ],
        in_specs=[
            SMEM,
            pl.BlockSpec((block, width), lambda i: (i, 0)),
            pl.BlockSpec((1, 3 * width), lambda i: (0, 0)),
        ]
        + [ANY] * len(sources),
        out_specs=[pl.BlockSpec((block, 3 * width), lambda i: (i, 0)), ANY],
        scratch_shapes=[
            pltpu.VMEM((2, 2, width, part), BF),
            pltpu.SemaphoreType.DMA((2,)),
            pltpu.SemaphoreType.DMA,
        ],
        compiler_params=pltpu.CompilerParams(vmem_limit_bytes=60 << 20),
        cost_estimate=cost(10),
        name="project_qkv",
    )(coords, normed, bias.reshape(1, -1), *[source[0] for source in sources])


def project_out(coords, sources, att, tokens, bias, gain_two, bias_two, r, m, first):
    rows, width = att.shape
    half = width // 2
    block = min(128, rows)
    steps = rows // block

    def kernel(coord, a_ref, t_ref, b_ref, g_ref, c_ref, *refs):
        mid_ref, norm_ref, w_out, w_ref, sems, osem = refs[-6:]
        i = pl.program_id(0)

        @pl.when(i == 0)
        def _():
            def put(chip, core):
                return [
                    (w_ref.at[aligned_rows(chip * r, r), aligned_cols(core * half, half)], first, half)
                ]

            start_pieces(refs, coord, sources, r, m, put, sems)
            for side in range(2):
                wait_bytes(w_ref.at[:, pl.ds(0, half)], sems.at[side])
            pltpu.make_async_copy(w_ref, w_out, osem).start()

        mid = (
            t_ref[...].astype(F32)
            + jnp.dot(a_ref[...], w_ref[...], preferred_element_type=F32)
            + b_ref[...]
        )
        mid_ref[...] = mid
        norm_ref[...] = layer_norm(mid, g_ref[...], c_ref[...]).astype(BF)

        @pl.when(i == steps - 1)
        def _():
            wait_bytes(w_ref, osem)

    tile = pl.BlockSpec((block, width), lambda i: (i, 0))
    line = pl.BlockSpec((1, width), lambda i: (0, 0))
    return pl.pallas_call(
        kernel,
        grid=(steps,),
        out_shape=[
            jax.ShapeDtypeStruct((rows, width), F32),
            jax.ShapeDtypeStruct((rows, width), BF),
            jax.ShapeDtypeStruct((width, width), BF),
        ],
        in_specs=[SMEM, tile, tile, line, line, line] + [ANY] * len(sources),
        out_specs=[tile, tile, ANY],
        scratch_shapes=[
            pltpu.VMEM((width, width), BF),
            pltpu.SemaphoreType.DMA((2,)),
            pltpu.SemaphoreType.DMA,
        ],
        compiler_params=pltpu.CompilerParams(vmem_limit_bytes=60 << 20),
        cost_estimate=cost(8),
        name="project_out",
    )(
        coords, att, tokens, bias.reshape(1, -1), gain_two.reshape(1, -1), bias_two.reshape(1, -1),
        *[source[0] for source in sources],
    )


def weight_grad(coords, scale, pairs, nz, m, name, us):
    tokens, total = pairs[0][0].shape
    halves = [right.shape[1] // 2 for _, right in pairs]
    cols = sum(halves)
    r = total // (nz * m * m)
    zrows = total // nz
    mt = min(1024, zrows)
    mc = zrows // mt
    count = len(pairs)

    def kernel(coord, scale_ref, *refs):
        x_hbm = refs[0 : 2 * count : 2]
        y_hbm = refs[1 : 2 * count : 2]
        outs = refs[2 * count : 2 * count + 2]
        scratch = refs[2 * count + 2 :]
        xv = scratch[0:count]
        yv = scratch[count : 2 * count]
        acc, xsem, ysem, osem = scratch[2 * count :]
        z, y, x, c = coord[0], coord[1], coord[2], coord[3]
        weight = scale_ref[0]

        def xcopy(p, dz, i):
            pz = lax.rem(z + dz, nz)
            return pltpu.make_async_copy(
                x_hbm[p].at[:, pl.ds(pl.multiple_of(pz * zrows + i * mt, 128), mt)],
                xv[p].at[dz * mc + i],
                xsem.at[p, dz * mc + i],
            )

        def ycopy(p, side):
            owner = c if side == 0 else 1 - c
            return pltpu.make_async_copy(
                y_hbm[p].at[:, pl.ds(pl.multiple_of(owner * halves[p], 128), halves[p])],
                yv[p].at[:, aligned_cols(owner * halves[p], halves[p])],
                ysem.at[p, side],
            )

        for p in range(count):
            xcopy(p, 0, 0).start()
            ycopy(p, 1).start()
            ycopy(p, 0).start()
        for p in range(count):
            for dz in range(nz):
                for i in range(mc):
                    if dz or i:
                        xcopy(p, dz, i).start()
        copies = []
        for dz in range(nz):
            for i in range(mc):
                for p in range(count):
                    low = sum(halves[:p])
                    xcopy(p, dz, i).wait()
                    left = xv[p][dz * mc + i].T
                    if dz == 0 and i == 0:
                        ycopy(p, 1).wait()
                        ycopy(p, 0).wait()
                    both = jnp.dot(left, yv[p][...], preferred_element_type=F32) * weight
                    acc[dz, i * mt : (i + 1) * mt, :] = both.astype(BF)
            for side in (1, 0):
                owner = c if side == 0 else 1 - c
                for ib in range(m):
                    for ia in range(m):
                        dx = jnp.where(owner == 0, ia, ib)
                        dy = jnp.where(owner == 0, ib, ia)
                        px = lax.rem(x + dx, m)
                        py = lax.rem(y + dy, m)
                        copy = pltpu.make_async_copy(
                            acc.at[dz, aligned_rows((py * m + px) * r, r), aligned_cols(owner * cols, cols)],
                            outs[side].at[ib, ia, dz],
                            osem.at[side, dz, ib * m + ia],
                        )
                        copy.start()
                        copies.append(copy)
        for copy in copies:
            copy.wait()

    return pl.pallas_call(
        kernel,
        out_shape=[jax.ShapeDtypeStruct((m, m, nz, r, cols), BF)] * 2,
        in_specs=[SMEM, SMEM] + [ANY] * (2 * count),
        out_specs=[ANY] * 2,
        scratch_shapes=[pltpu.VMEM((nz * mc, tokens, mt), BF) for _ in pairs]
        + [pltpu.VMEM((tokens, 2 * h), BF) for h in halves]
        + [
            pltpu.VMEM((nz, zrows, 2 * cols), BF),
            pltpu.SemaphoreType.DMA((count, nz * mc)),
            pltpu.SemaphoreType.DMA((count, 2)),
            pltpu.SemaphoreType.DMA((2, nz, m * m)),
        ],
        compiler_params=pltpu.CompilerParams(vmem_limit_bytes=60 << 20),
        cost_estimate=cost(us),
        name=name,
    )(coords, scale, *[v for pair in pairs for v in pair])


def weight_grad_both(coords, scales, pairs, nz, m, name, us):
    tokens, total = pairs[0][0].shape
    widths = [[own.shape[1] for own, _ in pair[2]] for pair in pairs]
    halves = [sum(w) for w in widths]
    cols = sum(halves)
    r = total // (nz * m * m)
    zrows = total // nz
    count = len(pairs)
    group = 2 if nz % 2 == 0 else 1
    operands, places = [], []
    for pair in pairs:
        places.append(len(operands))
        operands += [*pair[:2], *[v for both in pair[2] for v in both]]

    def kernel(coord, scale_ref, *refs):
        ins = refs[: len(operands)]
        outs = refs[len(operands) : len(operands) + m]
        scratch = refs[len(operands) + m :]
        held = scratch[: 4 * count]
        acc, xsem, ysem, osem = scratch[4 * count :]
        z, y, x, c = coord[0], coord[1], coord[2], coord[3]

        def xcopy(p, who, dz):
            pz = lax.rem(z + dz, nz)
            return pltpu.make_async_copy(
                ins[places[p] + who].at[:, pl.ds(pl.multiple_of(pz * zrows, 128), zrows)],
                held[4 * p + who].at[dz],
                xsem.at[p, who, dz],
            )

        def ycopies(p, who):
            dst = held[4 * p + 2 + who]
            found = []
            for k, h in enumerate(widths[p]):
                at = pl.ds(sum(widths[p][:k]), h)
                src = ins[places[p] + 2 + 2 * k + who]
                found.append(pltpu.make_async_copy(src, dst.at[:, at], ysem.at[p, who, k]))
            return found

        for p in range(count):
            for who in range(2):
                xcopy(p, who, 0).start()
                for copy in ycopies(p, who):
                    copy.start()
        for p in range(count):
            for dz in range(1, nz):
                for who in range(2):
                    xcopy(p, who, dz).start()
        copies = []
        for dz in range(nz):
            for p in range(count):
                low = sum(halves[:p])
                if dz % group:
                    continue
                out = None
                for who in range(2):
                    for k in range(group):
                        xcopy(p, who, dz + k).wait()
                    if dz == 0:
                        for copy in ycopies(p, who):
                            copy.wait()
                    left = jnp.concatenate([held[4 * p + who][dz + k].T for k in range(group)], 0)
                    part = jnp.dot(left, held[4 * p + 2 + who][...], preferred_element_type=F32)
                    part = part * scale_ref[who]
                    out = part if out is None else out + part
                out = out.astype(BF)
                for k in range(group):
                    acc[dz + k, :, low : low + halves[p]] = out[k * zrows : (k + 1) * zrows]
            for ib in range(m):
                for ia in range(m):
                    px = lax.rem(x + jnp.where(c == 0, ia, ib), m)
                    py = lax.rem(y + jnp.where(c == 0, ib, ia), m)
                    copy = pltpu.make_async_copy(
                        acc.at[dz, aligned_rows((py * m + px) * r, r), :],
                        outs[ib].at[ia, dz],
                        osem.at[dz, ib * m + ia],
                    )
                    copy.start()
                    copies.append(copy)
        for copy in copies:
            copy.wait()

    shapes = []
    for h in halves:
        shapes += [pltpu.VMEM((nz, tokens, zrows), BF)] * 2 + [pltpu.VMEM((tokens, h), BF)] * 2
    return pl.pallas_call(
        kernel,
        out_shape=[jax.ShapeDtypeStruct((m, nz, r, cols), BF)] * m,
        in_specs=[SMEM, SMEM] + [ANY] * len(operands),
        out_specs=[ANY] * m,
        scratch_shapes=shapes
        + [
            pltpu.VMEM((nz, zrows, cols), BF),
            pltpu.SemaphoreType.DMA((count, 2, nz)),
            pltpu.SemaphoreType.DMA((count, 2, max(len(w) for w in widths))),
            pltpu.SemaphoreType.DMA((nz, m * m)),
        ],
        compiler_params=pltpu.CompilerParams(vmem_limit_bytes=60 << 20),
        cost_estimate=cost(us),
        name=name,
    )(coords, scales, *operands)


def add_parts(keep, got):
    size, cols = keep.shape[0], keep.shape[-1]
    shape = keep.shape[1:]
    flat = math.prod(shape[:-1])
    most = 1 << (20 if size * flat * cols > 1200000 else 19)
    block = max(16, min(flat, most // (size * cols) // 16 * 16))
    while flat % block:
        block -= 16
    count = len(got) + 1

    def kernel(*refs):
        for k in range(size):
            total = refs[0][k].astype(F32)
            for ref in refs[1:count]:
                total += ref[k].astype(F32)
            refs[count + k][...] = total.astype(BF)

    outs = pl.pallas_call(
        kernel,
        grid=(flat // block,),
        out_shape=[jax.ShapeDtypeStruct((flat, cols), BF)] * size,
        in_specs=[pl.BlockSpec((size, block, cols), lambda i: (0, i, 0))] * count,
        out_specs=[pl.BlockSpec((block, cols), lambda i: (i, 0))] * size,
        compiler_params=pltpu.CompilerParams(vmem_limit_bytes=60 << 20),
        cost_estimate=cost(2),
        name="add_parts",
    )(*[v.reshape(size, flat, cols) for v in [keep, *got]])
    return [out.reshape(shape) for out in outs]


class Reduction:
    def __init__(self, parts, perms, nz, m):
        self.perms, self.sizes = perms, {"b": m, "a": m, "z": nz}
        self.left = ["a", "z"]
        self.pass_on("b", parts)

    def pass_on(self, axis, parts):
        self.keep = parts[0]
        self.got = [send(parts[k], self.perms[axis][k]) for k in range(1, self.sizes[axis])]

    def step(self, *deps):
        if not self.left:
            t = after(self.keep, *deps).astype(F32) if deps else self.keep.astype(F32)
            for part in self.got:
                t = t + part.astype(F32)
            return t
        axis = self.left.pop(0)
        parts = add_parts(after(self.keep, *deps), self.got)
        self.pass_on(axis, parts)
        return parts[-1]


def feed_up(coords, sources, normed, bias, r, m):
    rows, width = normed.shape
    hidden = bias.shape[0]
    half, cols, step = hidden // 2, 512, 256
    tiles = half // cols

    def kernel(coord, a_ref, b_ref, *refs):
        act_ref, slope_ref, w_out, w_ref, sems, osem = refs[-6:]
        j = pl.program_id(0)

        @pl.when(j == 0)
        def _():
            def put(chip, core):
                return [(w_ref.at[core, aligned_rows(chip * r, r), :], 0, half)]

            start_pieces(refs, coord, sources, r, m, put, sems)

        for side in range(2):

            @pl.when(j == side * tiles)
            def _():
                wait_bytes(w_ref.at[0], sems.at[side])
                core = coord[3] if side == 0 else 1 - coord[3]
                at = aligned_cols(core * half, half)
                pltpu.make_async_copy(w_ref.at[core], w_out.at[:, at], osem).start()

        @pl.when(j == 2 * tiles - 1)
        def _():
            wait_bytes(w_ref, osem)

        core = jnp.where(j < tiles, coord[3], 1 - coord[3])
        weight = w_ref[core, :, aligned_cols(lax.rem(j, tiles) * cols, cols)]
        c0, c1 = math.sqrt(2.0 / math.pi), 0.044715
        for i in range(0, rows, step):
            h = jnp.dot(a_ref[i : i + step, :], weight, preferred_element_type=F32) + b_ref[...]
            square = h * h
            gate = 0.5 + 0.5 * jnp.tanh(h * (c0 + (c0 * c1) * square))
            act = h * gate
            act_ref[i : i + step, :] = act.astype(BF)
            slope = gate + (act - act * gate) * (2.0 * c0 + (6.0 * c0 * c1) * square)
            slope_ref[i : i + step, :] = slope.astype(BF)

    def tile(j, coord):
        return (0, jnp.where(j < tiles, coord[3], 1 - coord[3]) * tiles + lax.rem(j, tiles))

    grid_spec = pltpu.PrefetchScalarGridSpec(
        num_scalar_prefetch=1,
        grid=(2 * tiles,),
        in_specs=[
            pl.BlockSpec((rows, width), lambda j, coord: (0, 0)),
            pl.BlockSpec((1, cols), tile),
        ]
        + [ANY] * len(sources),
        out_specs=[
            pl.BlockSpec((rows, cols), tile),
            pl.BlockSpec((rows, cols), tile),
            ANY,
        ],
        scratch_shapes=[
            pltpu.VMEM((2, width, half), BF),
            pltpu.SemaphoreType.DMA((2,)),
            pltpu.SemaphoreType.DMA,
        ],
    )
    return pl.pallas_call(
        kernel,
        grid_spec=grid_spec,
        out_shape=[
            jax.ShapeDtypeStruct((rows, hidden), BF),
            jax.ShapeDtypeStruct((rows, hidden), BF),
            jax.ShapeDtypeStruct((width, hidden), BF),
        ],
        compiler_params=pltpu.CompilerParams(vmem_limit_bytes=60 << 20),
        cost_estimate=cost(25),
        name="feed_up",
    )(coords, normed, bias.reshape(1, hidden), *[source[0] for source in sources])


def feed_back(coords, sources, grad, slope, up, r, m, ratio):
    rows, width = grad.shape
    hidden = up.shape[1]
    half, cols, step = width // 2, 512, 512
    tiles = hidden // cols

    def tile_at(j, coord):
        core = jnp.where(j < tiles // 2, coord[3], 1 - coord[3])
        return core * (tiles // 2) + lax.rem(j, tiles // 2)

    def kernel(coord, g_ref, s_ref, u_ref, *refs):
        mine_ref, other_ref, sum_ref, out_ref, d_out, d_ref, dh_ref, sems, osems = refs[-9:]
        j = pl.program_id(0)

        @pl.when(j == 0)
        def _():
            out_ref[...] = jnp.zeros_like(out_ref)

            def put(chip, core):
                return [
                    (
                        d_ref.at[
                            aligned_rows((chip * ratio + s) * r, r), aligned_cols(core * half, half)
                        ],
                        s * half,
                        half,
                    )
                    for s in range(ratio)
                ]

            start_pieces(refs, coord, sources, r, m, put, sems)
            for side in range(2):
                wait_bytes(d_ref.at[:, pl.ds(0, half)], sems.at[side])
            pltpu.make_async_copy(d_ref, d_out, osems.at[2]).start()

        slot = lax.rem(j, 2)

        @pl.when(j >= 2)
        def _():
            wait_bytes(dh_ref.at[0], osems.at[slot])

        down = d_ref[pl.ds(pl.multiple_of(tile_at(j, coord) * cols, cols), cols), :]
        total = jnp.zeros((1, cols), F32)
        for i in range(0, rows, step):
            part = lax.dot_general(
                g_ref[i : i + step, :], down, (((1,), (1,)), ((), ())), preferred_element_type=F32
            )
            dh = (part * s_ref[i : i + step, :].astype(F32)).astype(BF)
            dh_ref[slot, i : i + step, :] = dh
            total += jnp.sum(dh.astype(F32), 0, keepdims=True)
            out_ref[i : i + step, :] += lax.dot_general(
                dh, u_ref[...], (((1,), (1,)), ((), ())), preferred_element_type=F32
            )
        sum_ref[...] = total

        def copy_out(ref):
            at = aligned_cols(lax.rem(j, tiles // 2) * cols, cols)
            pltpu.make_async_copy(dh_ref.at[slot], ref.at[:, at], osems.at[slot]).start()

        @pl.when(j < tiles // 2)
        def _():
            copy_out(mine_ref)

        @pl.when(j >= tiles // 2)
        def _():
            copy_out(other_ref)

        @pl.when(j == tiles - 1)
        def _():
            for at in range(2):
                wait_bytes(dh_ref.at[0], osems.at[at])
            wait_bytes(d_ref, osems.at[2])

    grid_spec = pltpu.PrefetchScalarGridSpec(
        num_scalar_prefetch=1,
        grid=(tiles,),
        in_specs=[
            pl.BlockSpec((rows, width), lambda j, coord: (0, 0)),
            pl.BlockSpec((rows, cols), lambda j, coord: (0, tile_at(j, coord))),
            pl.BlockSpec((width, cols), lambda j, coord: (0, tile_at(j, coord))),
        ]
        + [ANY] * len(sources),
        out_specs=[
            ANY,
            ANY,
            pl.BlockSpec((1, cols), lambda j, coord: (0, tile_at(j, coord))),
            pl.BlockSpec((rows, width), lambda j, coord: (0, 0)),
            ANY,
        ],
        scratch_shapes=[
            pltpu.VMEM((hidden, width), BF),
            pltpu.VMEM((2, rows, cols), BF),
            pltpu.SemaphoreType.DMA((2,)),
            pltpu.SemaphoreType.DMA((3,)),
        ],
    )
    return pl.pallas_call(
        kernel,
        grid_spec=grid_spec,
        out_shape=[
            jax.ShapeDtypeStruct((rows, hidden // 2), BF),
            jax.ShapeDtypeStruct((rows, hidden // 2), BF),
            jax.ShapeDtypeStruct((1, hidden), F32),
            jax.ShapeDtypeStruct((rows, width), F32),
            jax.ShapeDtypeStruct((hidden, width), BF),
        ],
        compiler_params=pltpu.CompilerParams(vmem_limit_bytes=60 << 20),
        cost_estimate=cost(50),
        name="feed_back",
    )(coords, grad, slope, up, *[source[0] for source in sources])


def norm_back(x, grad, gain):
    mean = jnp.mean(x, -1, keepdims=True)
    centred = x - mean
    inv = lax.rsqrt(jnp.mean(centred * centred, -1, keepdims=True) + EPS_NORM)
    hat = centred * inv
    inner = grad * gain
    back = inv * (
        inner
        - jnp.mean(inner, -1, keepdims=True)
        - hat * jnp.mean(inner * hat, -1, keepdims=True)
    )
    return back, jnp.sum(grad * hat, 0, keepdims=True), jnp.sum(grad, 0, keepdims=True)


def middle_back(coords, cotangent, middle, grad, gain, out):
    rows, width = middle.shape
    block = min(256, rows)

    half = width // 2

    def kernel(coord, c_ref, m_ref, d_ref, g_ref, w_ref, *refs):
        dy_ref, mine_ref, other_ref, a_ref, gain_ref, bias_ref, bo_ref, bd_ref, e_ref = refs

        @pl.when(pl.program_id(0) == 0)
        def _():
            for ref in (gain_ref, bias_ref, bo_ref, bd_ref):
                ref[...] = jnp.zeros_like(ref)

        cot = c_ref[...].astype(F32)
        back, for_gain, for_bias = norm_back(m_ref[...], d_ref[...], g_ref[...])
        dy = cot + back
        low = dy.astype(BF)
        dy_ref[...] = dy
        e_ref[...] = low
        mine_ref[...] = e_ref[:, aligned_cols(coord[3] * half, half)]
        other_ref[...] = e_ref[:, aligned_cols((1 - coord[3]) * half, half)]
        a_ref[...] = lax.dot_general(
            low, w_ref[...], (((1,), (1,)), ((), ())), preferred_element_type=F32
        ).astype(BF)
        gain_ref[...] += for_gain
        bias_ref[...] += for_bias
        bo_ref[...] += jnp.sum(low.astype(F32), 0, keepdims=True)
        bd_ref[...] += jnp.sum(cot, 0, keepdims=True)

    tile = pl.BlockSpec((block, width), lambda i: (i, 0))
    part = pl.BlockSpec((block, half), lambda i: (i, 0))
    line = pl.BlockSpec((1, width), lambda i: (0, 0))
    return pl.pallas_call(
        kernel,
        grid=(rows // block,),
        out_shape=[
            jax.ShapeDtypeStruct((rows, cols), t)
            for cols, t in ((width, F32), (half, BF), (half, BF), (width, BF))
        ]
        + [jax.ShapeDtypeStruct((1, width), F32)] * 4,
        in_specs=[SMEM, tile, tile, tile, line, pl.BlockSpec((width, width), lambda i: (0, 0))],
        out_specs=[tile, part, part, tile] + [line] * 4,
        scratch_shapes=[pltpu.VMEM((block, width), BF)],
        compiler_params=pltpu.CompilerParams(vmem_limit_bytes=60 << 20),
        cost_estimate=cost(3),
        name="middle_back",
    )(coords, cotangent, middle, grad, gain.reshape(1, -1), out)


def input_back(coords, tokens, grad_mid, parts, weight, gain):
    rows, width = tokens.shape
    total = weight.shape[1]
    block = min(256, rows)
    count = len(parts)
    cols = total // count

    def kernel(coord, t_ref, m_ref, w_ref, g_ref, *refs):
        out_ref, gain_ref, bias_ref, sum_ref = refs[count:]

        @pl.when(pl.program_id(0) == 0)
        def _():
            for ref in (gain_ref, bias_ref, sum_ref):
                ref[...] = jnp.zeros_like(ref)

        grad = jnp.zeros((block, width), F32)
        for p in range(count):
            core = coord[3] if p % 2 == 0 else 1 - coord[3]
            part = refs[p][...]
            sum_ref[:, p * cols : (p + 1) * cols] += jnp.sum(part.astype(F32), 0, keepdims=True)
            weight_at = aligned_cols((p // 2 * 2 + core) * cols, cols)
            grad += lax.dot_general(
                part, w_ref[:, weight_at], (((1,), (1,)), ((), ())), preferred_element_type=F32
            )
        back, for_gain, for_bias = norm_back(t_ref[...].astype(F32), grad, g_ref[...])
        out_ref[...] = (m_ref[...] + back).astype(BF)
        gain_ref[...] += for_gain
        bias_ref[...] += for_bias

    tile = pl.BlockSpec((block, width), lambda i: (i, 0))
    line = pl.BlockSpec((1, width), lambda i: (0, 0))
    return pl.pallas_call(
        kernel,
        grid=(rows // block,),
        out_shape=[
            jax.ShapeDtypeStruct((rows, width), BF),
            jax.ShapeDtypeStruct((1, width), F32),
            jax.ShapeDtypeStruct((1, width), F32),
            jax.ShapeDtypeStruct((1, total), F32),
        ],
        in_specs=[SMEM, tile, tile, pl.BlockSpec((width, total), lambda i: (0, 0)), line]
        + [pl.BlockSpec((block, cols), lambda i: (i, 0))] * count,
        out_specs=[tile, line, line, pl.BlockSpec((1, total), lambda i: (0, 0))],
        compiler_params=pltpu.CompilerParams(vmem_limit_bytes=60 << 20),
        cost_estimate=cost(30),
        name="input_back",
    )(coords, tokens, grad_mid, weight, gain.reshape(1, -1), *parts)


def outcome(middle, act, down, bias, before, part, parts):
    rows, width = middle.shape
    hidden = act.shape[1]
    block = 128
    first = part * (rows // parts // block)

    def kernel(m_ref, a_ref, d_ref, b_ref, *refs):
        out = jnp.dot(a_ref[...], d_ref[...], preferred_element_type=F32)
        refs[-1][...] = (m_ref[...] + out + b_ref[...]).astype(BF)

    more = [] if before is None else [before]
    return pl.pallas_call(
        kernel,
        grid=(rows // parts // block,),
        out_shape=jax.ShapeDtypeStruct((rows, width), BF),
        in_specs=[
            pl.BlockSpec((block, width), lambda i: (first + i, 0)),
            pl.BlockSpec((block, hidden), lambda i: (first + i, 0)),
            pl.BlockSpec((hidden, width), lambda i: (0, 0)),
            pl.BlockSpec((1, width), lambda i: (0, 0)),
        ]
        + [ANY] * len(more),
        out_specs=pl.BlockSpec((block, width), lambda i: (first + i, 0)),
        input_output_aliases={4: 0} if more else {},
        compiler_params=pltpu.CompilerParams(vmem_limit_bytes=60 << 20),
        cost_estimate=cost(3 if part == 0 else 10),
        name="outcome_" + str(part),
    )(middle, act, down, bias.reshape(1, -1), *more)


def head_stack(block, low_lanes):
    zero = jnp.zeros_like(block)
    return jnp.concatenate(
        [jnp.where(low_lanes, block, zero), jnp.where(low_lanes, zero, block)], 0
    )


def window_block(t, rows):
    return jnp.clip(2 * t - 1, 0, rows // 64 - SPAN // 64)


def window_specs(rows, cols, at=0):
    return [
        pl.BlockSpec((64, cols), lambda t, i=i: (window_block(t, rows) + i, at)) for i in range(SPAN // 64)
    ]


def joined_rows(refs, lanes):
    return jnp.concatenate([ref[:, lanes] for ref in refs], 0)


def attention(project, seg_col, seg_row):
    rows, width = project.shape[0], project.shape[1] // 3
    pairs = width // (2 * HD)
    blocks = SPAN // 64

    def pair_lanes(pair, which):
        hh, rest = divmod(pair, pairs // 2)
        core, within = divmod(rest, pairs // 4)
        quarter = width // 4
        first = (hh * 2 + core) * 3 * quarter + which * quarter + within * 2 * HD
        return slice(first, first + 2 * HD)

    def kernel(row_ref, q_ref, *refs):
        cols, windows, (out_ref, probs_ref) = refs[:blocks], refs[blocks : 2 * blocks], refs[2 * blocks :]
        same = joined_rows(cols, slice(0, 1)) == row_ref[...]
        same = jnp.concatenate([same, same], 1)
        low = lax.broadcasted_iota(jnp.int32, (TILE, 2 * HD), 1) < HD
        for h in range(pairs):
            stack = head_stack(q_ref[:, pair_lanes(h, 0)] * HD**-0.5, low)
            keys = joined_rows(windows, pair_lanes(h, 1))
            scores = lax.dot_general(keys, stack, (((1,), (1,)), ((), ())), preferred_element_type=F32)
            scores = jnp.where(same, scores, -1e30)
            expo = jnp.exp(scores - jnp.max(scores, 0, keepdims=True))
            probs = (expo * (1.0 / jnp.sum(expo, 0, keepdims=True))).astype(BF)
            probs_ref[0, h] = probs
            mixed = lax.dot_general(
                probs,
                joined_rows(windows, pair_lanes(h, 2)),
                (((0,), (0,)), ((), ())),
                preferred_element_type=F32,
            )
            out_ref[:, h * 2 * HD : (h + 1) * 2 * HD] = jnp.where(low, mixed[:TILE], mixed[TILE:]).astype(BF)

    return pl.pallas_call(
        kernel,
        grid=(rows // TILE,),
        out_shape=[
            jax.ShapeDtypeStruct((rows, width), BF),
            jax.ShapeDtypeStruct((rows // TILE, pairs, SPAN, 2 * TILE), BF),
        ],
        in_specs=[
            pl.BlockSpec((1, TILE), lambda t: (0, t)),
            pl.BlockSpec((TILE, 3 * width), lambda t: (t, 0)),
        ]
        + window_specs(rows, 1)
        + window_specs(rows, 3 * width),
        out_specs=[
            pl.BlockSpec((TILE, width), lambda t: (t, 0)),
            pl.BlockSpec((1, pairs, SPAN, 2 * TILE), lambda t: (t, 0, 0, 0)),
        ],
        compiler_params=pltpu.CompilerParams(vmem_limit_bytes=60 << 20),
        cost_estimate=cost(14),
        name="attention",
    )(seg_row, project, *[seg_col] * blocks, *[project] * blocks)


def attention_back(coords, project, probs, grad, hh):
    rows, width = project.shape[0], project.shape[1] // 3
    quarter = width // 4
    pairs = width // (2 * HD)
    tiles = rows // TILE
    blocks = SPAN // 64

    def kernel(coord, q_ref, p_ref, g_ref, *refs):
        windows, (mine_ref, other_ref, dk, dv) = refs[:blocks], refs[blocks:]
        t = pl.program_id(0)

        @pl.when(t == 0)
        def _():
            dk[...] = jnp.zeros_like(dk)
            dv[...] = jnp.zeros_like(dv)

        window = pl.ds(pl.multiple_of(window_block(t, rows) * 64, 64), SPAN)
        own = pl.ds(pl.multiple_of(t * TILE, TILE), TILE)
        low = lax.broadcasted_iota(jnp.int32, (TILE, 2 * HD), 1) < HD
        scale = HD**-0.5
        for side, out_ref in enumerate((mine_ref, other_ref)):
            core = coord[3] if side == 0 else 1 - coord[3]
            for within in range(pairs // 4):
                h = within * 2 * HD
                held = slice(side * quarter + h, side * quarter + h + 2 * HD)

                def lanes(which):
                    return aligned_cols(core * 3 * quarter + which * quarter + h, 2 * HD)

                queries = head_stack(q_ref[:, lanes(0)], low)
                grads = head_stack(g_ref[:, aligned_cols(core * quarter + h, 2 * HD)], low)
                soft = p_ref[0, core * (pairs // 4) + within]
                wide = soft.astype(F32)
                grad_probs = lax.dot_general(
                    joined_rows(windows, lanes(2)), grads, (((1,), (1,)), ((), ())),
                    preferred_element_type=F32,
                )
                inner = jnp.sum(wide * grad_probs, 0, keepdims=True)
                grad_scores = (wide * (grad_probs - inner)).astype(BF)
                dv[window, held] += jnp.dot(soft, grads, preferred_element_type=F32)
                dk[window, held] += jnp.dot(grad_scores, queries, preferred_element_type=F32)
                dq = lax.dot_general(
                    grad_scores, joined_rows(windows, lanes(1)), (((0,), (0,)), ((), ())),
                    preferred_element_type=F32,
                )
                out_ref[own, h : h + 2 * HD] = (
                    jnp.where(low, dq[:TILE], dq[TILE:]) * scale
                ).astype(BF)

        @pl.when(t == tiles - 1)
        def _():
            for side, out_ref in enumerate((mine_ref, other_ref)):
                held = slice(side * quarter, (side + 1) * quarter)
                out_ref[:, quarter : 2 * quarter] = (dk[:, held] * scale).astype(BF)
                out_ref[:, 2 * quarter :] = dv[:, held].astype(BF)

    whole = pl.BlockSpec((rows, 3 * quarter), lambda t: (0, 0))
    return pl.pallas_call(
        kernel,
        grid=(tiles,),
        out_shape=[jax.ShapeDtypeStruct((rows, 3 * quarter), BF)] * 2,
        in_specs=[
            SMEM,
            pl.BlockSpec((TILE, 6 * quarter), lambda t: (t, hh)),
            pl.BlockSpec((1, pairs // 2, SPAN, 2 * TILE), lambda t: (t, hh, 0, 0)),
            pl.BlockSpec((TILE, 2 * quarter), lambda t: (t, hh)),
        ]
        + window_specs(rows, 6 * quarter, hh),
        out_specs=[whole, whole],
        scratch_shapes=[pltpu.VMEM((rows, 2 * quarter), F32)] * 2,
        compiler_params=pltpu.CompilerParams(vmem_limit_bytes=60 << 20),
        cost_estimate=cost(16),
        name="attention_back_" + str(hh),
    )(coords, project, probs, grad, *[project] * blocks)


def update(coords, clip, lows, got, weights, firsts, seconds):
    r, width = weights[1].shape
    hidden = weights[2].shape[1]
    ratio = weights[3].shape[0] // r
    quarter, half = width // 4, width // 2
    steps = max(1, r // 16)
    block = r // steps

    def kernel(coord, clip_ref, *refs):
        halves = refs[0:3], refs[3:6]
        olds = refs[6:18]
        news = refs[18:30]
        scale = clip_ref[0]
        for side in range(2):
            core = coord[3] if side == 0 else 1 - coord[3]
            qkv, rest, down = halves[side]

            def put(i, source, first, cols, col):
                at = aligned_cols(col, cols)
                grad = source[:, first : first + cols].astype(F32) * scale
                found = adam(olds[i][:, at], olds[4 + i][:, at], olds[8 + i][:, at], grad, DECAY, RATE)
                for k in range(3):
                    news[4 * k + i][:, at] = found[k]

            for hh in range(2):
                for t in range(3):
                    put(0, qkv, (hh * 3 + t) * quarter, quarter, t * width + hh * half + core * quarter)
            put(1, rest, hidden // 2, half, core * half)
            put(2, rest, 0, hidden // 2, core * (hidden // 2))
            put(3, down, 0, half, core * half)

    def rows_of(v):
        return pl.BlockSpec((v.shape[0] // steps, v.shape[1]), lambda i: (i, 0))

    arrays = [*weights, *firsts, *seconds]
    return pl.pallas_call(
        kernel,
        grid=(steps,),
        out_shape=[jax.ShapeDtypeStruct(v.shape, F32) for v in arrays],
        in_specs=[SMEM, SMEM] + [rows_of(v) for v in (*lows, *got, *arrays)],
        out_specs=[rows_of(v) for v in arrays],
        compiler_params=pltpu.CompilerParams(vmem_limit_bytes=60 << 20),
        cost_estimate=cost(10),
        name="update",
    )(coords, clip, *lows, *got, *arrays)


def shards(
    tokens, cotangent, segment_ids, group_counts,
    qkv_weight, out_weight, up_weight, down_weight, small_params,
    qkv_first, out_first, up_first, down_first, small_first,
    qkv_second, out_second, up_second, down_second, small_second,
):
    width = tokens.shape[1]
    hidden = up_weight.shape[1]
    rows = tokens.shape[0]
    n = lax.axis_size("fsdp")
    nz, m = dims(n)
    perms = build_perms(n)
    chip = lax.axis_index("fsdp")
    core = lax.axis_index("grp")
    z, y, x = chip // (m * m), chip // m % m, chip % m
    coords = jnp.stack([z, y, x, core]).astype(jnp.int32)
    r = qkv_weight.shape[0]
    ratio = down_weight.shape[0] // r

    counts = group_counts.astype(F32)
    share = counts / jnp.sum(counts)
    is_local = core >= lax.axis_size("grp") // 2
    mine = jnp.where(is_local, share[1], share[0])
    scales = jnp.stack([mine, jnp.where(is_local, share[0], share[1])])
    scale = mine.reshape(1)
    quarter = width // 4
    hq, ho = 3 * width // 2, width // 2

    gather = Gather(perms, nz, m)
    piece = jnp.broadcast_to(small_params.astype(BF).astype(F32), (2 * n,) + small_params.shape)
    small_full = lax.all_to_all(piece, BOTH, 0, 0, tiled=True)[:n].reshape(-1)
    packed, own_one, own_rest = pack(
        coords, qkv_weight, out_weight, up_weight, down_weight, width
    )
    columns = [0, own_one.shape[2], own_one.shape[2] + hidden // 2]
    near_a = gather.first(packed[0])
    pair_one = gather.far_start(own_one)
    near = gather.second(near_a, pair_one)
    near_got = gather.swapped(near)
    far_one = gather.far(pair_one, (), (small_full,))
    small_full = after(small_full, *near[1:])
    gain_one, bias_one, bias_query, bias_value, bias_out, gain_two, bias_two, bias_up, bias_down = (
        unpack(small_full, width, hidden)
    )
    normed_one = layer_norm(after(tokens, *near[1:]).astype(F32), gain_one, bias_one).astype(BF)
    qkv_bias = jnp.stack([bias_query, jnp.zeros_like(bias_query), bias_value])
    qkv_bias = qkv_bias.reshape(3, 2, 2, quarter).transpose(1, 2, 0, 3).reshape(-1)
    a_one = gather.first(after(far_one, *near[1:]))
    pair_rest = gather.far_start(after(own_rest, near_a), a_one)
    pair_two, pair_three = pair_rest[:, :, : hidden // 2], pair_rest[:, :, hidden // 2 :]
    wide_one = gather.second(a_one, normed_one, qkv_bias, pair_rest)
    far_two = gather.far(pair_two, (far_one,))
    one = gather.sources(0, near, near_got, wide_one, gather.swapped(wide_one, far_two, a_one))

    def exchange(value, *deps):
        return lax.ppermute(after(value, *deps) if deps else value, "grp", SWAP)

    project, qkv_full = project_qkv(coords, one, after(normed_one, far_two), qkv_bias, r, m)
    a_two = gather.first(after(far_two, wide_one[-1]), project)
    wide_two = gather.second(a_two, project)
    seg_col, seg_row = segment_ids.reshape(rows, 1), segment_ids.reshape(1, rows)
    att, probs = attention(after(project, a_two), seg_col, seg_row)
    far_three = gather.far(pair_three, (far_two,), (att,))
    middle, normed_two, out_full = project_out(
        coords, one, after(att, far_three), tokens, bias_out, gain_two, bias_two, r, m, hq
    )
    a_three = gather.first(after(far_three, att), middle)
    wide_three = gather.second(a_three, middle)
    two = gather.sources(columns[1], near, near_got, wide_two, gather.swapped(wide_two, project, att))
    got_att = exchange(att)
    act, slope, up_full = feed_up(coords, two, after(normed_two, a_three), bias_up, r, m)
    swap_three = gather.swapped(wide_three, act)
    three = gather.sources(columns[2], near, near_got, wide_three, swap_three)

    got_one = exchange(normed_one, act)
    got_two = exchange(normed_two, act)
    own, other = weight_grad(
        coords, scale, [(after(act, got_att, *wide_three[1:]), cotangent)], nz, m, "grad_down", 15
    )
    own_got = exchange(other, *swap_three)
    dh_mine, dh_other, grad_bias_up, grad_normed_two, down_full = feed_back(
        coords, three, after(cotangent, other), slope, up_full, r, m, ratio
    )
    grad_bias_up = grad_bias_up.reshape(-1)
    dh_got = exchange(dh_other)
    parts = add_parts(after(own, grad_normed_two), [own_got])
    sum_down = Reduction(parts, perms, nz, m)
    (grad_mid, e_mine, e_other, grad_att, *sums) = middle_back(
        coords, cotangent, middle, after(grad_normed_two, parts[-1]), gain_two, out_full
    )
    grad_gain_two, grad_bias_two, grad_bias_out, grad_bias_down = (v.reshape(-1) for v in sums)
    e_got = exchange(e_other)
    top = outcome(middle, after(act, grad_mid), down_full, bias_down, None, 0, 2)
    done = sum_down.step(top)
    parts = weight_grad_both(
        coords,
        scales,
        [
            (normed_two, got_two, [(after(dh_mine, done), dh_got)]),
            (att, got_att, [(e_mine, e_got)]),
        ],
        nz, m, "grad_up_out", 17,
    )
    done = sum_down.step(parts[0])
    sum_up = Reduction([parts[0]] + [after(part, done) for part in parts[1:]], perms, nz, m)
    mine_one, other_one = attention_back(coords, project, probs, after(grad_att, done), 0)
    one_got = exchange(other_one, sum_down.got[0], *sum_down.got[2:])
    mine_two, other_two = attention_back(coords, project, probs, after(grad_att, mine_one, sum_down.got[0], *sum_down.got[2:]), 1)
    two_got = exchange(other_two, sum_down.got[1])
    done = sum_up.step(mine_two)
    parts = weight_grad_both(
        coords,
        scales,
        [(normed_one, got_one, [(after(mine_one, done), one_got), (mine_two, two_got)])],
        nz, m, "grad_qkv", 14,
    )
    done = sum_up.step(parts[0])
    sum_one = Reduction([parts[0]] + [after(part, done) for part in parts[1:]], perms, nz, m)

    tokens_grad, *sums = input_back(coords, tokens, grad_mid, [mine_one, other_one, mine_two, other_two], after(qkv_full, done), gain_one)
    done = sum_one.step(tokens_grad, sum_up.got[0])
    sums = after_all(sums, done)
    grad_gain_one, grad_bias_one = sums[0].reshape(-1), sums[1].reshape(-1)
    sums = sums[2].reshape(2, 2, 3, quarter)
    sums = jnp.where(core == 0, sums, sums[:, ::-1]).transpose(2, 0, 1, 3)
    grad_bias_query = sums[0].reshape(-1)
    grad_bias_value = sums[2].reshape(-1)

    grad_small = jnp.concatenate(
        [
            grad_gain_one, grad_bias_one, grad_bias_query, grad_bias_value, grad_bias_out,
            grad_gain_two, grad_bias_two, grad_bias_up, grad_bias_down,
        ]
    )
    grad_small = mine * grad_small.reshape(n, -1)

    low = outcome(middle, after(act, done), down_full, bias_down, top, 1, 2)
    done = sum_one.step(low)
    grad_small = lax.all_to_all(
        after(jnp.concatenate([grad_small, grad_small]), done, sum_one.got[0]), BOTH, 0, 0, tiled=True
    )
    half_up = sum_up.step(done)
    half_down = sum_down.step(done)
    block_output = low
    half_qkv = sum_one.step(half_up, half_down)
    merged_small = jnp.sum(after(grad_small, half_qkv), 0)
    hu = hidden // 2

    lows = [piece.astype(BF) for piece in (half_qkv, half_up, half_down)]
    small_sq = jnp.where(core == 0, jnp.sum(merged_small * merged_small), 0.0)
    local_sq = sum((jnp.sum(jnp.square(piece.astype(F32))) for piece in lows)) + small_sq
    everyone = 2 * n
    shared = lax.all_to_all(jnp.full((everyone, 128), local_sq, F32), BOTH, 0, 0, tiled=True)
    total_sq = jnp.sum(shared[:, 0])
    got = [lax.ppermute(low, "grp", SWAP) for low in lows]
    clip = jnp.minimum(1.0, CLIP * lax.rsqrt(total_sq))
    news = update(
        coords,
        clip.reshape(1),
        lows,
        got,
        (qkv_weight, out_weight, up_weight, down_weight),
        (qkv_first, out_first, up_first, down_first),
        (qkv_second, out_second, up_second, down_second),
    )
    small = adam(small_params, small_first, small_second, merged_small * clip, 0.0, RATE_SMALL)
    return (
        block_output,
        tokens_grad,
        *news[0:4],
        small[0],
        *news[4:8],
        small[1],
        *news[8:12],
        small[2],
        total_sq,
    )


def solution(mesh):
    token, flat, row, vec = P(BOTH, None), P(BOTH), P("fsdp", None), P("fsdp")
    params = (row, row, row, row, vec)
    return jax.shard_map(
        shards,
        mesh=mesh,
        in_specs=(token, token, flat, P()) + params * 3,
        out_specs=(token, token) + params * 3 + (P(),),
        check_vma=False,
    )
```
